32 devices in a mesh: rep: 4 (over z), shard: 8 (over y, x, core).
Axes of the slice: x: 2, y: 2, z: 4, core: 2. Of those that a mesh axis runs over, the one named last changes fastest.
Arguments:
- tokens: bfloat16 [16384, 768], P(('rep', 'shard')), may hold values from -6 to 6
- cotangent: bfloat16 [16384, 768], P(('rep', 'shard')), may hold values from -6 to 6
- segments: int32 [16384], P(('rep', 'shard')), may hold values from 0 to 31, never falling along the last dimension, each value on 1 to 1024 neighbouring positions
- buckets: int32 [512], replicated, may hold values from 0 to 31, as said below
- routes: int32 [16384, 2], P(('rep', 'shard')), may hold values from 0 to 7, all different within a row; in each aligned block of 512 rows (0 to 511, 512 to 1023, ...) at most 224 rows name the same one
- attn_gain: bfloat16 [768], P('shard'), may hold values from 0.5 to 1.5
- qkv_weight: bfloat16 [768, 2304], P('shard'), may hold values from -0.21875 to 0.21875
- proj_weight: bfloat16 [768, 768], P('shard'), may hold values from -1.25 to 1.25
- rel_bias: float32 [32, 12], replicated, may hold values from -4 to 4
- moe_gain: bfloat16 [768], P('shard'), may hold values from 0.5 to 1.5
- router: bfloat16 [768, 8], P('shard'), may hold values from -0.15625 to 0.15625
- expert_in: bfloat16 [8, 768, 3072], P('shard'), may hold values from -0.21875 to 0.21875
- expert_out: bfloat16 [8, 3072, 768], P('shard'), may hold values from -0.21875 to 0.21875
Outputs:
- output: bfloat16 [16384, 768], P(('rep', 'shard'))
- grad_tokens: bfloat16 [16384, 768], P(('rep', 'shard'))
- grad_qkv: float32 [768, 2304], P('shard')
- grad_proj: float32 [768, 768], P('shard')
- grad_router: float32 [768, 8], P('shard')
- grad_attn_gain: float32 [768], P('shard')
- grad_moe_gain: float32 [768], P('shard')
- grad_rel_bias: float32 [32, 12], replicated
- grad_expert_in: float32 [8, 768, 3072], P('shard', 'rep')
- grad_expert_out: float32 [8, 3072, 768], P('shard', 'rep')
The draws below stay inside these ranges and needn't reach their ends.
Inputs may be any that keep to these rules, and one draw needn't show every extreme that they name: `segments`: never falling along the tokens; one number covers at most 1024 tokens, and some number exactly that many. `buckets`: never falling with the distance, 0 at distance 0. `routes`: a token's 2 experts differ; the 512 tokens of one device name one expert at most 224 times, and some device's tokens name some expert exactly 224 times.
All inputs are finite; a program needn't handle non-finite values.
Results may differ from the reference program's by a relative error of at most 0.017.
Values may be sent and summed in bfloat16 or wider, within the bound.
No kernel may reach another device: no remote copies, remote signals or barrier semaphores. Data moves between devices by JAX's collectives and lax.ppermute only.
A program may use at most 192 MiB of HBM per device.

```python
import math
import jax
import jax.numpy as jnp
import numpy as np
from jax import lax

D = 768
HEADS = 12
HEAD_DIM = 64
FF = 3072
TOP = 2
BUCKETS = 32
TOK_DEV = 512
EXPERTS = 8
CAP = 192
CROWD = 224
SEQ = 512
TOKENS = 16384
DOCS = 32


def draw_buckets(key, part):
    increments = jax.random.randint(key, (SEQ,), 0, 2)
    places = jnp.arange(SEQ)
    increments = jnp.where(places == 0, 0, increments)
    table = jnp.minimum(jnp.cumsum(increments), BUCKETS - 1)
    return jnp.where(places == SEQ - 1, BUCKETS - 1, table).astype(jnp.int32)


def block_levels(key, dims, split, least, top_value):
    def one(axis_at, parts):
        heights = jax.random.uniform(jax.random.fold_in(jax.random.fold_in(key, 6), axis_at), (parts,), jnp.float32, least / len(split), top_value / len(split))
        return jnp.repeat(jnp.exp(heights), dims[axis_at] // parts).reshape((-1,) + (1,) * (len(dims) - axis_at - 1))

    loudness = one(*split[0])
    for cut in split[1:]:
        loudness = loudness * one(*cut)
    return loudness


def length_profile(amount, total, bound, lean):
    portions = [(1 << 20) // math.isqrt(rank ** lean) + 1 for rank in range(2, amount + 1)]
    spare, holding = total - bound - (amount - 1), [1] * (amount - 1)
    while spare > 0:
        movable = [i for i in range(amount - 1) if holding[i] < bound]
        mass, remaining = sum([portions[i] for i in movable]), spare
        for i in movable:
            extra = min(bound - holding[i], max(1, remaining * portions[i] // mass), spare)
            holding[i] = holding[i] + extra
            spare = spare - extra
    return np.array([bound] + holding)


def ragged(rng, amount, total, limit, slope):
    if amount == 2:
        one = jax.random.randint(rng, (), max(1, total - limit), min(limit, total - 1) + 1)
        return jnp.stack([one, total - one])
    sizes = jnp.asarray(length_profile(amount, total, limit, slope), jnp.int32)
    twos = (amount - 1) // 2
    source_of, receiver = sizes[1:1 + 2 * twos:2], sizes[2:2 + 2 * twos:2]
    margin = jnp.minimum(source_of - 1, limit - receiver)
    moved = jax.random.randint(jax.random.fold_in(rng, 1), (twos,), 0, 1 << 20) % (margin + 1)
    sizes = sizes.at[1:1 + 2 * twos:2].set(source_of - moved).at[2:2 + 2 * twos:2].set(receiver + moved)
    return sizes[jax.random.permutation(jax.random.fold_in(rng, 2), amount)]


def shared_out(key, own, number, rows, number_of, top, most, skew):
    sequence = jax.random.permutation(key, number_of)
    heavy_load, common = load_shares(number_of, rows * top, most, skew, True), load_shares(number_of, rows * top, most, skew, False)
    places = jnp.arange(number_of)

    def named(sizes, turn):
        used = int((sizes > 0).sum())
        fixed = max(1, used // 4)
        moved = fixed + (places - fixed + turn * (used - fixed)) % max(1, number_of - fixed)
        return jnp.zeros((number_of,), jnp.int32).at[sequence[jnp.where(places < fixed, places, moved)]].set(jnp.asarray(sizes, jnp.int32))

    sizes = jnp.where(number % 4 == 0, named(heavy_load, number // 4), named(common, number - number // 4 - 1))
    mixed = jax.random.permutation(jax.random.fold_in(own, 3), number_of)
    donor, receiver = mixed[0:number_of // 2 * 2:2], mixed[1:number_of // 2 * 2:2]
    slack = jnp.minimum(sizes[donor] - 1, most - sizes[receiver]) // 2
    slack = jnp.where((donor == sequence[0]) | (receiver == sequence[0]) | (sizes[receiver] == 0), 0, jnp.maximum(slack, 0))
    moved = jax.random.randint(jax.random.fold_in(own, 4), (number_of // 2,), 0, 1 << 20) % (slack + 1)
    sizes = sizes.at[donor].add(-moved).at[receiver].add(moved)
    members = jnp.searchsorted(jnp.cumsum(sizes), jnp.arange(rows * top), side="right").astype(jnp.int32)
    listing = members.reshape(top, rows).T
    listing = listing[jax.random.permutation(jax.random.fold_in(own, 1), rows)]
    turn = jax.random.randint(jax.random.fold_in(own, 2), (rows, 1), 0, top)
    return jnp.take_along_axis(listing, (jnp.arange(top)[None, :] + turn) % top, axis=1)


def load_shares(number_of, total, reach, lean, full):
    portions = [(1 << 20) // math.isqrt(grade ** lean) + 1 for grade in range(1, number_of + 1)]
    largest = reach if full else min(reach, max(-(-total // number_of), total * portions[0] // sum(portions)))
    least = 1 if total - largest >= number_of - 1 else 0
    given, rest = [largest] + [least] * (number_of - 1), total - largest - least * (number_of - 1)
    while rest > 0:
        movable = [i for i in range(1, number_of) if given[i] < largest] or [i for i in range(1, number_of) if given[i] < reach]
        mass, remaining = sum([portions[i] for i in movable]), rest
        for i in movable:
            more = min(reach - given[i], max(1, remaining * portions[i] // mass), rest)
            given[i] = given[i] + more
            rest = rest - more
    return np.array(given)


def normal_values(own_key, shape, width, reach, cuts=(), kind=jnp.bfloat16):
    values = jax.random.normal(own_key, shape, jnp.float32) * width
    if len(cuts) > 0:
        values = block_levels(own_key, shape, cuts, -0.22, 0.18) * values
    return jnp.clip(values, min=-reach, max=reach).astype(kind)


def setup_inputs(seed: int = 0) -> dict:
    streams_of = jax.random.split(jax.random.key(seed), 14)
    tokens = normal_values(streams_of[0], (TOKENS, D), 1.0, 6.0, ((0, 32),))
    cotangent = normal_values(streams_of[1], (TOKENS, D), 1.0, 6.0, ((0, 32),))
    segments = jnp.searchsorted(jnp.cumsum(ragged(streams_of[2], DOCS, TOKENS, 2 * TOK_DEV, 0)), jnp.arange(TOKENS), side="right").astype(jnp.int32)
    buckets = draw_buckets(jax.random.fold_in(streams_of[13], 71), 0)
    routes_keys = jax.random.split(jax.random.fold_in(streams_of[4], 1), TOKENS // TOK_DEV)
    routes_turns = jax.random.permutation(jax.random.fold_in(streams_of[4], 3), TOKENS // TOK_DEV)
    routes = jax.vmap(lambda own, number: shared_out(jax.random.fold_in(streams_of[4], 2), own, number, TOK_DEV, EXPERTS, TOP, CROWD, 1))(routes_keys, routes_turns).reshape((TOKENS, TOP))
    attn_gain = jnp.clip(1.0 + 0.1 * jax.random.normal(streams_of[5], (D,), jnp.float32), 0.5, 1.5).astype(jnp.bfloat16)
    qkv_weight = normal_values(streams_of[6], (D, 3 * D), D ** -0.5, 0.21875, ((0, 8),))
    proj_weight = normal_values(streams_of[7], (D, D), (D // 32) ** -0.5, 1.25, ((0, 8),))
    rel_bias = normal_values(streams_of[8], (BUCKETS, HEADS), 1.0, 4.0, (), jnp.float32)
    moe_gain = jnp.clip(1.0 + 0.1 * jax.random.normal(streams_of[9], (D,), jnp.float32), 0.5, 1.5).astype(jnp.bfloat16)
    router = normal_values(streams_of[10], (D, EXPERTS), (2 * D) ** -0.5, 0.15625, ((0, 8),))
    expert_in = normal_values(streams_of[11], (EXPERTS, D, FF), D ** -0.5, 0.21875, ((0, 8),))
    expert_out = normal_values(streams_of[12], (EXPERTS, FF, D), (FF // 4) ** -0.5, 0.21875, ((0, 8),))
    return {"tokens": tokens, "cotangent": cotangent, "segments": segments, "buckets": buckets, "routes": routes, "attn_gain": attn_gain, "qkv_weight": qkv_weight, "proj_weight": proj_weight, "rel_bias": rel_bias, "moe_gain": moe_gain, "router": router, "expert_in": expert_in, "expert_out": expert_out}


@jax.custom_vjp
def low(v):
    return lax.optimization_barrier(v.astype(jnp.bfloat16)).astype(jnp.float32)

@jax.custom_vjp
def low_back(v):
    return v

def low_keep(v):
    return (low(v), None)

def low_pass(kept, grad):
    return (grad,)

def back_keep(v):
    return (v, None)

def back_low(kept, grad):
    return (low(grad),)
low.defvjp(low_keep, low_pass)
low_back.defvjp(back_keep, back_low)
epsilon = 1e-06
neg_fill = -1e+30
highest = lax.Precision.HIGHEST

def rms_norm(values, gain_vector):
    return values * lax.rsqrt(lax.optimization_barrier(jnp.mean(values * values, axis=-1, keepdims=True)) + epsilon) * gain_vector

def attend_group(normed, segment_rows, buckets, qkv_weight, rel_bias):
    group_size, seq_len, model_width = normed.shape
    projected = low_back(low(jnp.einsum('gsd,de->gse', normed, qkv_weight, precision=highest)))
    queries = projected[..., :model_width].reshape(group_size, seq_len, HEADS, HEAD_DIM)
    keys_all = projected[..., model_width:2 * model_width].reshape(group_size, seq_len, HEADS, HEAD_DIM)
    values_all = projected[..., 2 * model_width:].reshape(group_size, seq_len, HEADS, HEAD_DIM)
    raw_scores = jnp.einsum('gqhd,gkhd->ghqk', queries, keys_all, precision=highest)
    offset = jnp.arange(seq_len)[:, None] - jnp.arange(seq_len)[None, :]
    bias_table = jnp.transpose(rel_bias[buckets[jnp.clip(offset, 0, seq_len - 1)]], (2, 0, 1))
    scores = low_back(raw_scores * HEAD_DIM ** (-0.5) + bias_table[None])
    allowed = (offset[None] >= 0) & (segment_rows[:, :, None] == segment_rows[:, None, :])
    scores = jnp.where(allowed[:, None], scores, neg_fill)
    row_top = lax.optimization_barrier(jnp.max(scores, axis=-1, keepdims=True))
    weights = jnp.exp(scores - row_top)
    weights = low(weights / lax.optimization_barrier(jnp.sum(weights, axis=-1, keepdims=True)))
    attended = jnp.einsum('ghqk,gkhd->gqhd', weights, values_all, precision=highest)
    return low_back(low(attended.reshape(group_size, seq_len, model_width)))

def expert_rows(operands):
    rows_in, weight_in, weight_out = operands
    pre_act = low_back(jnp.dot(rows_in, weight_in, precision=highest))
    activated = low(jax.nn.gelu(pre_act, approximate=False))
    return low_back(low(jnp.dot(activated, weight_out, precision=highest)))

def layer_forward(inputs, attn_gain, qkv_weight, proj_weight, rel_bias, moe_gain, router, expert_in, expert_out, segments, buckets, routes):
    tokens_all, model_width = inputs.shape
    seq_count = tokens_all // SEQ
    group_size = math.gcd(seq_count, max(1, 4096 // SEQ))
    normed_one = low(rms_norm(inputs, attn_gain))

    def attend_one(operands):
        return attend_group(operands[0], operands[1], buckets, qkv_weight, rel_bias)
    attended = lax.map(jax.checkpoint(attend_one), (normed_one.reshape(seq_count // group_size, group_size, SEQ, model_width), segments.reshape(seq_count // group_size, group_size, SEQ)))
    attended = attended.reshape(tokens_all, model_width)
    residual = inputs + low_back(jnp.dot(attended, proj_weight, precision=highest))
    normed_two = low(rms_norm(residual, moe_gain))
    logits = low_back(jnp.dot(normed_two, router, precision=highest))
    gate_weights = jax.nn.softmax(jnp.take_along_axis(logits, routes, axis=1), axis=1)
    expert_count = expert_in.shape[0]
    block_count = tokens_all // TOK_DEV
    pair_expert = routes.reshape(block_count, TOK_DEV * TOP)
    matches = (pair_expert[..., None] == jnp.arange(expert_count)[None, None, :]).astype(jnp.int32)
    slot_rank = lax.optimization_barrier(jnp.sum((jnp.cumsum(matches, axis=1) - matches) * matches, axis=2))
    kept = slot_rank < CAP
    kept_scale = kept.astype(jnp.float32)[..., None]
    flat_slot = jnp.where(kept, pair_expert * CAP + slot_rank, 0).astype(jnp.int32)
    block_ids = jnp.broadcast_to(jnp.arange(block_count)[:, None], flat_slot.shape)
    pair_rows = jnp.repeat(normed_two, TOP, axis=0).reshape(block_count, TOK_DEV * TOP, model_width) * kept_scale
    slot_rows = jnp.zeros((block_count, expert_count * CAP, model_width), normed_two.dtype).at[block_ids, flat_slot].add(pair_rows)
    slot_rows = low_back(slot_rows)
    by_expert = slot_rows.reshape(block_count, expert_count, CAP, model_width).transpose(1, 0, 2, 3).reshape(expert_count, block_count * CAP, model_width)
    results = lax.map(jax.checkpoint(expert_rows), (by_expert, expert_in, expert_out))
    returned = results.reshape(expert_count, block_count, CAP, model_width).transpose(1, 0, 2, 3).reshape(block_count, expert_count * CAP, model_width)
    picked = (returned[block_ids, flat_slot] * kept_scale).reshape(tokens_all, TOP, model_width)
    return residual + lax.optimization_barrier(jnp.sum(gate_weights[:, :, None] * picked, axis=1))

def reference(tokens, cotangent, segments, buckets, routes, attn_gain, qkv_weight, proj_weight, rel_bias, moe_gain, router, expert_in, expert_out):
    floats = tuple((item.astype(jnp.float32) for item in (tokens, attn_gain, qkv_weight, proj_weight, rel_bias, moe_gain, router, expert_in, expert_out)))

    def forward(*operands):
        return layer_forward(*operands, segments, buckets, routes)
    output, pullback = jax.vjp(forward, *floats)
    grads = pullback(cotangent.astype(jnp.float32))
    return (output.astype(jnp.bfloat16), grads[0].astype(jnp.bfloat16), grads[2], grads[3], grads[6], grads[1], grads[5], grads[4], grads[7], grads[8])
```

```python
import functools
import math

import jax
import jax.numpy as jnp
from jax import lax
from jax.experimental import pallas as pl
from jax.experimental.pallas import tpu as pltpu
from jax.sharding import PartitionSpec as P

F32 = jnp.float32
BF16 = jnp.bfloat16
EPS = 1e-06
NEG = -1e30
LANES = 128
HEAD_DIM = 64
GROUP = 256
VMEM_LIMIT = 60 * 1024 * 1024


def dot(a, b):
    return jnp.dot(a, b, preferred_element_type=F32)


def dot_nt(a, b):
    return lax.dot_general(a, b, (((1,), (1,)), ((), ())), preferred_element_type=F32)


def dot_tn(a, b):
    return lax.dot_general(a, b, (((0,), (0,)), ((), ())), preferred_element_type=F32)


def call(kernel, out_shape, **kw):
    flops = kw.pop("flops", 0)
    moved = kw.pop("moved", 0)
    return pl.pallas_call(
        kernel,
        out_shape=out_shape,
        compiler_params=pltpu.CompilerParams(vmem_limit_bytes=VMEM_LIMIT),
        cost_estimate=pl.CostEstimate(flops=flops, bytes_accessed=moved, transcendentals=0),
        **kw,
    )


def whole(shape):
    rank = len(shape)
    return pl.BlockSpec(shape, lambda *_: (0,) * rank)


def smem():
    return pl.BlockSpec(memory_space=pltpu.SMEM)


def sds(shape, dtype):
    return jax.ShapeDtypeStruct(shape, dtype)


def iota(shape, dim):
    return lax.broadcasted_iota(jnp.int32, shape, dim)


def prep_kernel(
    experts, capacity, routes_ref, seg_row, seg_col, rev_ref, bias_ref, cot_ref,
    table_ref, slot_row_ref, slot_col_ref, cot_out_ref, mask_scr, series_scr, extra_scr,
):
    step = pl.program_id(0)
    seq = cot_ref.shape[0]
    width = cot_ref.shape[1]
    per = cot_out_ref.shape[0]

    @pl.when(step == 0)
    def _():
        keep = (iota((seq, seq), 0) >= iota((seq, seq), 1)) & (seg_col[...] == seg_row[...])
        mask_scr[...] = jnp.where(keep, 0.0, NEG)
        rev = rev_ref[...]
        bias = bias_ref[...]
        series = jnp.zeros((bias.shape[0], seq), F32)
        for bucket in range(bias.shape[1]):
            series = jnp.where(rev == bucket, bias[:, bucket : bucket + 1], series)
        series_scr[...] = series
        first, second = routes_ref[0:1, :], routes_ref[1:2, :]
        ids = iota((experts, seq), 0)
        m0 = (ids == first).astype(F32)
        m1 = (ids == second).astype(F32)
        before = (iota((seq, seq), 0) < iota((seq, seq), 1)).astype(BF16)
        count = dot((m0 + m1).astype(BF16), before)
        rank0 = jnp.sum(count * m0, axis=0, keepdims=True)
        rank1 = jnp.sum(count * m1, axis=0, keepdims=True)
        r0, r1 = first.astype(F32), second.astype(F32)
        slot0 = jnp.where(rank0 < capacity, r0 * capacity + rank0, -1.0)
        slot1 = jnp.where(rank1 < capacity, r1 * capacity + rank1, -1.0)
        place = iota((LANES, seq), 0)
        rows = jnp.where(place == 0, slot0, -1.0)
        rows = jnp.where(place == 1, slot1, rows)
        rows = jnp.where(place == 2, r0, rows)
        rows = jnp.where(place == 3, r1, rows)
        slot_row_ref[...] = rows[0:8, :].astype(jnp.int32)
        cols = rows.T
        slot_col_ref[...] = cols
        lane = iota((seq, LANES), 1)
        extra_scr[0] = jnp.where(lane == 0, cols[:, 3:4], 0.0).astype(BF16)
        extra_scr[1] = jnp.where(lane == 0, cols[:, 2:3], 0.0).astype(BF16)

    row = series_scr[pl.ds(step, 1), :]
    table_ref[0] = pltpu.roll(jnp.broadcast_to(row, (seq, seq)), 0, 1, stride=1, stride_axis=0) + mask_scr[...]

    @pl.when(step < 8)
    def _():
        slots = iota((per, seq), 0) + step * per
        hit0 = (slots == slot_row_ref[0:1, :]).astype(F32)
        hit1 = (slots == slot_row_ref[1:2, :]).astype(F32)
        cot_out_ref[:, :width] = dot((hit0 + hit1).astype(BF16), cot_ref[...]).astype(BF16)
        cot_out_ref[:, width:] = (
            dot(hit0.astype(BF16), extra_scr[0]) + dot(hit1.astype(BF16), extra_scr[1])
        ).astype(BF16)


def prep(routes_t, segments, rev_buckets, rel_bias, cotangent, experts, capacity):
    seq, width = cotangent.shape
    heads = rel_bias.shape[1]
    buckets = rel_bias.shape[0]
    slots = experts * capacity
    per = slots // 8
    hp = -(-heads // 8) * 8
    bias_t = jnp.zeros((hp, buckets), F32).at[:heads].set(rel_bias.T)
    return call(
        functools.partial(prep_kernel, experts, capacity),
        [
            sds((heads, seq, seq), F32),
            sds((8, seq), jnp.int32),
            sds((seq, LANES), F32),
            sds((slots, width + LANES), BF16),
        ],
        grid=(heads,),
        in_specs=[
            whole((2, seq)), whole((1, seq)), whole((seq, 1)), whole((1, seq)),
            whole((hp, buckets)), whole((seq, width)),
        ],
        out_specs=[
            pl.BlockSpec((1, seq, seq), lambda h: (h, 0, 0)),
            whole((8, seq)),
            whole((seq, LANES)),
            pl.BlockSpec((per, width + LANES), lambda h: (jnp.minimum(h, 7), 0)),
        ],
        scratch_shapes=[
            pltpu.VMEM((seq, seq), F32),
            pltpu.VMEM((hp, seq), F32),
            pltpu.VMEM((2, seq, LANES), BF16),
        ],
        flops=2 * slots * seq * width,
        moved=heads * seq * seq * 4 + 4 * seq * width,
        name="prep",
    )(routes_t, segments[None, :], segments[:, None], rev_buckets[None, :], bias_t, cotangent)


def front_kernel(
    blocks, experts, me_ref, tokens_ref, table_ref, slot_row_ref, *refs,
):
    w_in = refs[:blocks]
    p_in = refs[blocks : 2 * blocks]
    (q_ref, k_ref, v_ref, lse_ref, att_ref, res_ref, n1_ref, n2_ref, logit_ref, sent_ref,
     qkv_ref, proj_ref, small_ref, small_t_ref) = refs[2 * blocks :]
    step = pl.program_id(0)
    last = pl.num_programs(0) - 1
    seq, width = tokens_ref.shape
    rows = w_in[0].shape[0]
    scale = HEAD_DIM ** (-0.5)

    @pl.when(step == 0)
    def _():
        me = me_ref[0]
        for j in range(blocks):
            start = pl.multiple_of((me ^ j) * rows, rows) if blocks > 1 else 0
            qkv_ref[pl.ds(start, rows), :] = w_in[j][:, : 3 * width]
            small_ref[pl.ds(start, rows), :] = w_in[j][:, 3 * width :]
            proj_ref[pl.ds(start, rows), :] = p_in[j][...]
        small_t_ref[...] = small_ref[...].astype(F32).T
        x = tokens_ref[...].astype(F32)
        r = lax.rsqrt(jnp.mean(x * x, axis=-1, keepdims=True) + EPS)
        n1_ref[...] = (x * r * small_t_ref[experts : experts + 1, :]).astype(BF16)
        lse_ref[...] = jnp.zeros_like(lse_ref)

    base = pl.multiple_of(step * GROUP, GROUP)
    n1 = n1_ref[...]
    q_ref[...] = dot(n1, qkv_ref[:, pl.ds(base, GROUP)]).astype(BF16)
    k_ref[...] = dot(n1, qkv_ref[:, pl.ds(width + base, GROUP)]).astype(BF16)
    v_ref[...] = dot(n1, qkv_ref[:, pl.ds(2 * width + base, GROUP)]).astype(BF16)

    half = seq // 2
    lane = iota((half, LANES), 1)
    for pair in range(GROUP // LANES):
        cols = slice(pair * LANES, (pair + 1) * LANES)
        for rb in range(2):
            span = (rb + 1) * half
            qrows = slice(rb * half, (rb + 1) * half)
            qp = q_ref[qrows, cols]
            kp = k_ref[:span, cols]
            vp = v_ref[:span, cols]
            mixed = []
            for parity in range(2):
                mine = (lane // HEAD_DIM) == parity
                qm = jnp.where(mine, qp, jnp.zeros_like(qp))
                s = dot_nt(qm, kp) * scale + table_ref[2 * pair + parity, qrows, :span]
                top = jnp.max(s, axis=-1, keepdims=True)
                e = jnp.exp(s - top)
                total = jnp.sum(e, axis=-1, keepdims=True)
                p = (e * (1.0 / total)).astype(BF16)
                mixed.append(dot(p, vp))
                head = step * (GROUP // HEAD_DIM) + 2 * pair + parity
                lse_ref[qrows, :] = jnp.where(lane == head, top + jnp.log(total), lse_ref[qrows, :])
            at = pl.multiple_of(base + pair * LANES, LANES)
            att_ref[qrows, pl.ds(at, LANES)] = jnp.where(lane < HEAD_DIM, mixed[0], mixed[1]).astype(BF16)

    @pl.when(step == last)
    def _():
        x = tokens_ref[...].astype(F32) + dot(att_ref[...], proj_ref[...])
        res_ref[...] = x
        r = lax.rsqrt(jnp.mean(x * x, axis=-1, keepdims=True) + EPS)
        n2 = (x * r * small_t_ref[experts + 1 : experts + 2, :]).astype(BF16)
        n2_ref[...] = n2
        logit_ref[...] = dot(n2, small_ref[...])
        per = sent_ref.shape[0] // 8
        for e in range(8):
            slots = iota((per, seq), 0) + e * per
            hit = (slots == slot_row_ref[0:1, :]) | (slots == slot_row_ref[1:2, :])
            sent_ref[e * per : (e + 1) * per, :] = dot(hit.astype(BF16), n2).astype(BF16)


def front(me, tokens, table, slot_row, w_blocks, p_blocks, experts, slots):
    seq, width = tokens.shape
    blocks = len(w_blocks)
    groups = width // GROUP
    per_group = GROUP // HEAD_DIM
    col = pl.BlockSpec((seq, GROUP), lambda g: (0, g))
    return call(
        functools.partial(front_kernel, blocks, experts),
        [
            sds((seq, width), BF16), sds((seq, width), BF16), sds((seq, width), BF16),
            sds((seq, LANES), F32), sds((seq, width), BF16), sds((seq, width), F32),
            sds((seq, width), BF16), sds((seq, width), BF16), sds((seq, LANES), F32),
            sds((slots, width), BF16),
            sds((width, 3 * width), BF16), sds((width, width), BF16), sds((width, LANES), BF16),
            sds((LANES, width), F32),
        ],
        grid=(groups,),
        in_specs=[
            smem(), whole((seq, width)),
            pl.BlockSpec((per_group, seq, seq), lambda g: (g, 0, 0)),
            whole((8, seq)),
        ]
        + [whole(b.shape) for b in w_blocks]
        + [whole(b.shape) for b in p_blocks],
        out_specs=[
            col, col, col,
            whole((seq, LANES)), whole((seq, width)), whole((seq, width)),
            whole((seq, width)), whole((seq, width)), whole((seq, LANES)),
            whole((slots, width)),
            whole((width, 3 * width)), whole((width, width)), whole((width, LANES)),
            whole((LANES, width)),
        ],
        flops=2 * seq * width * width * 4 + 2 * slots * seq * width + 8 * seq * seq * width,
        moved=30_000_000,
        name="front",
    )(me, tokens, table, slot_row, *w_blocks, *p_blocks)


def gelu_parts(v):
    size = jnp.abs(v) * (2.0 ** -0.5)
    t = 1.0 / (1.0 + 0.3275911 * size)
    bell = jnp.exp(-0.5 * v * v)
    poly = t * (
        0.5 * 0.254829592
        + t * (0.5 * -0.284496736 + t * (0.5 * 1.421413741 + t * (0.5 * -1.453152027 + t * (0.5 * 1.061405429))))
    )
    tail = poly * bell
    below = jnp.where(v < 0, tail, 1.0 - tail)
    return v * below, below + v * bell * (1.0 / math.sqrt(2.0 * math.pi))


def expert_kernel(first, ranks, tile, *refs):
    if first:
        (me_ref, rows_ref, cotx_ref, small_ref, win_ref, wout_ref,
         act_ref, gp_ref, buf_ref, rows_t, sg_ref, sg_t) = refs
    else:
        (rows_ref, sg_ref, rows_t, sg_t, win_ref, wout_ref, _a, _g,
         act_ref, gp_ref, buf_ref) = refs
    step = pl.program_id(0)
    total, width = rows_ref.shape
    if first:

        @pl.when(step == 0)
        def _():
            me = me_ref[0]
            for at in range(0, total, tile):
                here = slice(at, at + tile)
                logits = dot(rows_ref[here, :], small_ref[...])
                lane = iota((tile, LANES), 1)
                other_id = cotx_ref[here, width : width + 1].astype(F32).astype(jnp.int32)
                own = jnp.sum(jnp.where(lane == me, logits, 0.0), axis=1, keepdims=True)
                other = jnp.sum(jnp.where(lane == other_id, logits, 0.0), axis=1, keepdims=True)
                top = jnp.maximum(own, other)
                a, b = jnp.exp(own - top), jnp.exp(other - top)
                gate = a / (a + b)
                sg_ref[here, :] = (gate * cotx_ref[here, :width].astype(F32)).astype(BF16)
            rows_t[...] = rows_ref[...].T
            sg_t[...] = sg_ref[...].T

    w1 = win_ref[...]
    w2 = wout_ref[...]
    for at in range(0, total, tile):
        here = slice(at, at + tile)
        pre = dot(rows_ref[here, :], w1)
        ga = dot_nt(sg_ref[here, :], w2)
        act, slope = gelu_parts(pre)
        act_ref[here, :] = act.astype(BF16)
        gp_ref[here, :] = (ga * slope).astype(BF16)
    block = w1.shape[1]
    part = width // ranks
    gwin = dot(rows_t[...], gp_ref[...]).astype(BF16)
    gwout = dot(sg_t[...], act_ref[...]).T.astype(BF16)
    rank = lax.rem(step, ranks)
    cb = lax.div(step, ranks)
    lane0 = pl.multiple_of(rank * block, block)
    for dest in range(ranks):
        buf_ref[dest, cb, 0:part, pl.ds(lane0, block)] = gwin[dest * part : (dest + 1) * part, :]
    piece = block // ranks
    for i in range(ranks):
        for j in range(width // block):
            buf_ref[rank, cb, part + j * piece : part + (j + 1) * piece, i * block : (i + 1) * block] = gwout[
                i * piece : (i + 1) * piece, j * block : (j + 1) * block
            ]


def expert_chunk(first, ins, chunk, ranks, total, width, hidden):
    start, count = chunk
    block = 256
    per_rank = hidden // ranks // block
    part = width // ranks
    piece = block // ranks
    high = part + (width // block) * piece

    def at(s):
        return lax.rem(s, ranks) * per_rank + start + lax.div(s, ranks)

    win_spec = pl.BlockSpec((width, block), lambda s: (0, at(s)))
    wout_spec = pl.BlockSpec((block, width), lambda s: (at(s), 0))
    col = pl.BlockSpec((total, block), lambda s: (0, at(s)))
    outs = [
        sds((total, hidden), BF16),
        sds((total, hidden), BF16),
        sds((ranks, count, high, ranks * block), BF16),
    ]
    out_specs = [col, col, whole((ranks, count, high, ranks * block))]
    kw = {}
    if first:
        in_specs = [smem(), whole((total, width)), whole((total, width + LANES)), whole((width, LANES)), win_spec, wout_spec]
        outs += [sds((width, total), BF16), sds((total, width), BF16), sds((width, total), BF16)]
        out_specs += [whole((width, total)), whole((total, width)), whole((width, total))]
    else:
        in_specs = [
            whole((total, width)), whole((total, width)), whole((width, total)), whole((width, total)),
            win_spec, wout_spec,
            pl.BlockSpec(memory_space=pl.ANY), pl.BlockSpec(memory_space=pl.ANY),
        ]
        kw["input_output_aliases"] = {6: 0, 7: 1}
    return call(
        functools.partial(expert_kernel, first, ranks, 256),
        outs,
        grid=(count * ranks,),
        in_specs=in_specs,
        out_specs=out_specs,
        flops=8 * total * width * block * ranks * count,
        moved=20_000_000,
        name="experts",
        **kw,
    )(*ins)


def rows_kernel(transposed, a_ref, w_ref, o_ref):
    prod = dot_nt if transposed else dot
    o_ref[...] = prod(a_ref[...], w_ref[...]).astype(BF16)


def rows_out(transposed, a, w, width):
    total, hidden = a.shape
    tile = total // 8
    return call(
        functools.partial(rows_kernel, transposed),
        sds((total, width), BF16),
        grid=(8,),
        in_specs=[pl.BlockSpec((tile, hidden), lambda i: (i, 0)), whole(w.shape)],
        out_specs=pl.BlockSpec((tile, width), lambda i: (i, 0)),
        flops=2 * total * hidden * width,
        moved=2 * (total * hidden + hidden * width + total * width),
        name="expert_rows_back" if transposed else "expert_rows_out",
    )(a, w)


def norm_back(x, grad, gain, count):
    r = lax.rsqrt(jnp.mean(x * x, axis=-1, keepdims=True) + EPS)
    u = grad * gain
    inner = jnp.mean(u * x, axis=-1, keepdims=True)
    xr = x * r
    return r * u - (r * r * r) * x * inner, jnp.sum(grad * xr, axis=0, keepdims=True)


def mid_kernel(
    experts, ret_ref, back_ref, slot_ref, res_ref, logit_ref, cot_ref, n2_ref, att_ref,
    proj_ref, small_ref, small_t_ref, out_ref, gres_ref, gatt_ref, gproj_ref, gsmall_ref,
):
    seq, width = res_ref.shape
    slots = ret_ref.shape[0]
    lane = iota((seq, LANES), 1)
    spot = iota((seq, slots), 1)
    s0 = slot_ref[:, 0:1].astype(jnp.int32)
    s1 = slot_ref[:, 1:2].astype(jnp.int32)
    h0 = (spot == s0).astype(BF16)
    h1 = (spot == s1).astype(BF16)
    hot0 = lane == slot_ref[:, 2:3].astype(jnp.int32)
    hot1 = lane == slot_ref[:, 3:4].astype(jnp.int32)
    logits = logit_ref[...]
    c0 = jnp.sum(jnp.where(hot0, logits, 0.0), axis=1, keepdims=True)
    c1 = jnp.sum(jnp.where(hot1, logits, 0.0), axis=1, keepdims=True)
    top = jnp.maximum(c0, c1)
    e0, e1 = jnp.exp(c0 - top), jnp.exp(c1 - top)
    g0, g1 = e0 / (e0 + e1), e1 / (e0 + e1)
    cot = cot_ref[...].astype(F32)
    ret = ret_ref[...]
    p0 = dot(h0, ret)
    p1 = dot(h1, ret)
    x = res_ref[...]
    out_ref[...] = (x + (g0 * p0 + g1 * p1)).astype(BF16)
    d0 = jnp.sum(cot * p0, axis=1, keepdims=True)
    d1 = jnp.sum(cot * p1, axis=1, keepdims=True)
    mean = g0 * d0 + g1 * d1
    glog = jnp.where(hot0, g0 * (d0 - mean), 0.0) + jnp.where(hot1, g1 * (d1 - mean), 0.0)
    glog = glog.astype(BF16)
    grad = dot(h0 + h1, back_ref[...]) + dot_nt(glog, jnp.where(iota((width, LANES), 1) < experts, small_ref[...], jnp.zeros_like(small_ref[...])))
    gx, ggain = norm_back(x, grad, small_t_ref[experts + 1 : experts + 2, :], width)
    gres = gx + cot
    gres_ref[...] = gres
    branch = gres.astype(BF16)
    gproj_ref[...] = dot_tn(att_ref[...], branch).astype(BF16)
    gatt_ref[...] = dot_nt(branch, proj_ref[...]).astype(BF16)
    gain_rows = jnp.where(iota((LANES, width), 0) == experts + 1, ggain, 0.0)
    gsmall_ref[...] = dot_tn(n2_ref[...], glog) + gain_rows.T


def mid(experts, returned, back, slot_col, res, logits, cot, n2, att, proj, small, small_t):
    seq, width = res.shape
    ins = (returned, back, slot_col, res, logits, cot, n2, att, proj, small, small_t)
    return call(
        functools.partial(mid_kernel, experts),
        [
            sds((seq, width), BF16), sds((seq, width), F32), sds((seq, width), BF16),
            sds((width, width), BF16), sds((width, LANES), F32),
        ],
        in_specs=[whole(a.shape) for a in ins],
        out_specs=[
            whole((seq, width)), whole((seq, width)), whole((seq, width)),
            whole((width, width)), whole((width, LANES)),
        ],
        grid=(1,),
        flops=6 * returned.shape[0] * seq * width + 4 * seq * width * width,
        moved=15_000_000,
        name="token_side",
    )(*ins)


def tail_kernel(
    experts, buckets, tokens_ref, table_ref, q_ref, k_ref, v_ref, gatt_ref, lse_ref, n1_ref, gres_ref,
    wq_ref, wk_ref, wv_ref, small_t_ref, rev_ref, gproj_ref, gsmall_ref,
    pack_ref, gtok_ref, gbias_ref, acc_scr, diag_scr, g_scr, n1t_scr,
):
    step = pl.program_id(0)
    last = pl.num_programs(0) - 1
    seq, width = tokens_ref.shape
    half = seq // 2
    scale = HEAD_DIM ** (-0.5)

    @pl.when(step == 0)
    def _():
        acc_scr[...] = jnp.zeros_like(acc_scr)
        diag_scr[...] = jnp.zeros_like(diag_scr)
        n1t_scr[...] = n1_ref[...].T

    lane = iota((half, LANES), 1)
    full_lane = iota((seq, LANES), 1)
    for pair in range(GROUP // LANES):
        cols = slice(pair * LANES, (pair + 1) * LANES)
        dk = [jnp.zeros((seq, LANES), F32)] * 2
        dv = [jnp.zeros((seq, LANES), F32)] * 2
        skew = [jnp.zeros((LANES, seq), F32)] * 2
        for rb in range(2):
            span = (rb + 1) * half
            qrows = slice(rb * half, (rb + 1) * half)
            qp = q_ref[qrows, cols]
            gp = gatt_ref[qrows, cols]
            kp = k_ref[:span, cols]
            vp = v_ref[:span, cols]
            dq = []
            for parity in range(2):
                mine = (lane // HEAD_DIM) == parity
                head = step * (GROUP // HEAD_DIM) + 2 * pair + parity
                level = jnp.sum(jnp.where(lane == head, lse_ref[qrows, :], 0.0), axis=1, keepdims=True)
                qm = jnp.where(mine, qp, jnp.zeros_like(qp))
                gm = jnp.where(mine, gp, jnp.zeros_like(gp))
                s = dot_nt(qm, kp) * scale + table_ref[2 * pair + parity, qrows, :span]
                p = jnp.exp(s - level)
                dp = dot_nt(gm, vp)
                d = jnp.sum(p * dp, axis=1, keepdims=True)
                ds = p * (dp - d)
                low = ds.astype(BF16)
                dq.append(dot(low, kp) * scale)
                add_k = dot_tn(low, qp) * scale
                add_v = dot_tn(p.astype(BF16), gp)
                if span < seq:
                    zero = jnp.zeros((seq - span, LANES), F32)
                    add_k = jnp.concatenate([add_k, zero], axis=0)
                    add_v = jnp.concatenate([add_v, zero], axis=0)
                dk[parity] = dk[parity] + add_k
                dv[parity] = dv[parity] + add_v
                wide = low.astype(F32)
                if span < seq:
                    wide = jnp.concatenate([wide, jnp.zeros((half, seq - span), F32)], axis=1)
                for b in range(half // LANES):
                    shift = rb * half + b * LANES
                    rows = wide[b * LANES : (b + 1) * LANES, :]
                    if shift:
                        rows = jnp.concatenate([rows[:, shift:], rows[:, :shift]], axis=1)
                    skew[parity] = skew[parity] + rows
            g_scr[0, qrows, cols] = jnp.where(lane < HEAD_DIM, dq[0], dq[1]).astype(BF16)
        g_scr[1, :, cols] = jnp.where(full_lane < HEAD_DIM, dk[0], dk[1]).astype(BF16)
        g_scr[2, :, cols] = jnp.where(full_lane < HEAD_DIM, dv[0], dv[1]).astype(BF16)
        for parity in range(2):
            acc = skew[parity][0:8, :]
            for i in range(1, LANES // 8):
                acc = acc + pltpu.roll(skew[parity][i * 8 : (i + 1) * 8, :], seq - i * 8, 1)
            head = step * (GROUP // HEAD_DIM) + 2 * pair + parity
            diag_scr[pl.ds(pl.multiple_of(head * 8, 8), 8), :] = acc

    base = pl.multiple_of(step * GROUP, GROUP)
    w_refs = (wq_ref, wk_ref, wv_ref)
    n1t = n1t_scr[...]
    for i in range(3):
        g = g_scr[i]
        at = pl.multiple_of(i * width + base, GROUP)
        pack_ref[:, pl.ds(at, GROUP)] = dot(n1t, g).astype(BF16)
        acc_scr[...] += dot_nt(g, w_refs[i][...])

    @pl.when(step == last)
    def _():
        x = tokens_ref[...].astype(F32)
        gx, ggain = norm_back(x, acc_scr[...], small_t_ref[experts : experts + 1, :], width)
        gtok_ref[...] = (gx + gres_ref[...]).astype(BF16)
        gain_rows = jnp.where(iota((LANES, width), 0) == experts, ggain, 0.0)
        pack_ref[:, 3 * width : 4 * width] = gproj_ref[...]
        pack_ref[:, 4 * width :] = (gsmall_ref[...] + gain_rows.T).astype(BF16)
        count = diag_scr.shape[0]
        place = lax.rem(iota((count, seq), 0), 8)
        diag = diag_scr[...]
        total = jnp.where(place == 0, diag, 0.0)
        for r in range(1, 8):
            total = total + jnp.where(place == r, pltpu.roll(diag, seq - r, 1), 0.0)
        hot = (iota((buckets, seq), 0) == rev_ref[...]).astype(F32)
        per_row = lax.dot_general(
            total, hot, (((1,), (1,)), ((), ())), precision=lax.Precision.HIGHEST, preferred_element_type=F32
        )
        gbias_ref[...] = jnp.sum(per_row.reshape(count // 8, 8, buckets), axis=1)


def tail(experts, buckets, tokens, table, q, k, v, gatt, lse, n1, gres, qkv, small_t, rev_buckets, gproj, gsmall):
    seq, width = tokens.shape
    heads = table.shape[0]
    groups = width // GROUP
    per_group = GROUP // HEAD_DIM
    col = pl.BlockSpec((seq, GROUP), lambda g: (0, g))

    def wcol(i):
        return pl.BlockSpec((width, GROUP), lambda g: (0, i * groups + g))

    return call(
        functools.partial(tail_kernel, experts, buckets),
        [sds((width, 4 * width + LANES), BF16), sds((seq, width), BF16), sds((heads, buckets), F32)],
        grid=(groups,),
        in_specs=[
            whole((seq, width)),
            pl.BlockSpec((per_group, seq, seq), lambda g: (g, 0, 0)),
            col, col, col, col,
            whole((seq, LANES)), whole((seq, width)), whole((seq, width)),
            wcol(0), wcol(1), wcol(2),
            whole((LANES, width)), whole((1, seq)), whole((width, width)), whole((width, LANES)),
        ],
        out_specs=[whole((width, 4 * width + LANES)), whole((seq, width)), whole((heads, buckets))],
        scratch_shapes=[
            pltpu.VMEM((seq, width), F32),
            pltpu.VMEM((heads * 8, seq), F32),
            pltpu.VMEM((3, seq, GROUP), BF16),
            pltpu.VMEM((width, seq), BF16),
        ],
        flops=12 * seq * width * width + 20 * seq * seq * width,
        moved=30_000_000,
        name="tail",
    )(tokens, table, q, k, v, gatt, lse, n1, gres, qkv, qkv, qkv, small_t, rev_buckets[None, :], gproj, gsmall)


def swap(value, mask, size):
    return lax.ppermute(value, "shard", [(i, i ^ mask) for i in range(size)])


def gather_blocks(value, size):
    if size != 8:
        return [lax.all_gather(value, "shard", axis=0, tiled=True)]
    far = {j: swap(value, j, size) for j in (6, 2, 4)}
    far[0] = value
    near = {j ^ 1: swap(far[j], 1, size) for j in (0, 6, 2, 4)}
    return [far[j] if j in far else near[j] for j in range(8)]


def line_total(value, ranks):
    own = value.astype(F32)
    right = left = value
    gained = own
    for t in range(1, ranks):
        a = lax.ppermute(right, "rep", [(t - 1, t)])
        b = lax.ppermute(left, "rep", [(ranks - t, ranks - 1 - t)])
        gained = gained + (a.astype(F32) + b.astype(F32))
        right = (own + a.astype(F32)).astype(BF16)
        left = (own + b.astype(F32)).astype(BF16)
    return gained


def reduce_small(pack, me, size, ranks):
    if size != 8:
        owned = lax.psum_scatter(pack, "shard", scatter_dimension=0, tiled=True)
        return line_total(owned, ranks)
    rows = pack.shape[0] // size
    blocks = pack.reshape(4, 2, rows, pack.shape[1])
    core = me % 2
    chip = me // 2
    keep = lax.dynamic_index_in_dim(blocks, core, 1, keepdims=False)
    send = lax.dynamic_index_in_dim(blocks, 1 - core, 1, keepdims=False)
    both = keep.astype(F32) + swap(send, 1, size).astype(F32)
    low = both.astype(BF16)
    got = [
        swap(lax.dynamic_index_in_dim(low, chip ^ (j // 2), 0, keepdims=False), j, size).astype(F32)
        for j in (6, 2, 4)
    ]
    owned = lax.dynamic_index_in_dim(both, chip, 0, keepdims=False) + got[0] + got[1] + got[2]
    return line_total(owned.astype(BF16), ranks)


def body(
    tokens, cotangent, segments, buckets, routes, attn_gain, qkv_weight, proj_weight,
    rel_bias, moe_gain, router, expert_in, expert_out,
):
    seq, width = tokens.shape
    size = lax.axis_size("shard")
    ranks = lax.axis_size("rep")
    top = routes.shape[1]
    experts = expert_in.shape[0] * size
    hidden = expert_in.shape[2]
    capacity = 3 * seq * top // (2 * experts)
    slots = experts * capacity
    bucket_count = rel_bias.shape[0]
    me = lax.axis_index("shard").astype(jnp.int32)
    me_arr = me.reshape(1)
    own_rows = router.shape[0]

    small = jnp.concatenate(
        [router, attn_gain[:, None], moe_gain[:, None], jnp.zeros((own_rows, LANES - experts - 2), BF16)], axis=1
    )
    w_blocks = gather_blocks(jnp.concatenate([qkv_weight, small], axis=1), size)
    p_blocks = gather_blocks(proj_weight, size)
    rev_buckets = jnp.roll(buckets[::-1], 1)
    table, slot_row, slot_col, cot_slots = prep(
        routes.T, segments, rev_buckets, rel_bias, cotangent, experts, capacity
    )
    (q, k, v, lse, att, res, n1, n2, logits, sent, qkv_full, proj_full, small_full, small_t) = front(
        me_arr, tokens, table, slot_row, w_blocks, p_blocks, experts, slots
    )

    def exchange(value):
        wide = value.shape[1]
        moved = lax.all_to_all(
            value.reshape(size, slots // size, wide), "shard", split_axis=0, concat_axis=0, tiled=True
        )
        return moved.reshape(slots, wide)

    cot_rows = exchange(cot_slots)
    rows = exchange(sent)
    win = expert_in[0]
    wout = expert_out[0]
    per_rank = hidden // ranks // 256
    act, gpre, buf0, rows_t, sg, sg_t = expert_chunk(
        True, (me_arr, rows, cot_rows, small_full, win, wout), (0, 1), ranks, slots, width, hidden
    )
    act, gpre, buf1 = expert_chunk(
        False, (rows, sg, rows_t, sg_t, win, wout, act, gpre), (1, per_rank - 1), ranks, slots, width, hidden
    )
    result = rows_out(False, act, wout, width)
    returned = exchange(result)
    grad_sent = rows_out(True, gpre, win, width)
    back = exchange(grad_sent)

    def scatter(buf):
        count, high, wide = buf.shape[1:]
        return lax.psum_scatter(
            buf.reshape(ranks * count * high, wide), "rep", scatter_dimension=0, tiled=True
        ).reshape(count, high, wide)

    done = [scatter(buf0), scatter(buf1)]
    output, gres, gatt, gproj, gsmall = mid(
        experts, returned, back, slot_col, res, logits, cotangent, n2, att, proj_full, small_full, small_t
    )
    pack, grad_tokens, gbias = tail(
        experts, bucket_count, tokens, table, q, k, v, gatt, lse, n1, gres, qkv_full, small_t,
        rev_buckets, gproj, gsmall,
    )
    grad_rel_bias = lax.psum(gbias, ("rep", "shard")).T
    owned = reduce_small(pack, me, size, ranks)

    pieces = jnp.concatenate(done, axis=0).astype(F32)
    part = width // ranks
    gin = pieces[:, :part, :].reshape(per_rank, part, ranks, 256)
    grad_in = gin.transpose(1, 2, 0, 3).reshape(1, part, hidden)
    piece = 256 // ranks
    gout = pieces[:, part:, :].reshape(per_rank, width // 256, piece, ranks, 256)
    grad_out = gout.transpose(0, 3, 2, 1, 4).reshape(1, hidden // ranks, width)
    return (
        output,
        grad_tokens,
        owned[:, : 3 * width],
        owned[:, 3 * width : 4 * width],
        owned[:, 4 * width : 4 * width + experts],
        owned[:, 4 * width + experts],
        owned[:, 4 * width + experts + 1],
        grad_rel_bias,
        grad_in,
        grad_out,
    )


def solution(mesh):
    both = P(("rep", "shard"), None)
    return jax.shard_map(
        body,
        mesh=mesh,
        in_specs=(
            both, both, P(("rep", "shard")), P(), both,
            P("shard"), P("shard", None), P("shard", None), P(), P("shard"), P("shard", None),
            P("shard", None, None), P("shard", None, None),
        ),
        out_specs=(
            both, both, P("shard", None), P("shard", None), P("shard", None), P("shard"), P("shard"), P(),
            P("shard", "rep", None), P("shard", "rep", None),
        ),
        check_vma=False,
    )
```

```python
import functools
import math

import jax
import jax.numpy as jnp
from jax import lax
from jax.experimental import pallas as pl
from jax.experimental.pallas import tpu as pltpu
from jax.sharding import PartitionSpec as P

F32 = jnp.float32
BF16 = jnp.bfloat16
EPS = 1e-06
NEG = -1e30
LANES = 128
HEAD_DIM = 64
GROUP = 256
VMEM_LIMIT = 60 * 1024 * 1024


def dot(a, b):
    return jnp.dot(a, b, preferred_element_type=F32)


def dot_nt(a, b):
    return lax.dot_general(a, b, (((1,), (1,)), ((), ())), preferred_element_type=F32)


def dot_tn(a, b):
    return lax.dot_general(a, b, (((0,), (0,)), ((), ())), preferred_element_type=F32)


def call(kernel, out_shape, **kw):
    flops = kw.pop("flops", 0)
    moved = kw.pop("moved", 0)
    return pl.pallas_call(
        kernel,
        out_shape=out_shape,
        compiler_params=pltpu.CompilerParams(vmem_limit_bytes=VMEM_LIMIT),
        cost_estimate=pl.CostEstimate(flops=flops, bytes_accessed=moved, transcendentals=0),
        **kw,
    )


def whole(shape):
    rank = len(shape)
    return pl.BlockSpec(shape, lambda *_: (0,) * rank)


def smem():
    return pl.BlockSpec(memory_space=pltpu.SMEM)


def sds(shape, dtype):
    return jax.ShapeDtypeStruct(shape, dtype)


def iota(shape, dim):
    return lax.broadcasted_iota(jnp.int32, shape, dim)


def prep_kernel(
    experts, capacity, routes_ref, seg_row, seg_col, rev_ref, bias_ref, cot_ref,
    table_ref, slot_row_ref, slot_col_ref, cot_out_ref, mask_scr, series_scr, extra_scr,
):
    step = pl.program_id(0)
    seq = cot_ref.shape[0]
    width = cot_ref.shape[1]
    per = cot_out_ref.shape[0]

    @pl.when(step == 0)
    def _():
        keep = (iota((seq, seq), 0) >= iota((seq, seq), 1)) & (seg_col[...] == seg_row[...])
        mask_scr[...] = jnp.where(keep, 0.0, NEG)
        rev = rev_ref[...]
        bias = bias_ref[...]
        series = jnp.zeros((bias.shape[0], seq), F32)
        for bucket in range(bias.shape[1]):
            series = jnp.where(rev == bucket, bias[:, bucket : bucket + 1], series)
        series_scr[...] = series
        first, second = routes_ref[0:1, :], routes_ref[1:2, :]
        ids = iota((experts, seq), 0)
        m0 = (ids == first).astype(F32)
        m1 = (ids == second).astype(F32)
        before = (iota((seq, seq), 0) < iota((seq, seq), 1)).astype(BF16)
        count = dot((m0 + m1).astype(BF16), before)
        rank0 = jnp.sum(count * m0, axis=0, keepdims=True)
        rank1 = jnp.sum(count * m1, axis=0, keepdims=True)
        r0, r1 = first.astype(F32), second.astype(F32)
        slot0 = jnp.where(rank0 < capacity, r0 * capacity + rank0, -1.0)
        slot1 = jnp.where(rank1 < capacity, r1 * capacity + rank1, -1.0)
        place = iota((LANES, seq), 0)
        rows = jnp.where(place == 0, slot0, -1.0)
        rows = jnp.where(place == 1, slot1, rows)
        rows = jnp.where(place == 2, r0, rows)
        rows = jnp.where(place == 3, r1, rows)
        slot_row_ref[...] = rows[0:8, :].astype(jnp.int32)
        cols = rows.T
        slot_col_ref[...] = cols
        lane = iota((seq, LANES), 1)
        extra_scr[0] = jnp.where(lane == 0, cols[:, 3:4], 0.0).astype(BF16)
        extra_scr[1] = jnp.where(lane == 0, cols[:, 2:3], 0.0).astype(BF16)

    row = series_scr[pl.ds(step, 1), :]
    table_ref[0] = pltpu.roll(jnp.broadcast_to(row, (seq, seq)), 0, 1, stride=1, stride_axis=0) + mask_scr[...]

    @pl.when(step < 8)
    def _():
        slots = iota((per, seq), 0) + step * per
        hit0 = (slots == slot_row_ref[0:1, :]).astype(F32)
        hit1 = (slots == slot_row_ref[1:2, :]).astype(F32)
        cot_out_ref[:, :width] = dot((hit0 + hit1).astype(BF16), cot_ref[...]).astype(BF16)
        cot_out_ref[:, width:] = (
            dot(hit0.astype(BF16), extra_scr[0]) + dot(hit1.astype(BF16), extra_scr[1])
        ).astype(BF16)


def prep(routes_t, segments, rev_buckets, rel_bias, cotangent, experts, capacity):
    seq, width = cotangent.shape
    heads = rel_bias.shape[1]
    buckets = rel_bias.shape[0]
    slots = experts * capacity
    per = slots // 8
    hp = -(-heads // 8) * 8
    bias_t = jnp.zeros((hp, buckets), F32).at[:heads].set(rel_bias.T)
    return call(
        functools.partial(prep_kernel, experts, capacity),
        [
            sds((heads, seq, seq), F32),
            sds((8, seq), jnp.int32),
            sds((seq, LANES), F32),
            sds((slots, width + LANES), BF16),
        ],
        grid=(heads,),
        in_specs=[
            whole((2, seq)), whole((1, seq)), whole((seq, 1)), whole((1, seq)),
            whole((hp, buckets)), whole((seq, width)),
        ],
        out_specs=[
            pl.BlockSpec((1, seq, seq), lambda h: (h, 0, 0)),
            whole((8, seq)),
            whole((seq, LANES)),
            pl.BlockSpec((per, width + LANES), lambda h: (jnp.minimum(h, 7), 0)),
        ],
        scratch_shapes=[
            pltpu.VMEM((seq, seq), F32),
            pltpu.VMEM((hp, seq), F32),
            pltpu.VMEM((2, seq, LANES), BF16),
        ],
        flops=2 * slots * seq * width,
        moved=heads * seq * seq * 4 + 4 * seq * width,
        name="prep",
    )(routes_t, segments[None, :], segments[:, None], rev_buckets[None, :], bias_t, cotangent)


def front_kernel(
    blocks, experts, me_ref, tokens_ref, table_ref, slot_row_ref, *refs,
):
    w_in = refs[:blocks]
    (q_ref, k_ref, v_ref, lse_ref, att_ref, res_ref, n1_ref, n2_ref, logit_ref, sent_ref,
     small_ref, small_t_ref, qkv_ref, proj_ref) = refs[blocks:]
    step = pl.program_id(0)
    last = pl.num_programs(0) - 1
    seq, width = tokens_ref.shape
    rows = w_in[0].shape[0]
    scale = HEAD_DIM ** (-0.5)

    @pl.when(step == 0)
    def _():
        me = me_ref[0]
        for j in range(blocks):
            start = pl.multiple_of((me ^ j) * rows, rows) if blocks > 1 else 0
            qkv_ref[pl.ds(start, rows), :] = w_in[j][:, : 3 * width]
            proj_ref[pl.ds(start, rows), :] = w_in[j][:, 3 * width : 4 * width]
            small_ref[pl.ds(start, rows), :] = w_in[j][:, 4 * width :]
        small_t_ref[...] = small_ref[...].astype(F32).T
        x = tokens_ref[...].astype(F32)
        r = lax.rsqrt(jnp.mean(x * x, axis=-1, keepdims=True) + EPS)
        n1_ref[...] = (x * r * small_t_ref[experts : experts + 1, :]).astype(BF16)
        lse_ref[...] = jnp.zeros_like(lse_ref)

    base = pl.multiple_of(step * GROUP, GROUP)
    n1 = n1_ref[...]
    q_ref[...] = dot(n1, qkv_ref[:, pl.ds(base, GROUP)]).astype(BF16)
    k_ref[...] = dot(n1, qkv_ref[:, pl.ds(width + base, GROUP)]).astype(BF16)
    v_ref[...] = dot(n1, qkv_ref[:, pl.ds(2 * width + base, GROUP)]).astype(BF16)

    half = seq // 2
    lane = iota((half, LANES), 1)
    for pair in range(GROUP // LANES):
        cols = slice(pair * LANES, (pair + 1) * LANES)
        for rb in range(2):
            span = (rb + 1) * half
            qrows = slice(rb * half, (rb + 1) * half)
            qp = q_ref[qrows, cols]
            kp = k_ref[:span, cols]
            vp = v_ref[:span, cols]
            mixed = []
            for parity in range(2):
                mine = (lane // HEAD_DIM) == parity
                qm = jnp.where(mine, qp, jnp.zeros_like(qp))
                s = dot_nt(qm, kp) * scale + table_ref[2 * pair + parity, qrows, :span]
                top = jnp.max(s, axis=-1, keepdims=True)
                e = jnp.exp(s - top)
                total = jnp.sum(e, axis=-1, keepdims=True)
                p = (e * (1.0 / total)).astype(BF16)
                mixed.append(dot(p, vp))
                head = step * (GROUP // HEAD_DIM) + 2 * pair + parity
                lse_ref[qrows, :] = jnp.where(lane == head, top + jnp.log(total), lse_ref[qrows, :])
            at = pl.multiple_of(base + pair * LANES, LANES)
            att_ref[qrows, pl.ds(at, LANES)] = jnp.where(lane < HEAD_DIM, mixed[0], mixed[1]).astype(BF16)

    @pl.when(step == last)
    def _():
        x = tokens_ref[...].astype(F32) + dot(att_ref[...], proj_ref[...])
        res_ref[...] = x
        r = lax.rsqrt(jnp.mean(x * x, axis=-1, keepdims=True) + EPS)
        n2 = (x * r * small_t_ref[experts + 1 : experts + 2, :]).astype(BF16)
        n2_ref[...] = n2
        logit_ref[...] = dot(n2, small_ref[...])
        per = sent_ref.shape[0] // 8
        for e in range(8):
            slots = iota((per, seq), 0) + e * per
            hit = (slots == slot_row_ref[0:1, :]) | (slots == slot_row_ref[1:2, :])
            sent_ref[e * per : (e + 1) * per, :] = dot(hit.astype(BF16), n2).astype(BF16)


def front(me, tokens, table, slot_row, w_blocks, experts, slots):
    seq, width = tokens.shape
    blocks = len(w_blocks)
    groups = width // GROUP
    per_group = GROUP // HEAD_DIM
    col = pl.BlockSpec((seq, GROUP), lambda g: (0, g))
    return call(
        functools.partial(front_kernel, blocks, experts),
        [
            sds((seq, width), BF16), sds((seq, width), BF16), sds((seq, width), BF16),
            sds((seq, LANES), F32), sds((seq, width), BF16), sds((seq, width), F32),
            sds((seq, width), BF16), sds((seq, width), BF16), sds((seq, LANES), F32),
            sds((slots, width), BF16),
            sds((width, LANES), BF16), sds((LANES, width), F32),
        ],
        grid=(groups,),
        in_specs=[
            smem(), whole((seq, width)),
            pl.BlockSpec((per_group, seq, seq), lambda g: (g, 0, 0)),
            whole((8, seq)),
        ]
        + [whole(b.shape) for b in w_blocks],
        out_specs=[
            col, col, col,
            whole((seq, LANES)), whole((seq, width)), whole((seq, width)),
            whole((seq, width)), whole((seq, width)), whole((seq, LANES)),
            whole((slots, width)),
            whole((width, LANES)), whole((LANES, width)),
        ],
        scratch_shapes=[pltpu.VMEM((width, 3 * width), BF16), pltpu.VMEM((width, width), BF16)],
        flops=2 * seq * width * width * 4 + 2 * slots * seq * width + 8 * seq * seq * width,
        moved=30_000_000,
        name="front",
    )(me, tokens, table, slot_row, *w_blocks)


def assemble_kernel(blocks, me_ref, *refs):
    qkv_ref, proj_ref = refs[-2:]
    wide = qkv_ref.shape[1]
    high = proj_ref.shape[1]
    for j in range(blocks):
        rows = refs[j].shape[0]
        start = pl.multiple_of((me_ref[0] ^ j) * rows, rows) if blocks > 1 else 0
        qkv_ref[pl.ds(start, rows), :] = refs[j][:, :wide]
        proj_ref[pl.ds(start, rows), :] = refs[j][:, wide : wide + high]


def assemble(me, w_blocks, width):
    return call(
        functools.partial(assemble_kernel, len(w_blocks)),
        [sds((width, 3 * width), BF16), sds((width, width), BF16)],
        grid=(1,),
        in_specs=[smem()] + [whole(b.shape) for b in w_blocks],
        out_specs=[whole((width, 3 * width)), whole((width, width))],
        name="assemble",
    )(me, *w_blocks)


def gelu_parts(v):
    size = jnp.abs(v) * (2.0 ** -0.5)
    t = 1.0 / (1.0 + 0.3275911 * size)
    bell = jnp.exp(-0.5 * v * v)
    poly = t * (
        0.5 * 0.254829592
        + t * (0.5 * -0.284496736 + t * (0.5 * 1.421413741 + t * (0.5 * -1.453152027 + t * (0.5 * 1.061405429))))
    )
    tail = poly * bell
    below = jnp.where(v < 0, tail, 1.0 - tail)
    return v * below, below + v * bell * (1.0 / math.sqrt(2.0 * math.pi))


def expert_kernel(first, ranks, tile, *refs):
    if first:
        (me_ref, rows_ref, cotx_ref, small_ref, win_ref, wout_ref,
         act_ref, gp_ref, d_ref, buf_ref, rows_t, sg_ref, sg_t) = refs
    else:
        (rows_ref, sg_ref, rows_t, sg_t, win_ref, wout_ref, _a, _g,
         act_ref, gp_ref, d_ref, buf_ref) = refs
    step = pl.program_id(0)
    total, width = rows_ref.shape
    if first:

        @pl.when(step == 0)
        def _():
            me = me_ref[0]
            for at in range(0, total, tile):
                here = slice(at, at + tile)
                logits = dot(rows_ref[here, :], small_ref[...])
                lane = iota((tile, LANES), 1)
                other_id = cotx_ref[here, width : width + 1].astype(F32).astype(jnp.int32)
                own = jnp.sum(jnp.where(lane == me, logits, 0.0), axis=1, keepdims=True)
                other = jnp.sum(jnp.where(lane == other_id, logits, 0.0), axis=1, keepdims=True)
                top = jnp.maximum(own, other)
                a, b = jnp.exp(own - top), jnp.exp(other - top)
                gate = a / (a + b)
                sg_ref[here, :] = (gate * cotx_ref[here, :width].astype(F32)).astype(BF16)
            rows_t[...] = rows_ref[...].T
            sg_t[...] = sg_ref[...].T

    @pl.when(step == 0)
    def _():
        d_ref[...] = jnp.zeros_like(d_ref)

    w1 = win_ref[...]
    w2 = wout_ref[...]
    for at in range(0, total, tile):
        here = slice(at, at + tile)
        pre = dot(rows_ref[here, :], w1)
        ga = dot_nt(sg_ref[here, :], w2)
        act, slope = gelu_parts(pre)
        low = act.astype(BF16)
        act_ref[here, :] = low
        gp_ref[here, :] = (ga * slope).astype(BF16)
        d_ref[here, :] += jnp.sum(low.astype(F32) * ga, axis=1, keepdims=True)
    block = w1.shape[1]
    part = width // ranks
    gwin = dot(rows_t[...], gp_ref[...]).astype(BF16)
    gwout = dot(sg_t[...], act_ref[...]).T.astype(BF16)
    rank = lax.rem(step, ranks)
    cb = lax.div(step, ranks)
    lane0 = pl.multiple_of(rank * block, block)
    for dest in range(ranks):
        buf_ref[dest, cb, 0:part, pl.ds(lane0, block)] = gwin[dest * part : (dest + 1) * part, :]
    piece = block // ranks
    for i in range(ranks):
        for j in range(width // block):
            buf_ref[rank, cb, part + j * piece : part + (j + 1) * piece, i * block : (i + 1) * block] = gwout[
                i * piece : (i + 1) * piece, j * block : (j + 1) * block
            ]


def expert_chunk(first, ins, start, count, ranks, total, width, hidden):
    block = 256
    per_rank = hidden // ranks // block
    part = width // ranks
    piece = block // ranks
    high = part + (width // block) * piece
    wide = ranks * block

    def at(s):
        return lax.rem(s, ranks) * per_rank + start + lax.div(s, ranks)

    win_spec = pl.BlockSpec((width, block), lambda s: (0, at(s)))
    wout_spec = pl.BlockSpec((block, width), lambda s: (at(s), 0))
    col = pl.BlockSpec((total, block), lambda s: (0, at(s)))
    buf = (ranks, count, high, wide)
    outs = [sds((total, hidden), BF16), sds((total, hidden), BF16), sds((total, LANES), F32), sds(buf, BF16)]
    out_specs = [col, col, whole((total, LANES)), whole(buf)]
    kw = {}
    if first:
        in_specs = [smem(), whole((total, width)), whole((total, width + LANES)), whole((width, LANES)), win_spec, wout_spec]
        outs += [sds((width, total), BF16), sds((total, width), BF16), sds((width, total), BF16)]
        out_specs += [whole((width, total)), whole((total, width)), whole((width, total))]
    else:
        in_specs = [
            whole((total, width)), whole((total, width)), whole((width, total)), whole((width, total)),
            win_spec, wout_spec,
            pl.BlockSpec(memory_space=pl.ANY), pl.BlockSpec(memory_space=pl.ANY),
        ]
        kw["input_output_aliases"] = {6: 0, 7: 1}
    return call(
        functools.partial(expert_kernel, first, ranks, 256),
        outs,
        grid=(count * ranks,),
        in_specs=in_specs,
        out_specs=out_specs,
        flops=8 * total * width * block * ranks * count,
        moved=20_000_000,
        name="experts",
        **kw,
    )(*ins)


def rows_out_kernel(a_ref, w_ref, o_ref):
    o_ref[...] = dot(a_ref[...], w_ref[...]).astype(BF16)


def rows_back_kernel(a_ref, w_ref, *refs):
    o_ref = refs[-1]
    width = w_ref.shape[0]
    o_ref[:, :width] = dot_nt(a_ref[...], w_ref[...]).astype(BF16)
    d = refs[0][...]
    for other in refs[1:-1]:
        d = d + other[...]
    high = d.astype(BF16)
    low = (d - high.astype(F32)).astype(BF16)
    lane = iota(d.shape, 1)
    zero = jnp.zeros_like(d)
    o_ref[:, width:] = jnp.where(lane == 0, high.astype(F32), jnp.where(lane == 1, low.astype(F32), zero)).astype(BF16)


def rows_product(kernel, a, w, wide, extra, name):
    total, hidden = a.shape
    steps = 3
    tile = total // steps
    return call(
        kernel,
        sds((total, wide), BF16),
        grid=(steps,),
        in_specs=[pl.BlockSpec((tile, hidden), lambda i: (i, 0)), whole(w.shape)]
        + [pl.BlockSpec((tile, LANES), lambda i: (i, 0))] * len(extra),
        out_specs=pl.BlockSpec((tile, wide), lambda i: (i, 0)),
        flops=2 * total * hidden * wide,
        moved=2 * (total * hidden + hidden * wide + total * wide),
        name=name,
    )(a, w, *extra)


def norm_back(x, grad, gain):
    r = lax.rsqrt(jnp.mean(x * x, axis=-1, keepdims=True) + EPS)
    u = grad * gain
    inner = jnp.mean(u * x, axis=-1, keepdims=True)
    xr = x * r
    return r * u - (r * r * r) * x * inner, jnp.sum(grad * xr, axis=0, keepdims=True)


def pair_gates(slot_ref, logit_ref):
    logits = logit_ref[...]
    lane = iota(logits.shape, 1)
    hot0 = lane == slot_ref[:, 2:3].astype(jnp.int32)
    hot1 = lane == slot_ref[:, 3:4].astype(jnp.int32)
    c0 = jnp.sum(jnp.where(hot0, logits, 0.0), axis=1, keepdims=True)
    c1 = jnp.sum(jnp.where(hot1, logits, 0.0), axis=1, keepdims=True)
    top = jnp.maximum(c0, c1)
    e0, e1 = jnp.exp(c0 - top), jnp.exp(c1 - top)
    return e0 / (e0 + e1), e1 / (e0 + e1), hot0, hot1


def pair_hits(slot_ref, slots):
    spot = iota((slot_ref.shape[0], slots), 1)
    h0 = (spot == slot_ref[:, 0:1].astype(jnp.int32)).astype(BF16)
    h1 = (spot == slot_ref[:, 1:2].astype(jnp.int32)).astype(BF16)
    return h0, h1


def output_kernel(ret_ref, slot_ref, res_ref, logit_ref, out_ref):
    h0, h1 = pair_hits(slot_ref, ret_ref.shape[0])
    g0, g1, _, _ = pair_gates(slot_ref, logit_ref)
    ret = ret_ref[...]
    out_ref[...] = (res_ref[...] + (g0 * dot(h0, ret) + g1 * dot(h1, ret))).astype(BF16)


def output_rows(returned, slot_col, res, logits):
    ins = (returned, slot_col, res, logits)
    return call(
        output_kernel,
        sds(res.shape, BF16),
        grid=(1,),
        in_specs=[whole(x.shape) for x in ins],
        out_specs=whole(res.shape),
        flops=4 * returned.shape[0] * res.size,
        moved=6_000_000,
        name="output_rows",
    )(*ins)


def mid_kernel(
    experts, back_ref, slot_ref, res_ref, logit_ref, cot_ref, n2_ref, att_ref,
    proj_ref, small_ref, small_t_ref, gres_ref, gatt_ref, gpack_ref,
):
    seq, width = res_ref.shape
    h0, h1 = pair_hits(slot_ref, back_ref.shape[0])
    g0, g1, hot0, hot1 = pair_gates(slot_ref, logit_ref)
    back = back_ref[:, :width]
    sides = back_ref[:, width:]
    d0 = jnp.sum(dot(h0, sides), axis=1, keepdims=True)
    d1 = jnp.sum(dot(h1, sides), axis=1, keepdims=True)
    glog = jnp.where(hot0, d0 - g0 * (d0 + d1), 0.0) + jnp.where(hot1, d1 - g1 * (d0 + d1), 0.0)
    glog = glog.astype(BF16)
    x = res_ref[...]
    small = small_ref[...]
    router = jnp.where(iota((width, LANES), 1) < experts, small, jnp.zeros_like(small))
    grad = dot(h0 + h1, back) + dot_nt(glog, router)
    gx, ggain = norm_back(x, grad, small_t_ref[experts + 1 : experts + 2, :])
    gres = gx + cot_ref[...].astype(F32)
    gres_ref[...] = gres
    branch = gres.astype(BF16)
    gatt_ref[...] = dot_nt(branch, proj_ref[...]).astype(BF16)
    gpack_ref[:, :width] = dot_tn(att_ref[...], branch).astype(BF16)
    gain_rows = jnp.where(iota((LANES, width), 0) == experts + 1, ggain, 0.0)
    gpack_ref[:, width:] = (dot_tn(n2_ref[...], glog) + gain_rows.T).astype(BF16)


def mid(experts, back, slot_col, res, logits, cot, n2, att, proj, small, small_t):
    seq, width = res.shape
    ins = (back, slot_col, res, logits, cot, n2, att, proj, small, small_t)
    return call(
        functools.partial(mid_kernel, experts),
        [sds((seq, width), F32), sds((seq, width), BF16), sds((width, width + LANES), BF16)],
        in_specs=[whole(a.shape) for a in ins],
        out_specs=[whole((seq, width)), whole((seq, width)), whole((width, width + LANES))],
        grid=(1,),
        flops=2 * back.shape[0] * seq * width + 4 * seq * width * width,
        moved=12_000_000,
        name="token_side",
    )(*ins)


def heads_back(group, table_ref, q_ref, k_ref, v_ref, gatt_ref, lse_ref, g_scr, diag_ref):
    seq = q_ref.shape[0]
    half = seq // 2
    scale = HEAD_DIM ** (-0.5)
    lane = iota((half, LANES), 1)
    full_lane = iota((seq, LANES), 1)
    for pair in range(GROUP // LANES):
        cols = slice(pair * LANES, (pair + 1) * LANES)
        dk = [jnp.zeros((seq, LANES), F32)] * 2
        dv = [jnp.zeros((seq, LANES), F32)] * 2
        skew = [jnp.zeros((LANES, seq), F32)] * 2
        for rb in range(2):
            span = (rb + 1) * half
            qrows = slice(rb * half, (rb + 1) * half)
            qp = q_ref[qrows, cols]
            gp = gatt_ref[qrows, cols]
            kp = k_ref[:span, cols]
            vp = v_ref[:span, cols]
            dq = []
            for parity in range(2):
                mine = (lane // HEAD_DIM) == parity
                head = group * (GROUP // HEAD_DIM) + 2 * pair + parity
                level = lse_ref[qrows, head : head + 1]
                qm = jnp.where(mine, qp, jnp.zeros_like(qp))
                gm = jnp.where(mine, gp, jnp.zeros_like(gp))
                s = dot_nt(qm, kp) * scale + table_ref[2 * pair + parity, qrows, :span]
                p = jnp.exp(s - level)
                dp = dot_nt(gm, vp)
                d = jnp.sum(p * dp, axis=1, keepdims=True)
                ds = p * (dp - d)
                low = ds.astype(BF16)
                dq.append(dot(low, kp) * scale)
                add_k = dot_tn(low, qp) * scale
                add_v = dot_tn(p.astype(BF16), gp)
                if span < seq:
                    zero = jnp.zeros((seq - span, LANES), F32)
                    add_k = jnp.concatenate([add_k, zero], axis=0)
                    add_v = jnp.concatenate([add_v, zero], axis=0)
                dk[parity] = dk[parity] + add_k
                dv[parity] = dv[parity] + add_v
                wide = low.astype(F32)
                if span < seq:
                    wide = jnp.concatenate([wide, jnp.zeros((half, seq - span), F32)], axis=1)
                for b in range(half // LANES):
                    shift = rb * half + b * LANES
                    rows = wide[b * LANES : (b + 1) * LANES, :]
                    if shift:
                        rows = jnp.concatenate([rows[:, shift:], rows[:, :shift]], axis=1)
                    skew[parity] = skew[parity] + rows
            g_scr[0, qrows, cols] = jnp.where(lane < HEAD_DIM, dq[0], dq[1]).astype(BF16)
        g_scr[1, :, cols] = jnp.where(full_lane < HEAD_DIM, dk[0], dk[1]).astype(BF16)
        g_scr[2, :, cols] = jnp.where(full_lane < HEAD_DIM, dv[0], dv[1]).astype(BF16)
        for parity in range(2):
            acc = skew[parity][0:8, :]
            for i in range(1, LANES // 8):
                acc = acc + pltpu.roll(skew[parity][i * 8 : (i + 1) * 8, :], seq - i * 8, 1)
            at = 8 * (2 * pair + parity)
            diag_ref[at : at + 8, :] = acc


def tail_kernel(group, *refs):
    (table_ref, q_ref, k_ref, v_ref, gatt_ref, lse_ref, n1_ref, wq_ref, wk_ref, wv_ref) = refs[:10]
    acc_in = refs[10] if group else None
    pack_ref, acc_ref, diag_ref, g_scr = refs[-4:]
    heads_back(group, table_ref, q_ref, k_ref, v_ref, gatt_ref, lse_ref, g_scr, diag_ref)
    acc = acc_in[...] if group else None
    for i, w_ref in enumerate((wq_ref, wk_ref, wv_ref)):
        g = g_scr[i]
        pack_ref[:, i * GROUP : (i + 1) * GROUP] = dot_tn(n1_ref[...], g).astype(BF16)
        more = dot_nt(g, w_ref[...])
        acc = more if acc is None else acc + more
    acc_ref[...] = acc


def tail(group, table, q, k, v, gatt, lse, n1, qkv, acc):
    seq, width = n1.shape
    groups = width // GROUP
    per_group = GROUP // HEAD_DIM
    col = pl.BlockSpec((seq, GROUP), lambda _: (0, group))

    def wcol(i):
        return pl.BlockSpec((width, GROUP), lambda _: (0, i * groups + group))

    return call(
        functools.partial(tail_kernel, group),
        [sds((width, 3 * GROUP), BF16), sds((seq, width), F32), sds((8 * per_group, seq), F32)],
        grid=(1,),
        in_specs=[
            pl.BlockSpec((per_group, seq, seq), lambda _: (group, 0, 0)),
            col, col, col, col,
            whole((seq, LANES)), whole((seq, width)),
            wcol(0), wcol(1), wcol(2),
        ]
        + [whole((seq, width))] * len(acc),
        out_specs=[whole((width, 3 * GROUP)), whole((seq, width)), whole((8 * per_group, seq))],
        scratch_shapes=[pltpu.VMEM((3, seq, GROUP), BF16)],
        flops=4 * seq * width * width + 7 * seq * seq * width,
        moved=10_000_000,
        name="tail",
    )(table, q, k, v, gatt, lse, n1, qkv, qkv, qkv, *acc)


def last_kernel(
    experts, own_rows, parts, tokens_ref, gres_ref, acc_ref, small_t_ref, rev_ref, *refs,
):
    diag_refs = refs[:parts]
    gtok_ref, small_ref = refs[parts:]
    seq, width = tokens_ref.shape
    x = tokens_ref[...].astype(F32)
    gx, ggain = norm_back(x, acc_ref[...], small_t_ref[experts : experts + 1, :])
    gtok_ref[...] = (gx + gres_ref[...]).astype(BF16)
    gain_rows = jnp.where(iota((LANES, width), 0) == experts, ggain, 0.0)
    diag = jnp.concatenate([d[...] for d in diag_refs], axis=0)
    count = diag.shape[0]
    place = lax.rem(iota((count, seq), 0), 8)
    total = jnp.where(place == 0, diag, 0.0)
    for r in range(1, 8):
        total = total + jnp.where(place == r, pltpu.roll(diag, seq - r, 1), 0.0)
    hot = (iota((LANES, seq), 0) - (experts + 2) == rev_ref[...]).astype(F32)
    per_row = lax.dot_general(
        total, hot, (((1,), (1,)), ((), ())), precision=lax.Precision.HIGHEST, preferred_element_type=F32
    )
    copies = (lax.rem(iota((width, count), 0), own_rows) == lax.div(iota((width, count), 1), 8)).astype(F32)
    spread = jnp.dot(copies, per_row, precision=lax.Precision.HIGHEST, preferred_element_type=F32)
    small_ref[...] = (gain_rows.T + spread).astype(BF16)


def last(experts, own_rows, tokens, gres, acc, small_t, rev_buckets, diags):
    seq, width = tokens.shape
    ins = (tokens, gres, acc, small_t, rev_buckets[None, :], *diags)
    return call(
        functools.partial(last_kernel, experts, own_rows, len(diags)),
        [sds((seq, width), BF16), sds((width, LANES), BF16)],
        grid=(1,),
        in_specs=[whole(x.shape) for x in ins],
        out_specs=[whole((seq, width)), whole((width, LANES))],
        moved=5_000_000,
        name="last",
    )(*ins)


def swap(value, mask, size):
    return lax.ppermute(value, "shard", [(i, i ^ mask) for i in range(size)])


def gather_blocks(value, size, beside):
    if size != 8:
        return [lax.all_gather(value, "shard", axis=0, tiled=True)], beside
    one, six, two, four = (swap(value, j, size) for j in (1, 6, 2, 4))
    one, six, two, four, *beside = lax.optimization_barrier((one, six, two, four, *beside))
    far = {0: value, 1: one, 6: six, 2: two, 4: four}
    near = {j ^ 1: swap(far[j], 1, size) for j in (6, 2, 4)}
    return [far[j] if j in far else near[j] for j in range(8)], beside


def tie(*values):
    return lax.optimization_barrier(values)


def inward(value):
    return lax.ppermute(value, "rep", [(0, 1), (3, 2)])


def across(value):
    return lax.ppermute(value, "rep", [(1, 2), (2, 1)])


def outward(value):
    return lax.ppermute(value, "rep", [(1, 0), (2, 3)])


def add(*values):
    total = values[0].astype(F32)
    for value in values[1:]:
        total = total + value.astype(F32)
    return total.astype(BF16)


def line_total(value, at_end):
    near = add(value, inward(value))
    total = add(near, across(near))
    return jnp.where(at_end, outward(total), total)


def finish_kernel(width, src_ref, *refs):
    in_ref, out_ref = refs[-2:]
    total = src_ref[0].astype(F32)
    part, block = in_ref.shape
    piece = out_ref.shape[0]
    in_ref[...] = total[:part, :]
    for j in range(width // block):
        out_ref[:, j * block : (j + 1) * block] = total[part + j * piece : part + (j + 1) * piece, :]


def finish(src, start, earlier, width, hidden, ranks):
    count, high, wide = src.shape
    block = wide // ranks
    part = width // ranks
    piece = block // ranks
    per_rank = hidden // ranks // block
    return call(
        functools.partial(finish_kernel, width),
        [sds((part, hidden), F32), sds((hidden // ranks, width), F32)],
        grid=(count, ranks),
        in_specs=[pl.BlockSpec((1, high, block), lambda c, r: (c, 0, r))]
        + [pl.BlockSpec(memory_space=pl.ANY)] * len(earlier),
        out_specs=[
            pl.BlockSpec((part, block), lambda c, r: (0, r * per_rank + start + c)),
            pl.BlockSpec((piece, width), lambda c, r: ((start + c) * ranks + r, 0)),
        ],
        input_output_aliases={1: 0, 2: 1} if earlier else {},
        name="finish",
    )(src, *earlier)


def chip_sum(pack, me, size):
    if size != 8:
        return pack
    blocks = pack.reshape(4, 2, pack.shape[0] // size, pack.shape[1])
    core = me % 2
    keep = lax.dynamic_index_in_dim(blocks, core, 1, keepdims=False)
    send = lax.dynamic_index_in_dim(blocks, 1 - core, 1, keepdims=False)
    return add(keep, swap(send, 1, size))


def group_sum(both, me, size):
    if size != 8:
        return lax.psum_scatter(both, "shard", scatter_dimension=0, tiled=True)
    chip = me // 2
    got = [swap(lax.dynamic_index_in_dim(both, chip ^ (j // 2), 0, keepdims=False), j, size) for j in (6, 2, 4)]
    return add(lax.dynamic_index_in_dim(both, chip, 0, keepdims=False), *got)


def body(
    tokens, cotangent, segments, buckets, routes, attn_gain, qkv_weight, proj_weight,
    rel_bias, moe_gain, router, expert_in, expert_out,
):
    seq, width = tokens.shape
    size = lax.axis_size("shard")
    ranks = lax.axis_size("rep")
    top = routes.shape[1]
    experts = expert_in.shape[0] * size
    hidden = expert_in.shape[2]
    capacity = 3 * seq * top // (2 * experts)
    slots = experts * capacity
    bucket_count = rel_bias.shape[0]
    me = lax.axis_index("shard").astype(jnp.int32)
    me_arr = me.reshape(1)
    own_rows = router.shape[0]

    small = jnp.concatenate(
        [router, attn_gain[:, None], moe_gain[:, None], jnp.zeros((own_rows, LANES - experts - 2), BF16)], axis=1
    )
    packed = jnp.concatenate([qkv_weight, proj_weight, small], axis=1)
    rev_buckets = jnp.roll(buckets[::-1], 1)
    w_blocks, (table, slot_row, slot_col, cot_slots) = gather_blocks(
        packed, size, prep(routes.T, segments, rev_buckets, rel_bias, cotangent, experts, capacity)
    )
    (q, k, v, lse, att, res, n1, n2, logits, sent, small_full, small_t) = front(
        me_arr, tokens, table, slot_row, w_blocks, experts, slots
    )
    me_late, logits = tie(me_arr, logits)
    qkv_full, proj_full = assemble(me_late, w_blocks, width)

    def exchange(value):
        wide = value.shape[1]
        moved = lax.all_to_all(
            value.reshape(size, slots // size, wide), "shard", split_axis=0, concat_axis=0, tiled=True
        )
        return moved.reshape(slots, wide)

    cot_rows = exchange(cot_slots)
    cot_rows, sent = tie(cot_rows, sent)
    rows = exchange(sent)
    win = expert_in[0]
    wout = expert_out[0]
    rank = lax.axis_index("rep").astype(jnp.int32)
    at_end = (rank == 0) | (rank == ranks - 1)
    per_rank = hidden // ranks // 256

    def scatter(buf):
        count, high, wide = buf.shape[1:]
        moved = lax.psum_scatter(buf.reshape(ranks * count * high, wide), "rep", scatter_dimension=0, tiled=True)
        return moved.reshape(count, high, wide)

    def chunk_of(first, ins, start, count):
        return expert_chunk(first, ins, start, count, ranks, slots, width, hidden)

    qkv_full, proj_full, rows = tie(qkv_full, proj_full, rows)
    act, gpre, d0, buf0, rows_t, sg, sg_t = chunk_of(True, (me_arr, rows, cot_rows, small_full, win, wout), 0, 1)
    part0 = scatter(buf0)
    act, gpre, d1, buf1 = chunk_of(False, (rows, sg, rows_t, sg_t, win, wout, act, gpre), 1, per_rank - 1)
    grad_sent = rows_product(rows_back_kernel, gpre, win, width + LANES, (d0, d1), "expert_rows_back")
    back = exchange(grad_sent)
    act, part0 = tie(act, part0)
    part1 = scatter(buf1)
    result = rows_product(rows_out_kernel, act, wout, width, (), "expert_rows_out")
    back, result = tie(back, result)
    returned = exchange(result)
    gres, gatt, gproj = mid(experts, back, slot_col, res, logits, cotangent, n2, att, proj_full, small_full, small_t)
    groups = width // GROUP
    packs, diags, acc = [], [], ()

    def tail_of(group, gatt):
        pack, total, diag = tail(group, table, q, k, v, gatt, lse, n1, qkv_full, acc)
        packs.append(pack)
        diags.append(diag)
        return (total,)

    acc = tail_of(0, gatt)
    sum_a = chip_sum(gproj, me, size)
    gatt, sum_a = tie(gatt, sum_a)
    acc = tail_of(1, gatt)
    owned_a = group_sum(sum_a, me, size)
    sum_b = chip_sum(jnp.concatenate(packs, axis=1), me, size)
    gatt, owned_a, returned, sum_b = tie(gatt, owned_a, returned, sum_b)
    acc = tail_of(2, gatt)
    grad_tokens, gsmall = last(experts, own_rows, tokens, gres, acc[0], small_t, rev_buckets, diags)
    sum_c = chip_sum(jnp.concatenate(packs[2:] + [gsmall], axis=1), me, size)
    owned_a = line_total(owned_a, at_end).astype(F32)
    owned_b = line_total(group_sum(sum_b, me, size), at_end).astype(F32)
    owned_c = line_total(group_sum(sum_c, me, size), at_end).astype(F32)
    output = output_rows(returned, slot_col, res, logits)
    done = finish(part0, 0, (), width, hidden, ranks)
    done = finish(part1, 1, done, width, hidden, ranks)
    grad_in, grad_out = done[0][None], done[1][None]
    heads = rel_bias.shape[1]
    small_at = 3 * GROUP
    bias_at = small_at + experts + 2
    by_group = jnp.concatenate([owned_b, owned_c[:, :small_at]], axis=1)
    grad_qkv = by_group.reshape(own_rows, groups, 3, GROUP).transpose(0, 2, 1, 3).reshape(own_rows, 3 * width)
    return (
        output,
        grad_tokens,
        grad_qkv,
        owned_a[:, :width],
        owned_a[:, width : width + experts],
        owned_c[:, small_at + experts],
        owned_a[:, width + experts + 1],
        owned_c[:heads, bias_at : bias_at + bucket_count].T,
        grad_in,
        grad_out,
    )


def solution(mesh):
    both = P(("rep", "shard"), None)
    return jax.shard_map(
        body,
        mesh=mesh,
        in_specs=(
            both, both, P(("rep", "shard")), P(), both,
            P("shard"), P("shard", None), P("shard", None), P(), P("shard"), P("shard", None),
            P("shard", None, None), P("shard", None, None),
        ),
        out_specs=(
            both, both, P("shard", None), P("shard", None), P("shard", None), P("shard"), P("shard"), P(),
            P("shard", "rep", None), P("shard", "rep", None),
        ),
        check_vma=False,
    )
```

```python
import functools
import math

import jax
import jax.numpy as jnp
from jax import lax
from jax.experimental import pallas as pl
from jax.experimental.pallas import tpu as pltpu
from jax.sharding import PartitionSpec as P

F32 = jnp.float32
BF16 = jnp.bfloat16
EPS = 1e-06
NEG = -1e30
LANES = 128
HEAD_DIM = 64
GROUP = 256
BLOCK = 256
VMEM_LIMIT = 60 * 1024 * 1024


def dot(a, b):
    return jnp.dot(a, b, preferred_element_type=F32)


def dot_nt(a, b):
    return lax.dot_general(a, b, (((1,), (1,)), ((), ())), preferred_element_type=F32)


def dot_tn(a, b):
    return lax.dot_general(a, b, (((0,), (0,)), ((), ())), preferred_element_type=F32)


def call(kernel, out_shape, **kw):
    flops = kw.pop("flops", 0)
    moved = kw.pop("moved", 0)
    return pl.pallas_call(
        kernel,
        out_shape=out_shape,
        compiler_params=pltpu.CompilerParams(vmem_limit_bytes=VMEM_LIMIT),
        cost_estimate=pl.CostEstimate(flops=flops, bytes_accessed=moved, transcendentals=0),
        **kw,
    )


def whole(shape):
    rank = len(shape)
    return pl.BlockSpec(shape, lambda *_: (0,) * rank)


def smem():
    return pl.BlockSpec(memory_space=pltpu.SMEM)


def sds(shape, dtype):
    return jax.ShapeDtypeStruct(shape, dtype)


def iota(shape, dim):
    return lax.broadcasted_iota(jnp.int32, shape, dim)


def prep_kernel(
    experts, capacity, routes_ref, seg_row, seg_col, rev_ref, bias_ref, cot_ref,
    table_ref, slot_row_ref, slot_col_ref, cot_out_ref, mask_scr, series_scr, extra_scr,
):
    step = pl.program_id(0)
    seq = cot_ref.shape[0]
    width = cot_ref.shape[1]
    per = cot_out_ref.shape[0]

    @pl.when(step == 0)
    def _():
        keep = (iota((seq, seq), 0) >= iota((seq, seq), 1)) & (seg_col[...] == seg_row[...])
        mask_scr[...] = jnp.where(keep, 0.0, NEG)
        rev = rev_ref[...]
        bias = bias_ref[...]
        series = jnp.zeros((bias.shape[0], seq), F32)
        for bucket in range(bias.shape[1]):
            series = jnp.where(rev == bucket, bias[:, bucket : bucket + 1], series)
        series_scr[...] = series
        first, second = routes_ref[0:1, :], routes_ref[1:2, :]
        ids = iota((experts, seq), 0)
        m0 = (ids == first).astype(F32)
        m1 = (ids == second).astype(F32)
        before = (iota((seq, seq), 0) < iota((seq, seq), 1)).astype(BF16)
        count = dot((m0 + m1).astype(BF16), before)
        rank0 = jnp.sum(count * m0, axis=0, keepdims=True)
        rank1 = jnp.sum(count * m1, axis=0, keepdims=True)
        r0, r1 = first.astype(F32), second.astype(F32)
        slot0 = jnp.where(rank0 < capacity, r0 * capacity + rank0, -1.0)
        slot1 = jnp.where(rank1 < capacity, r1 * capacity + rank1, -1.0)
        place = iota((LANES, seq), 0)
        rows = jnp.where(place == 0, slot0, -1.0)
        rows = jnp.where(place == 1, slot1, rows)
        rows = jnp.where(place == 2, r0, rows)
        rows = jnp.where(place == 3, r1, rows)
        slot_row_ref[...] = rows[0:8, :].astype(jnp.int32)
        cols = rows.T
        slot_col_ref[...] = cols
        lane = iota((seq, LANES), 1)
        extra_scr[0] = jnp.where(lane == 0, cols[:, 3:4], 0.0).astype(BF16)
        extra_scr[1] = jnp.where(lane == 0, cols[:, 2:3], 0.0).astype(BF16)

    row = series_scr[pl.ds(step, 1), :]
    table_ref[0] = pltpu.roll(jnp.broadcast_to(row, (seq, seq)), 0, 1, stride=1, stride_axis=0) + mask_scr[...]

    @pl.when(step < 8)
    def _():
        slots = iota((per, seq), 0) + step * per
        hit0 = (slots == slot_row_ref[0:1, :]).astype(F32)
        hit1 = (slots == slot_row_ref[1:2, :]).astype(F32)
        cot_out_ref[:, :width] = dot((hit0 + hit1).astype(BF16), cot_ref[...]).astype(BF16)
        cot_out_ref[:, width:] = (
            dot(hit0.astype(BF16), extra_scr[0]) + dot(hit1.astype(BF16), extra_scr[1])
        ).astype(BF16)


def prep(routes_t, segments, rev_buckets, rel_bias, cotangent, experts, capacity):
    seq, width = cotangent.shape
    heads = rel_bias.shape[1]
    buckets = rel_bias.shape[0]
    slots = experts * capacity
    per = slots // 8
    hp = -(-heads // 8) * 8
    bias_t = jnp.zeros((hp, buckets), F32).at[:heads].set(rel_bias.T)
    return call(
        functools.partial(prep_kernel, experts, capacity),
        [
            sds((heads, seq, seq), F32),
            sds((8, seq), jnp.int32),
            sds((seq, LANES), F32),
            sds((slots, width + LANES), BF16),
        ],
        grid=(heads,),
        in_specs=[
            whole((2, seq)), whole((1, seq)), whole((seq, 1)), whole((1, seq)),
            whole((hp, buckets)), whole((seq, width)),
        ],
        out_specs=[
            pl.BlockSpec((1, seq, seq), lambda h: (h, 0, 0)),
            whole((8, seq)),
            whole((seq, LANES)),
            pl.BlockSpec((per, width + LANES), lambda h: (jnp.minimum(h, 7), 0)),
        ],
        scratch_shapes=[
            pltpu.VMEM((seq, seq), F32),
            pltpu.VMEM((hp, seq), F32),
            pltpu.VMEM((2, seq, LANES), BF16),
        ],
        flops=2 * slots * seq * width,
        moved=heads * seq * seq * 4 + 4 * seq * width,
        name="prep",
    )(routes_t, segments[None, :], segments[:, None], rev_buckets[None, :], bias_t, cotangent)


def pack_kernel(qkv_ref, proj_ref, router_ref, gain_a, gain_b, out_ref):
    rows, width = proj_ref.shape
    experts = router_ref.shape[0]
    out_ref[:, : 3 * width] = qkv_ref[...]
    out_ref[:, 3 * width : 4 * width] = proj_ref[...]
    place = iota((LANES, rows), 0)
    a = gain_a[...].astype(F32).reshape(1, rows)
    b = gain_b[...].astype(F32).reshape(1, rows)
    gains = jnp.where(place == experts, a, jnp.where(place == experts + 1, b, 0.0))
    if rows < LANES:
        gains = jnp.concatenate([gains, jnp.zeros((LANES, LANES - rows), F32)], axis=1)
    spread = (iota((experts, LANES), 0) == iota((experts, LANES), 1)).astype(BF16)
    out_ref[:, 4 * width :] = (dot_tn(router_ref[...], spread) + gains.T[:rows, :]).astype(BF16)


def pack_weights(qkv, proj, router, gain_a, gain_b):
    rows, width = proj.shape
    ins = (qkv, proj, router, gain_a, gain_b)
    return call(
        pack_kernel,
        sds((rows, 4 * width + LANES), BF16),
        grid=(1,),
        in_specs=[whole(x.shape) for x in ins],
        out_specs=whole((rows, 4 * width + LANES)),
        name="pack_weights",
    )(*ins)


def front_kernel(
    blocks, experts, me_ref, tokens_ref, table_ref, slot_row_ref, *refs,
):
    w_in = refs[:blocks]
    (q_ref, k_ref, v_ref, lse_ref, att_ref, res_ref, n1_ref, n2_ref, logit_ref,
     small_ref, small_t_ref) = refs[blocks : blocks + 11]
    qkv_ref, proj_ref = refs[-2:]
    sent_refs = refs[blocks + 11 : -2]
    step = pl.program_id(0)
    last = pl.num_programs(0) - 1
    seq, width = tokens_ref.shape
    rows = w_in[0].shape[0]
    scale = HEAD_DIM ** (-0.5)

    @pl.when(step == 0)
    def _():
        me = me_ref[0]
        for j in range(blocks):
            start = pl.multiple_of((me ^ j) * rows, rows) if blocks > 1 else 0
            qkv_ref[pl.ds(start, rows), :] = w_in[j][:, : 3 * width]
            proj_ref[pl.ds(start, rows), :] = w_in[j][:, 3 * width : 4 * width]
            small_ref[pl.ds(start, rows), :] = w_in[j][:, 4 * width :]
        small_t_ref[...] = small_ref[...].astype(F32).T
        x = tokens_ref[...].astype(F32)
        r = lax.rsqrt(jnp.mean(x * x, axis=-1, keepdims=True) + EPS)
        n1_ref[...] = (x * r * small_t_ref[experts : experts + 1, :]).astype(BF16)
        lse_ref[...] = jnp.zeros_like(lse_ref)

    base = pl.multiple_of(step * GROUP, GROUP)
    n1 = n1_ref[...]
    q_ref[...] = dot(n1, qkv_ref[:, pl.ds(base, GROUP)]).astype(BF16)
    k_ref[...] = dot(n1, qkv_ref[:, pl.ds(width + base, GROUP)]).astype(BF16)
    v_ref[...] = dot(n1, qkv_ref[:, pl.ds(2 * width + base, GROUP)]).astype(BF16)

    half = seq // 2
    lane = iota((half, LANES), 1)
    for pair in range(GROUP // LANES):
        cols = slice(pair * LANES, (pair + 1) * LANES)
        for rb in range(2):
            span = (rb + 1) * half
            qrows = slice(rb * half, (rb + 1) * half)
            qp = q_ref[qrows, cols]
            kp = k_ref[:span, cols]
            vp = v_ref[:span, cols]
            mixed = []
            for parity in range(2):
                mine = (lane // HEAD_DIM) == parity
                qm = jnp.where(mine, qp, jnp.zeros_like(qp))
                s = dot_nt(qm, kp) * scale + table_ref[2 * pair + parity, qrows, :span]
                top = jnp.max(s, axis=-1, keepdims=True)
                e = jnp.exp(s - top)
                total = jnp.sum(e, axis=-1, keepdims=True)
                p = (e * (1.0 / total)).astype(BF16)
                mixed.append(dot(p, vp))
                head = step * (GROUP // HEAD_DIM) + 2 * pair + parity
                lse_ref[qrows, :] = jnp.where(lane == head, top + jnp.log(total), lse_ref[qrows, :])
            at = pl.multiple_of(base + pair * LANES, LANES)
            att_ref[qrows, pl.ds(at, LANES)] = jnp.where(lane < HEAD_DIM, mixed[0], mixed[1]).astype(BF16)

    @pl.when(step == last)
    def _():
        x = tokens_ref[...].astype(F32) + dot(att_ref[...], proj_ref[...])
        res_ref[...] = x
        r = lax.rsqrt(jnp.mean(x * x, axis=-1, keepdims=True) + EPS)
        n2 = (x * r * small_t_ref[experts + 1 : experts + 2, :]).astype(BF16)
        n2_ref[...] = n2
        logit_ref[...] = dot(n2, small_ref[...])
        many = len(sent_refs) > 1
        per = sent_refs[0].shape[0] if many else sent_refs[0].shape[0] // 8
        for j in range(8):
            slots = iota((per, seq), 0) + ((me_ref[0] ^ j) * per if many else j * per)
            hit = (slots == slot_row_ref[0:1, :]) | (slots == slot_row_ref[1:2, :])
            rows_j = dot(hit.astype(BF16), n2).astype(BF16)
            if many:
                sent_refs[j][...] = rows_j
            else:
                sent_refs[0][j * per : (j + 1) * per, :] = rows_j


def front(me, tokens, table, slot_row, w_blocks, experts, slots):
    seq, width = tokens.shape
    blocks = len(w_blocks)
    groups = width // GROUP
    per_group = GROUP // HEAD_DIM
    col = pl.BlockSpec((seq, GROUP), lambda g: (0, g))
    return call(
        functools.partial(front_kernel, blocks, experts),
        [
            sds((seq, width), BF16), sds((seq, width), BF16), sds((seq, width), BF16),
            sds((seq, LANES), F32), sds((seq, width), BF16), sds((seq, width), F32),
            sds((seq, width), BF16), sds((seq, width), BF16), sds((seq, LANES), F32),
            sds((width, LANES), BF16), sds((LANES, width), F32),
        ]
        + [sds((slots // blocks, width), BF16)] * blocks,
        grid=(groups,),
        in_specs=[
            smem(), whole((seq, width)),
            pl.BlockSpec((per_group, seq, seq), lambda g: (g, 0, 0)),
            whole((8, seq)),
        ]
        + [whole(b.shape) for b in w_blocks],
        out_specs=[
            col, col, col,
            whole((seq, LANES)), whole((seq, width)), whole((seq, width)),
            whole((seq, width)), whole((seq, width)), whole((seq, LANES)),
            whole((width, LANES)), whole((LANES, width)),
        ]
        + [whole((slots // blocks, width))] * blocks,
        scratch_shapes=[pltpu.VMEM((width, 3 * width), BF16), pltpu.VMEM((width, width), BF16)],
        flops=2 * seq * width * width * 4 + 2 * slots * seq * width + 8 * seq * seq * width,
        moved=30_000_000,
        name="front",
    )(me, tokens, table, slot_row, *w_blocks)


def assemble_kernel(blocks, me_ref, *refs):
    qkv_ref, proj_ref = refs[-2:]
    wide = qkv_ref.shape[1]
    high = proj_ref.shape[1]
    for j in range(blocks):
        rows = refs[j].shape[0]
        start = pl.multiple_of((me_ref[0] ^ j) * rows, rows) if blocks > 1 else 0
        qkv_ref[pl.ds(start, rows), :] = refs[j][:, :wide]
        proj_ref[pl.ds(start, rows), :] = refs[j][:, wide : wide + high]


def assemble(me, w_blocks, width):
    return call(
        functools.partial(assemble_kernel, len(w_blocks)),
        [sds((width, 3 * width), BF16), sds((width, width), BF16)],
        grid=(1,),
        in_specs=[smem()] + [whole(b.shape) for b in w_blocks],
        out_specs=[whole((width, 3 * width)), whole((width, width))],
        name="assemble",
    )(me, *w_blocks)


def gelu_parts(v):
    size = jnp.abs(v) * (2.0 ** -0.5)
    t = 1.0 / (1.0 + 0.3275911 * size)
    bell = jnp.exp(-0.5 * v * v)
    poly = t * (
        0.5 * 0.254829592
        + t * (0.5 * -0.284496736 + t * (0.5 * 1.421413741 + t * (0.5 * -1.453152027 + t * (0.5 * 1.061405429))))
    )
    tail = poly * bell
    below = jnp.where(v < 0, tail, 1.0 - tail)
    return v * below, below + v * bell * (1.0 / math.sqrt(2.0 * math.pi))


def join_rows(blocks, rows_ref):
    per = blocks[0].shape[0]
    for j, block in enumerate(blocks):
        rows_ref[j * per : (j + 1) * per, :] = block[...]


def gated_rows(me, parts, rows_ref, cotx_ref, small_ref, sg_ref):
    total, width = rows_ref.shape
    tile = total // 8
    for j in range(8):
        here = slice(j * tile, (j + 1) * tile)
        there = pl.ds(pl.multiple_of((me ^ j) * tile, tile), tile) if parts > 1 else here
        logits = dot(rows_ref[here, :], small_ref[...])
        lane = iota((tile, LANES), 1)
        other_id = cotx_ref[there, width:].astype(F32)[:, 0:1].astype(jnp.int32)
        own = jnp.sum(jnp.where(lane == me, logits, 0.0), axis=1, keepdims=True)
        other = jnp.sum(jnp.where(lane == other_id, logits, 0.0), axis=1, keepdims=True)
        top = jnp.maximum(own, other)
        a, b = jnp.exp(own - top), jnp.exp(other - top)
        gate = a / (a + b)
        sg_ref[here, :] = (gate * cotx_ref[there, :width].astype(F32)).astype(BF16)


def expert_acts(w1, w2, rows_ref, sg_ref, act_ref, gp_ref, d_ref, tile):
    for at in range(0, rows_ref.shape[0], tile):
        here = slice(at, at + tile)
        pre = dot(rows_ref[here, :], w1)
        ga = dot_nt(sg_ref[here, :], w2)
        act, slope = gelu_parts(pre)
        low = act.astype(BF16)
        act_ref[here, :] = low
        gp_ref[here, :] = (ga * slope).astype(BF16)
        d_ref[here, :] += jnp.sum(low.astype(F32) * ga, axis=1, keepdims=True)


def expert_weights(rows_t, sg_t, act_ref, gp_ref, buf_ref, cb, pair, ranks):
    width = rows_t.shape[0]
    block = BLOCK
    part = width // ranks
    piece = block // ranks
    gwin = dot(rows_t[...], gp_ref[...]).astype(BF16)
    lane0 = pl.multiple_of(pair * 2 * block, block)
    for dest in range(ranks):
        buf_ref[dest, cb, 0:part, pl.ds(lane0, 2 * block)] = gwin[dest * part : (dest + 1) * part, :]
    gwout = dot(sg_t[...], act_ref[...]).T.astype(BF16)
    for half in range(2):
        rank = 2 * pair + half
        for i in range(ranks):
            for j in range(width // block):
                buf_ref[rank, cb, part + j * piece : part + (j + 1) * piece, i * block : (i + 1) * block] = gwout[
                    half * block + i * piece : half * block + (i + 1) * piece, j * block : (j + 1) * block
                ]


def expert_first_kernel(
    ranks, tile, parts, me_ref, cotx_ref, small_ref, w1a, w1b, w2a, w2b, *refs,
):
    blocks = refs[:parts]
    act_ref, gp_ref, d_ref, buf_ref, sg_ref, rows_t, sg_t, rows_ref = refs[parts:]
    step = pl.program_id(0)

    @pl.when(step == 0)
    def _():
        join_rows(blocks, rows_ref)
        gated_rows(me_ref[0], parts, rows_ref, cotx_ref, small_ref, sg_ref)
        rows_t[...] = rows_ref[...].T
        sg_t[...] = sg_ref[...].T
        d_ref[...] = jnp.zeros_like(d_ref)

    w1 = jnp.concatenate([w1a[...], w1b[...]], axis=1)
    w2 = jnp.concatenate([w2a[...], w2b[...]], axis=0)
    expert_acts(w1, w2, rows_ref, sg_ref, act_ref, gp_ref, d_ref, tile)
    expert_weights(rows_t, sg_t, act_ref, gp_ref, buf_ref, 0, step, ranks)


def expert_rest_kernel(
    ranks, per_rank, start, tile, parts, sg_ref, win_ref, w2a, w2b, gp0_ref, d0_ref, *refs,
):
    blocks = refs[:parts]
    act_ref, gp_ref = refs[parts : parts + 2]
    back_refs = refs[parts + 2 : -3]
    gp_scr, d_scr, rows_ref = refs[-3:]
    step = pl.program_id(0)
    total, width = rows_ref.shape
    block = BLOCK

    @pl.when(step == 0)
    def _():
        join_rows(blocks, rows_ref)
        d_scr[...] = d0_ref[...]
        for c in range(start):
            for r in range(ranks):
                to = (r * per_rank + c) * block
                gp_scr[:, to : to + block] = gp0_ref[:, (c * ranks + r) * block : (c * ranks + r + 1) * block]

    pairs = ranks // 2
    cb, pair = lax.div(step, pairs), lax.rem(step, pairs)
    at_a = pl.multiple_of((2 * pair * per_rank + start + cb) * block, block)
    at_b = pl.multiple_of(((2 * pair + 1) * per_rank + start + cb) * block, block)
    w1 = jnp.concatenate([win_ref[:, pl.ds(at_a, block)], win_ref[:, pl.ds(at_b, block)]], axis=1)
    w2 = jnp.concatenate([w2a[...], w2b[...]], axis=0)
    expert_acts(w1, w2, rows_ref, sg_ref, act_ref, gp_ref, d_scr, tile)
    gp_scr[:, pl.ds(at_a, block)] = gp_ref[:, :block]
    gp_scr[:, pl.ds(at_b, block)] = gp_ref[:, block:]

    @pl.when(step == pl.num_programs(0) - 1)
    def _():
        per = total // 8
        join = 2
        for at in range(0, 8, join):
            here = slice(at * per, (at + join) * per)
            back = dot_nt(gp_scr[here, :], win_ref[...]).astype(BF16)
            d = d_scr[here, :]
            high = d.astype(BF16).astype(F32)
            lane = iota(d.shape, 1)
            side = jnp.where(lane == 0, high, jnp.where(lane == 1, d - high, 0.0)).astype(BF16)
            for i in range(join):
                inner = slice(i * per, (i + 1) * per)
                if parts > 1:
                    ref, to = back_refs[at + i], slice(0, per)
                else:
                    ref, to = back_refs[0], slice((at + i) * per, (at + i + 1) * per)
                ref[to, :width] = back[inner, :]
                ref[to, width:] = side[inner, :]


def expert_weights_kernel(ranks, parts, sg_ref, act_ref, gp_ref, *refs):
    blocks = refs[:parts]
    buf_ref, rows_t, sg_t = refs[parts:]
    step = pl.program_id(0)
    pairs = ranks // 2
    per = blocks[0].shape[0]

    @pl.when(step == 0)
    def _():
        if per % LANES and parts > 1:
            for j in range(0, parts, 2):
                pair = jnp.concatenate([blocks[j][...], blocks[j + 1][...]], axis=0)
                rows_t[:, j * per : (j + 2) * per] = pair.T
        else:
            for j, block in enumerate(blocks):
                rows_t[:, j * per : (j + 1) * per] = block[...].T
        sg_t[...] = sg_ref[...].T

    expert_weights(rows_t, sg_t, act_ref, gp_ref, buf_ref, lax.div(step, pairs), lax.rem(step, pairs), ranks)


def expert_weight_grads(blocks, sg, act, gp, hidden, ranks):
    total, width = sg.shape
    high, wide, per_rank = expert_sizes(width, hidden, ranks)
    count = act.shape[1] // wide
    buf = (ranks, count, high, wide)
    col = pl.BlockSpec((total, 2 * BLOCK), lambda s: (0, s))
    return call(
        functools.partial(expert_weights_kernel, ranks, len(blocks)),
        sds(buf, BF16),
        grid=(count * ranks // 2,),
        in_specs=[once((total, width)), col, col] + [once(b.shape) for b in blocks],
        out_specs=whole(buf),
        scratch_shapes=[pltpu.VMEM((width, total), BF16), pltpu.VMEM((width, total), BF16)],
        flops=4 * total * width * wide * count,
        moved=20_000_000,
        name="experts_weights",
    )(sg, act, gp, *blocks)


def once(shape):
    rank = len(shape)
    return pl.BlockSpec(shape, lambda *_: (0,) * rank, pipeline_mode=pl.Buffered(1))


def expert_sizes(width, hidden, ranks):
    high = width // ranks + (width // BLOCK) * (BLOCK // ranks)
    return high, ranks * BLOCK, hidden // ranks // BLOCK


def expert_first(me, blocks, cotx, small, win, wout, ranks):
    total = cotx.shape[0]
    width, hidden = win.shape
    high, wide, per_rank = expert_sizes(width, hidden, ranks)
    buf = (ranks, 1, high, wide)
    col = pl.BlockSpec((total, 2 * BLOCK), lambda s: (0, s))

    def win_spec(half):
        return pl.BlockSpec((width, BLOCK), lambda s: (0, (2 * s + half) * per_rank))

    def wout_spec(half):
        return pl.BlockSpec((BLOCK, width), lambda s: ((2 * s + half) * per_rank, 0))

    return call(
        functools.partial(expert_first_kernel, ranks, 256, len(blocks)),
        [
            sds((total, wide), BF16), sds((total, wide), BF16), sds((total, LANES), F32), sds(buf, BF16),
            sds((total, width), BF16),
        ],
        grid=(ranks // 2,),
        in_specs=[
            smem(), once((total, width + LANES)), once((width, LANES)),
            win_spec(0), win_spec(1), wout_spec(0), wout_spec(1),
        ]
        + [once(b.shape) for b in blocks],
        out_specs=[
            col, col, whole((total, LANES)), whole(buf), whole((total, width)),
        ],
        scratch_shapes=[
            pltpu.VMEM((width, total), BF16), pltpu.VMEM((width, total), BF16), pltpu.VMEM((total, width), BF16),
        ],
        flops=8 * total * width * wide,
        moved=20_000_000,
        name="experts_first",
    )(me, cotx, small, win, win, wout, wout, *blocks)


def expert_rest(blocks, sg, win, wout, gp0, d0, ranks):
    total, width = sg.shape
    hidden = win.shape[1]
    high, wide, per_rank = expert_sizes(width, hidden, ranks)
    start = 1
    count = per_rank - start
    pairs = ranks // 2
    parts = len(blocks)
    col = pl.BlockSpec((total, 2 * BLOCK), lambda s: (0, s))
    out = (total // parts, width + LANES)

    def wout_spec(half):
        return pl.BlockSpec(
            (BLOCK, width), lambda s: ((2 * lax.rem(s, pairs) + half) * per_rank + start + lax.div(s, pairs), 0)
        )

    return call(
        functools.partial(expert_rest_kernel, ranks, per_rank, start, 256, parts),
        [sds((total, count * wide), BF16), sds((total, count * wide), BF16)] + [sds(out, BF16)] * parts,
        grid=(count * pairs,),
        in_specs=[
            once((total, width)), once((width, hidden)), wout_spec(0), wout_spec(1),
            once((total, start * wide)), once((total, LANES)),
        ]
        + [once(b.shape) for b in blocks],
        out_specs=[col, col] + [whole(out)] * parts,
        scratch_shapes=[
            pltpu.VMEM((total, hidden), BF16), pltpu.VMEM((total, LANES), F32), pltpu.VMEM((total, width), BF16),
        ],
        flops=4 * total * width * wide * count + 2 * total * width * hidden,
        moved=30_000_000,
        name="experts_rest",
    )(sg, win, wout, wout, gp0, d0, *blocks)


def expert_rows_kernel(ranks, per_rank, parts, count, me_ref, *refs):
    acts, w_ref, o_ref, w_scr = refs[:count], refs[count], refs[count + 1], refs[count + 2]

    @pl.when(pl.program_id(0) == 0)
    def _():
        for c in range(per_rank):
            for r in range(ranks):
                to, src = (c * ranks + r) * BLOCK, (r * per_rank + c) * BLOCK
                w_scr[to : to + BLOCK, :] = w_ref[src : src + BLOCK, :]

    at, total = 0, None
    for act in acts:
        wide = act.shape[1]
        more = dot(act[...], w_scr[at : at + wide, :])
        total = more if total is None else total + more
        at += wide
    low = total.astype(BF16)
    if parts == 1:
        o_ref[...] = low
    else:
        per = low.shape[0] // 2
        flip = me_ref[0] % 2
        o_ref[pl.ds(pl.multiple_of(flip * per, per), per), :] = low[:per, :]
        o_ref[pl.ds(pl.multiple_of((1 - flip) * per, per), per), :] = low[per:, :]


def expert_rows(me, acts, wout, parts, ranks):
    total = acts[0].shape[0]
    hidden, width = wout.shape
    tile = total // 4

    def place(i, m):
        return ((m[0] // 2) ^ i if parts > 1 else i, 0)

    return pl.pallas_call(
        functools.partial(expert_rows_kernel, ranks, hidden // ranks // BLOCK, parts, len(acts)),
        sds((total, width), BF16),
        grid_spec=pltpu.PrefetchScalarGridSpec(
            num_scalar_prefetch=1,
            grid=(4,),
            in_specs=[pl.BlockSpec((tile, a.shape[1]), lambda i, m: (i, 0)) for a in acts] + [once(wout.shape)],
            out_specs=pl.BlockSpec((tile, width), place),
            scratch_shapes=[pltpu.VMEM(wout.shape, BF16)],
        ),
        compiler_params=pltpu.CompilerParams(vmem_limit_bytes=VMEM_LIMIT),
        name="expert_rows",
    )(me, *acts, wout)


def norm_back(x, grad, gain):
    r = lax.rsqrt(jnp.mean(x * x, axis=-1, keepdims=True) + EPS)
    u = grad * gain
    inner = jnp.mean(u * x, axis=-1, keepdims=True)
    xr = x * r
    return r * u - (r * r * r) * x * inner, jnp.sum(grad * xr, axis=0, keepdims=True)


def pair_gates(slot_ref, logit_ref):
    logits = logit_ref[...]
    lane = iota(logits.shape, 1)
    hot0 = lane == slot_ref[:, 2:3].astype(jnp.int32)
    hot1 = lane == slot_ref[:, 3:4].astype(jnp.int32)
    c0 = jnp.sum(jnp.where(hot0, logits, 0.0), axis=1, keepdims=True)
    c1 = jnp.sum(jnp.where(hot1, logits, 0.0), axis=1, keepdims=True)
    top = jnp.maximum(c0, c1)
    e0, e1 = jnp.exp(c0 - top), jnp.exp(c1 - top)
    return e0 / (e0 + e1), e1 / (e0 + e1), hot0, hot1


def pair_hits(slot_ref, slots):
    spot = iota((slot_ref.shape[0], slots), 1)
    h0 = (spot == slot_ref[:, 0:1].astype(jnp.int32)).astype(BF16)
    h1 = (spot == slot_ref[:, 1:2].astype(jnp.int32)).astype(BF16)
    return h0, h1


def output_kernel(ret_ref, slot_ref, res_ref, logit_ref, out_ref):
    h0, h1 = pair_hits(slot_ref, ret_ref.shape[0])
    g0, g1, _, _ = pair_gates(slot_ref, logit_ref)
    ret = ret_ref[...]
    out_ref[...] = (res_ref[...] + (g0 * dot(h0, ret) + g1 * dot(h1, ret))).astype(BF16)


def output_rows(returned, slot_col, res, logits):
    ins = (returned, slot_col, res, logits)
    return call(
        output_kernel,
        sds(res.shape, BF16),
        grid=(1,),
        in_specs=[whole(x.shape) for x in ins],
        out_specs=whole(res.shape),
        flops=4 * returned.shape[0] * res.size,
        moved=6_000_000,
        name="output_rows",
    )(*ins)


def heads_back(group, table_ref, q_ref, k_ref, v_ref, gatt_ref, lse_ref, g_scr, diag_ref):
    seq = q_ref.shape[0]
    half = seq // 2
    scale = HEAD_DIM ** (-0.5)
    lane = iota((half, LANES), 1)
    full_lane = iota((seq, LANES), 1)
    for pair in range(GROUP // LANES):
        cols = slice(pair * LANES, (pair + 1) * LANES)
        dk = [jnp.zeros((seq, LANES), F32)] * 2
        dv = [jnp.zeros((seq, LANES), F32)] * 2
        skew = [jnp.zeros((LANES, seq), F32)] * 2
        for rb in range(2):
            span = (rb + 1) * half
            qrows = slice(rb * half, (rb + 1) * half)
            qp = q_ref[qrows, cols]
            gp = gatt_ref[qrows, cols]
            kp = k_ref[:span, cols]
            vp = v_ref[:span, cols]
            dq = []
            for parity in range(2):
                mine = (lane // HEAD_DIM) == parity
                head = group * (GROUP // HEAD_DIM) + 2 * pair + parity
                level = jnp.sum(jnp.where(lane == head, lse_ref[qrows, :], 0.0), axis=1, keepdims=True)
                qm = jnp.where(mine, qp, jnp.zeros_like(qp))
                gm = jnp.where(mine, gp, jnp.zeros_like(gp))
                s = dot_nt(qm, kp) * scale + table_ref[2 * pair + parity, qrows, :span]
                p = jnp.exp(s - level)
                dp = dot_nt(gm, vp)
                d = jnp.sum(p * dp, axis=1, keepdims=True)
                ds = p * (dp - d)
                low = ds.astype(BF16)
                dq.append(dot(low, kp) * scale)
                add_k = dot_tn(low, qp) * scale
                add_v = dot_tn(p.astype(BF16), gp)
                if span < seq:
                    zero = jnp.zeros((seq - span, LANES), F32)
                    add_k = jnp.concatenate([add_k, zero], axis=0)
                    add_v = jnp.concatenate([add_v, zero], axis=0)
                dk[parity] = dk[parity] + add_k
                dv[parity] = dv[parity] + add_v
                wide = low.astype(F32)
                if span < seq:
                    wide = jnp.concatenate([wide, jnp.zeros((half, seq - span), F32)], axis=1)
                for b in range(half // LANES):
                    shift = rb * half + b * LANES
                    rows = wide[b * LANES : (b + 1) * LANES, :]
                    if shift:
                        rows = jnp.concatenate([rows[:, shift:], rows[:, :shift]], axis=1)
                    skew[parity] = skew[parity] + rows
            g_scr[0, qrows, cols] = jnp.where(lane < HEAD_DIM, dq[0], dq[1]).astype(BF16)
        g_scr[1, :, cols] = jnp.where(full_lane < HEAD_DIM, dk[0], dk[1]).astype(BF16)
        g_scr[2, :, cols] = jnp.where(full_lane < HEAD_DIM, dv[0], dv[1]).astype(BF16)
        for parity in range(2):
            acc = skew[parity][0:8, :]
            for i in range(1, LANES // 8):
                acc = acc + pltpu.roll(skew[parity][i * 8 : (i + 1) * 8, :], seq - i * 8, 1)
            at = 8 * (2 * pair + parity)
            diag_ref[at : at + 8, :] = acc


class Parted:
    def __init__(self, size, rows, refs, scratch):
        self.size, self.rows, self.refs, self.scratch = size, rows, refs, scratch

    def put(self, core, value, lanes):
        if self.size != 8:
            self.refs[0][:, lanes] = value
            return
        for b in range(8):
            self.scratch[(b % 2) ^ core, b // 2, :, lanes] = value[b * self.rows : (b + 1) * self.rows, :]

    def done(self):
        if self.size == 8:
            self.refs[0][...] = self.scratch[0]
            self.refs[1][...] = self.scratch[1]


def parted_shapes(size, rows, width, wide):
    if size != 8:
        return [(width, wide)], []
    return [(4, rows, wide)] * 2, [pltpu.VMEM((2, 4, rows, wide), BF16)]


def weights_back(group_at, n1_ref, g_scr, w_refs, core, parted):
    acc = None
    for i, w_ref in enumerate(w_refs):
        g = g_scr[i]
        at = group_at + i * GROUP
        if not isinstance(at, int):
            at = pl.multiple_of(at, GROUP)
        parted.put(core, dot_tn(n1_ref[...], g).astype(BF16), pl.ds(at, GROUP))
        more = dot_nt(g, w_ref[...])
        acc = more if acc is None else acc + more
    return acc


def token_kernel(
    experts, size, own_rows, outs, parts_in, me_ref, slot_ref, res_ref, logit_ref, cot_ref, n2_ref, att_ref,
    proj_ref, small_ref, small_t_ref, table_ref, q_ref, k_ref, v_ref, lse_ref, n1_ref, wq_ref, wk_ref, wv_ref, *refs,
):
    blocks, refs = refs[:parts_in], refs[parts_in:]
    gres_ref, gatt_ref, acc_ref, diag_ref = refs[:4]
    parts = refs[4 : 4 + outs]
    g_scr, gatt_scr, back_ref = refs[4 + outs : 7 + outs]
    parted = Parted(size, own_rows, parts, refs[7 + outs] if size == 8 else None)
    step = pl.program_id(0)
    seq, width = res_ref.shape
    core = me_ref[0] % 2
    groups = width // GROUP
    extra = (groups - 1) * 3 * GROUP

    @pl.when(step == 0)
    def _():
        per = blocks[0].shape[0]
        for j, block in enumerate(blocks):
            to = pl.multiple_of((me_ref[0] ^ j) * per, per) if parts_in > 1 else 0
            back_ref[pl.ds(to, per), :] = block[...]
        h0, h1 = pair_hits(slot_ref, back_ref.shape[0])
        g0, g1, hot0, hot1 = pair_gates(slot_ref, logit_ref)
        back = back_ref[:, :width]
        sides = back_ref[:, width:]
        d0 = jnp.sum(dot(h0, sides), axis=1, keepdims=True)
        d1 = jnp.sum(dot(h1, sides), axis=1, keepdims=True)
        glog = jnp.where(hot0, d0 - g0 * (d0 + d1), 0.0) + jnp.where(hot1, d1 - g1 * (d0 + d1), 0.0)
        glog = glog.astype(BF16)
        x = res_ref[...]
        small = small_ref[...]
        router = jnp.where(iota((width, LANES), 1) < experts, small, jnp.zeros_like(small))
        grad = dot(h0 + h1, back) + dot_nt(glog, router)
        gx, ggain = norm_back(x, grad, small_t_ref[experts + 1 : experts + 2, :])
        gres = gx + cot_ref[...].astype(F32)
        gres_ref[...] = gres
        branch = gres.astype(BF16)
        gatt = dot_nt(branch, proj_ref[...]).astype(BF16)
        for g in range(groups):
            gatt_scr[g] = gatt[:, g * GROUP : (g + 1) * GROUP]
        gatt_ref[...] = gatt[:, (groups - 1) * GROUP :]
        parted.put(core, dot_tn(att_ref[...], branch).astype(BF16), slice(extra, extra + width))
        gain_rows = jnp.where(iota((LANES, width), 0) == experts + 1, ggain, 0.0)
        more = (dot_tn(n2_ref[...], glog) + gain_rows.T).astype(BF16)
        parted.put(core, more, slice(extra + width, extra + width + LANES))

    @pl.when(step > 0)
    def _():
        group = step - 1
        heads_back(group, table_ref, q_ref, k_ref, v_ref, gatt_scr.at[group], lse_ref, g_scr, diag_ref)
        more = weights_back(group * 3 * GROUP, n1_ref, g_scr, (wq_ref, wk_ref, wv_ref), core, parted)

        @pl.when(step == 1)
        def _():
            acc_ref[...] = more

        @pl.when(step > 1)
        def _():
            acc_ref[...] += more

    @pl.when(step == pl.num_programs(0) - 1)
    def _():
        parted.done()


def token_side(
    experts, size, own_rows, me, back, slot_col, res, logits, cot, n2, att, proj, small, small_t,
    table, q, k, v, lse, n1, qkv,
):
    seq, width = res.shape
    groups = width // GROUP
    per_group = GROUP // HEAD_DIM
    wide = (groups - 1) * 3 * GROUP + width + LANES
    shapes, scratch = parted_shapes(size, own_rows, width, wide)

    def at(s):
        return jnp.maximum(s - 1, 0)

    col = pl.BlockSpec((seq, GROUP), lambda s: (0, at(s)))

    def wcol(i):
        return pl.BlockSpec((width, GROUP), lambda s: (0, i * groups + at(s)))

    first = (slot_col, res, logits, cot, n2, att, proj, small, small_t)
    return call(
        functools.partial(token_kernel, experts, size, own_rows, len(shapes), len(back)),
        [
            sds((seq, width), F32), sds((seq, GROUP), BF16), sds((seq, width), F32),
            sds(((groups - 1) * 8 * per_group, seq), F32),
        ]
        + [sds(x, BF16) for x in shapes],
        grid=(groups,),
        in_specs=[smem()] + [once(a.shape) for a in first]
        + [pl.BlockSpec((per_group, seq, seq), lambda s: (at(s), 0, 0)), col, col, col]
        + [once((seq, LANES)), once((seq, width)), wcol(0), wcol(1), wcol(2)]
        + [once(b.shape) for b in back],
        out_specs=[
            whole((seq, width)), whole((seq, GROUP)), whole((seq, width)),
            pl.BlockSpec((8 * per_group, seq), lambda s: (at(s), 0)),
        ]
        + [whole(x) for x in shapes],
        scratch_shapes=[
            pltpu.VMEM((3, seq, GROUP), BF16), pltpu.VMEM((groups, seq, GROUP), BF16),
            pltpu.VMEM((len(back) * back[0].shape[0], width + LANES), BF16),
        ]
        + scratch,
        flops=3072 * seq * width + 12 * seq * width * width + 14 * seq * seq * width,
        moved=30_000_000,
        name="token_side",
    )(me, *first, table, q, k, v, lse, n1, qkv, qkv, qkv, *back)


def tail_kernel(
    experts, size, own_rows, group, outs, me_ref, table_ref, q_ref, k_ref, v_ref, gatt_ref, lse_ref, n1_ref,
    wq_ref, wk_ref, wv_ref, acc_ref, diag_in, tokens_ref, gres_ref, small_t_ref, rev_ref, gtok_ref, *refs,
):
    parts = refs[:outs]
    g_scr, diag_scr = refs[outs : outs + 2]
    parted = Parted(size, own_rows, parts, refs[outs + 2] if size == 8 else None)
    seq, width = tokens_ref.shape
    core = me_ref[0] % 2
    heads_back(group, table_ref, q_ref, k_ref, v_ref, gatt_ref, lse_ref, g_scr, diag_scr)
    acc = acc_ref[...] + weights_back(0, n1_ref, g_scr, (wq_ref, wk_ref, wv_ref), core, parted)
    x = tokens_ref[...].astype(F32)
    gx, ggain = norm_back(x, acc, small_t_ref[experts : experts + 1, :])
    gtok_ref[...] = (gx + gres_ref[...]).astype(BF16)
    gain_rows = jnp.where(iota((LANES, width), 0) == experts, ggain, 0.0)
    diag = jnp.concatenate([diag_in[...], diag_scr[...]], axis=0)
    count = diag.shape[0]
    place = lax.rem(iota((count, seq), 0), 8)
    total = jnp.where(place == 0, diag, 0.0)
    for r in range(1, 8):
        total = total + jnp.where(place == r, pltpu.roll(diag, seq - r, 1), 0.0)
    hot = (iota((LANES, seq), 0) - (experts + 2) == rev_ref[...]).astype(F32)
    per_row = lax.dot_general(
        total, hot, (((1,), (1,)), ((), ())), precision=lax.Precision.HIGHEST, preferred_element_type=F32
    )
    copies = (lax.rem(iota((width, count), 0), own_rows) == lax.div(iota((width, count), 1), 8)).astype(F32)
    spread = jnp.dot(copies, per_row, precision=lax.Precision.HIGHEST, preferred_element_type=F32)
    parted.put(core, (gain_rows.T + spread).astype(BF16), slice(3 * GROUP, 3 * GROUP + LANES))
    parted.done()


def tail(experts, size, own_rows, me, table, q, k, v, gatt, lse, n1, qkv, acc, diag, tokens, gres, small_t, rev_buckets):
    seq, width = n1.shape
    groups = width // GROUP
    group = groups - 1
    per_group = GROUP // HEAD_DIM
    col = pl.BlockSpec((seq, GROUP), lambda _: (0, group))
    shapes, scratch = parted_shapes(size, own_rows, width, 3 * GROUP + LANES)

    def wcol(i):
        return pl.BlockSpec((width, GROUP), lambda _: (0, i * groups + group))

    rest = (acc, diag, tokens, gres, small_t, rev_buckets[None, :])
    return call(
        functools.partial(tail_kernel, experts, size, own_rows, group, len(shapes)),
        [sds((seq, width), BF16)] + [sds(x, BF16) for x in shapes],
        grid=(1,),
        in_specs=[
            smem(), pl.BlockSpec((per_group, seq, seq), lambda _: (group, 0, 0)),
            col, col, col, whole((seq, GROUP)),
            whole((seq, LANES)), whole((seq, width)),
            wcol(0), wcol(1), wcol(2),
        ]
        + [whole(x.shape) for x in rest],
        out_specs=[whole((seq, width))] + [whole(x) for x in shapes],
        scratch_shapes=[pltpu.VMEM((3, seq, GROUP), BF16), pltpu.VMEM((8 * per_group, seq), F32)] + scratch,
        flops=4 * seq * width * width + 7 * seq * seq * width,
        moved=10_000_000,
        name="tail",
    )(me, table, q, k, v, gatt, lse, n1, qkv, qkv, qkv, *rest)


def swap(value, mask, size):
    return lax.ppermute(value, "shard", [(i, i ^ mask) for i in range(size)])


def gather_blocks(value, size, beside):
    if size != 8:
        return [lax.all_gather(value, "shard", axis=0, tiled=True)], beside
    one, six, two, four = (swap(value, j, size) for j in (1, 6, 2, 4))
    one, six, two, four, *beside = lax.optimization_barrier((one, six, two, four, *beside))
    far = {0: value, 1: one, 6: six, 2: two, 4: four}
    near = {j ^ 1: swap(far[j], 1, size) for j in (6, 2, 4)}
    return [far[j] if j in far else near[j] for j in range(8)], beside


def tie(*values):
    return lax.optimization_barrier(values)


def inward(value):
    return lax.ppermute(value, "rep", [(0, 1), (3, 2)])


def across(value):
    return lax.ppermute(value, "rep", [(1, 2), (2, 1)])


def outward(value):
    return lax.ppermute(value, "rep", [(1, 0), (2, 3)])


def add(*values):
    total = values[0].astype(F32)
    for value in values[1:]:
        total = total + value.astype(F32)
    return total.astype(BF16)


def line_total(value, at_end):
    near = add(value, inward(value))
    total = add(near, across(near))
    return jnp.where(at_end, outward(total), total)


def finish_kernel(width, src_ref, *refs):
    in_ref, out_ref = refs[-2:]
    total = src_ref[0].astype(F32)
    part, block = in_ref.shape
    piece = out_ref.shape[0]
    in_ref[...] = total[:part, :]
    for j in range(width // block):
        out_ref[:, j * block : (j + 1) * block] = total[part + j * piece : part + (j + 1) * piece, :]


def finish(src, start, earlier, width, hidden, ranks):
    count, high, wide = src.shape
    block = wide // ranks
    part = width // ranks
    piece = block // ranks
    per_rank = hidden // ranks // block
    return call(
        functools.partial(finish_kernel, width),
        [sds((part, hidden), F32), sds((hidden // ranks, width), F32)],
        grid=(count, ranks),
        in_specs=[pl.BlockSpec((1, high, block), lambda c, r: (c, 0, r))]
        + [pl.BlockSpec(memory_space=pl.ANY)] * len(earlier),
        out_specs=[
            pl.BlockSpec((part, block), lambda c, r: (0, r * per_rank + start + c)),
            pl.BlockSpec((piece, width), lambda c, r: ((start + c) * ranks + r, 0)),
        ],
        input_output_aliases={1: 0, 2: 1} if earlier else {},
        name="finish",
    )(src, *earlier)


def pick_kernel(chip_ref, keep_ref, got_ref, six_ref, two_ref, four_ref, own_ref):
    chip = chip_ref[0]
    for ref, other in ((six_ref, 3), (two_ref, 1), (four_ref, 2), (own_ref, 0)):
        at = chip ^ other
        ref[...] = (keep_ref[at].astype(F32) + got_ref[at].astype(F32)).astype(BF16)


def core_sum(parts, me, size):
    if size != 8:
        return [parts[0]]
    keep, send = parts
    got = swap(send, 1, size)
    block = keep.shape[1:]
    return call(
        pick_kernel,
        [sds(block, BF16)] * 4,
        grid=(1,),
        in_specs=[smem(), whole(keep.shape), whole(keep.shape)],
        out_specs=[whole(block)] * 4,
        name="pick",
    )((me // 2).reshape(1), keep, got)


def chips_sum(blocks, size):
    if size != 8:
        return [lax.psum_scatter(blocks[0], "shard", scatter_dimension=0, tiled=True)]
    return [blocks[3]] + [swap(block, j, size) for block, j in zip(blocks, (6, 2, 4))]


def line_steps(value):
    near = add(value, inward(value))
    total = add(near, across(near))
    return total, outward(total)


def layout_kernel(
    width, experts, end_ref, a_in, a_out, b_in, b_out, qkv_ref, proj_ref, router_ref, gain_a, gain_b, bias_ref,
):
    at_end = end_ref[0] > 0
    a = jnp.where(at_end, a_out[...].astype(F32), a_in[...].astype(F32))
    b = jnp.where(at_end, b_out[...].astype(F32), b_in[...].astype(F32))
    groups = width // GROUP
    for g in range(groups):
        src, base = (a, g * 3 * GROUP) if g < groups - 1 else (b, 0)
        for i in range(3):
            qkv_ref[:, i * width + g * GROUP : i * width + (g + 1) * GROUP] = src[:, base + i * GROUP : base + (i + 1) * GROUP]
    extra = (groups - 1) * 3 * GROUP
    proj_ref[...] = a[:, extra : extra + width]
    small_a = a[:, extra + width :]
    small_b = b[:, 3 * GROUP :]
    rows = small_a.shape[0]
    pad = jnp.zeros((LANES - rows, LANES), F32)
    turned_a = jnp.concatenate([small_a, pad], axis=0).T
    turned_b = jnp.concatenate([small_b, pad], axis=0).T
    router_ref[...] = turned_a[:experts, :rows]
    gain_b[...] = turned_a[experts + 1, :rows]
    gain_a[...] = turned_b[experts, :rows]
    heads, buckets = bias_ref.shape
    bias_ref[...] = small_b[:heads, experts + 2 : experts + 2 + buckets]


def layout(end_flag, a, b, width, experts, bias_shape):
    rows = a[0].shape[0]
    ins = (*a, *b)
    shapes = [(rows, 3 * width), (rows, width), (experts, rows), (rows,), (rows,), bias_shape]
    return call(
        functools.partial(layout_kernel, width, experts),
        [sds(x, F32) for x in shapes],
        grid=(1,),
        in_specs=[smem()] + [whole(x.shape) for x in ins],
        out_specs=[whole(x) for x in shapes],
        name="layout",
    )(end_flag, *ins)


def body(
    tokens, cotangent, segments, buckets, routes, attn_gain, qkv_weight, proj_weight,
    rel_bias, moe_gain, router, expert_in, expert_out,
):
    seq, width = tokens.shape
    size = lax.axis_size("shard")
    ranks = lax.axis_size("rep")
    top = routes.shape[1]
    experts = expert_in.shape[0] * size
    hidden = expert_in.shape[2]
    capacity = 3 * seq * top // (2 * experts)
    slots = experts * capacity
    bucket_count = rel_bias.shape[0]
    me = lax.axis_index("shard").astype(jnp.int32)
    me_arr = me.reshape(1)
    own_rows = router.shape[0]

    packed = pack_weights(qkv_weight, proj_weight, router.T, attn_gain, moe_gain)
    rev_buckets = jnp.roll(buckets[::-1], 1)
    w_blocks, (table, slot_row, slot_col, cot_slots) = gather_blocks(
        packed, size, prep(routes.T, segments, rev_buckets, rel_bias, cotangent, experts, capacity)
    )
    (q, k, v, lse, att, res, n1, n2, logits, small_full, small_t, *sent) = front(
        me_arr, tokens, table, slot_row, w_blocks, experts, slots
    )
    me_late, logits = tie(me_arr, logits)
    qkv_full, proj_full = assemble(me_late, w_blocks, width)

    def exchange(value):
        wide = value.shape[1]
        moved = lax.all_to_all(
            value.reshape(size, slots // size, wide), "shard", split_axis=0, concat_axis=0, tiled=True
        )
        return moved.reshape(slots, wide)

    cot_rows = exchange(cot_slots)

    def exchange_blocks(blocks):
        if len(blocks) == 1:
            return [exchange(blocks[0])]
        return [blocks[0]] + [swap(block, j, size) for j, block in enumerate(blocks) if j]

    cot_rows, *sent = tie(cot_rows, *sent)
    rows = exchange_blocks(sent)
    win = expert_in[0]
    wout = expert_out[0]
    rank = lax.axis_index("rep").astype(jnp.int32)
    at_end = (rank == 0) | (rank == ranks - 1)
    per_rank = hidden // ranks // 256

    def scatter(buf):
        count, high, wide = buf.shape[1:]
        moved = lax.psum_scatter(buf.reshape(ranks * count * high, wide), "rep", scatter_dimension=0, tiled=True)
        return moved.reshape(count, high, wide)

    qkv_full, proj_full, *rows = tie(qkv_full, proj_full, *rows)
    act0, gp0, d0, buf0, sg = expert_first(me_arr, rows, cot_rows, small_full, win, wout, ranks)
    part0 = scatter(buf0)
    act1, gp1, *sends = expert_rest(rows, sg, win, wout, gp0, d0, ranks)
    back = exchange_blocks(sends)
    buf1 = expert_weight_grads(rows, sg, act1, gp1, hidden, ranks)
    act1, part0 = tie(act1, part0)
    part1 = scatter(buf1)
    result = expert_rows(me_arr, (act0, act1), wout, len(sends), ranks)
    done = finish(part0, 0, (), width, hidden, ranks)
    *back, result, one, two = tie(*back, result, *done)
    done = (one, two)
    returned = exchange(result)
    gres, gatt, acc, diag, *parts_a = token_side(
        experts, size, own_rows, me_arr, back, slot_col, res, logits, cotangent, n2, att, proj_full, small_full, small_t,
        table, q, k, v, lse, n1, qkv_full,
    )
    returned, *parts_a = tie(returned, *parts_a)
    blocks_a = core_sum(parts_a, me, size)
    gatt, *blocks_a = tie(gatt, *blocks_a)
    terms_a = chips_sum(blocks_a, size)
    grad_tokens, *parts_b = tail(
        experts, size, own_rows, me_arr, table, q, k, v, gatt, lse, n1, qkv_full, acc, diag, tokens, gres, small_t, rev_buckets
    )
    blocks_b = core_sum(parts_b, me, size)
    sum_a = add(*terms_a)
    terms_b = chips_sum(blocks_b, size)
    output = output_rows(returned, slot_col, res, logits)
    output, *terms_b = tie(output, *terms_b)
    sum_b = add(*terms_b)
    done = finish(part1, 1, done, width, hidden, ranks)
    line_a = line_steps(sum_a)
    line_b = line_steps(sum_b)
    total_a, *done = tie(line_a[0], *done)
    end_flag = at_end.astype(jnp.int32).reshape(1)
    grad_qkv, grad_proj, grad_router, gain_a, gain_b, grad_bias = layout(
        end_flag, (total_a, line_a[1]), line_b, width, experts, rel_bias.shape[::-1]
    )
    return (
        output,
        grad_tokens,
        grad_qkv,
        grad_proj,
        grad_router.T,
        gain_a,
        gain_b,
        grad_bias.T,
        done[0][None],
        done[1][None],
    )


def solution(mesh):
    both = P(("rep", "shard"), None)
    return jax.shard_map(
        body,
        mesh=mesh,
        in_specs=(
            both, both, P(("rep", "shard")), P(), both,
            P("shard"), P("shard", None), P("shard", None), P(), P("shard"), P("shard", None),
            P("shard", None, None), P("shard", None, None),
        ),
        out_specs=(
            both, both, P("shard", None), P("shard", None), P("shard", None), P("shard"), P("shard"), P(),
            P("shard", "rep", None), P("shard", "rep", None),
        ),
        check_vma=False,
    )
```

```python
import functools
import math

import jax
import jax.numpy as jnp
from jax import lax
from jax.experimental import pallas as pl
from jax.experimental.pallas import tpu as pltpu
from jax.sharding import PartitionSpec as P

F32 = jnp.float32
BF16 = jnp.bfloat16
EPS = 1e-06
NEG = -1e30
LANES = 128
HEAD_DIM = 64
GROUP = 256
BLOCK = 256
VMEM_LIMIT = 60 * 1024 * 1024


def dot(a, b):
    return jnp.dot(a, b, preferred_element_type=F32)


def dot_nt(a, b):
    return lax.dot_general(a, b, (((1,), (1,)), ((), ())), preferred_element_type=F32)


def dot_tn(a, b):
    return lax.dot_general(a, b, (((0,), (0,)), ((), ())), preferred_element_type=F32)


def call(kernel, out_shape, **kw):
    flops = kw.pop("flops", 0)
    moved = kw.pop("moved", 0)
    return pl.pallas_call(
        kernel,
        out_shape=out_shape,
        compiler_params=pltpu.CompilerParams(vmem_limit_bytes=VMEM_LIMIT),
        cost_estimate=pl.CostEstimate(flops=flops, bytes_accessed=moved, transcendentals=0),
        **kw,
    )


def whole(shape):
    rank = len(shape)
    return pl.BlockSpec(shape, lambda *_: (0,) * rank)


def smem():
    return pl.BlockSpec(memory_space=pltpu.SMEM)


def sds(shape, dtype):
    return jax.ShapeDtypeStruct(shape, dtype)


def iota(shape, dim):
    return lax.broadcasted_iota(jnp.int32, shape, dim)


def prep_kernel(
    experts, capacity, routes_ref, seg_row, seg_col, rev_ref, bias_ref, cot_ref,
    table_ref, slot_row_ref, slot_col_ref, cot_out_ref, mask_scr, series_scr, extra_scr,
):
    step = pl.program_id(0)
    seq = cot_ref.shape[0]
    width = cot_ref.shape[1]
    per = cot_out_ref.shape[0]

    @pl.when(step == 0)
    def _():
        keep = (iota((seq, seq), 0) >= iota((seq, seq), 1)) & (seg_col[...] == seg_row[...])
        mask_scr[...] = jnp.where(keep, 0.0, NEG)
        rev = rev_ref[...]
        bias = bias_ref[...]
        series = jnp.zeros((bias.shape[0], seq), F32)
        for bucket in range(bias.shape[1]):
            series = jnp.where(rev == bucket, bias[:, bucket : bucket + 1], series)
        series_scr[...] = series
        first, second = routes_ref[0:1, :], routes_ref[1:2, :]
        ids = iota((experts, seq), 0)
        m0 = (ids == first).astype(F32)
        m1 = (ids == second).astype(F32)
        before = (iota((seq, seq), 0) < iota((seq, seq), 1)).astype(BF16)
        count = dot((m0 + m1).astype(BF16), before)
        rank0 = jnp.sum(count * m0, axis=0, keepdims=True)
        rank1 = jnp.sum(count * m1, axis=0, keepdims=True)
        r0, r1 = first.astype(F32), second.astype(F32)
        slot0 = jnp.where(rank0 < capacity, r0 * capacity + rank0, -1.0)
        slot1 = jnp.where(rank1 < capacity, r1 * capacity + rank1, -1.0)
        place = iota((LANES, seq), 0)
        rows = jnp.where(place == 0, slot0, -1.0)
        rows = jnp.where(place == 1, slot1, rows)
        rows = jnp.where(place == 2, r0, rows)
        rows = jnp.where(place == 3, r1, rows)
        slot_row_ref[...] = rows[0:8, :].astype(jnp.int32)
        cols = rows.T
        slot_col_ref[...] = cols
        lane = iota((seq, LANES), 1)
        extra_scr[0] = jnp.where(lane == 0, cols[:, 3:4], 0.0).astype(BF16)
        extra_scr[1] = jnp.where(lane == 0, cols[:, 2:3], 0.0).astype(BF16)

    row = series_scr[pl.ds(step, 1), :]
    table_ref[0] = pltpu.roll(jnp.broadcast_to(row, (seq, seq)), 0, 1, stride=1, stride_axis=0) + mask_scr[...]

    @pl.when(step < 8)
    def _():
        slots = iota((per, seq), 0) + step * per
        hit0 = (slots == slot_row_ref[0:1, :]).astype(F32)
        hit1 = (slots == slot_row_ref[1:2, :]).astype(F32)
        cot_out_ref[:, :width] = dot((hit0 + hit1).astype(BF16), cot_ref[...]).astype(BF16)
        cot_out_ref[:, width:] = (
            dot(hit0.astype(BF16), extra_scr[0]) + dot(hit1.astype(BF16), extra_scr[1])
        ).astype(BF16)


def prep(routes_t, segments, rev_buckets, rel_bias, cotangent, experts, capacity):
    seq, width = cotangent.shape
    heads = rel_bias.shape[1]
    buckets = rel_bias.shape[0]
    slots = experts * capacity
    per = slots // 8
    hp = -(-heads // 8) * 8
    bias_t = jnp.zeros((hp, buckets), F32).at[:heads].set(rel_bias.T)
    return call(
        functools.partial(prep_kernel, experts, capacity),
        [
            sds((heads, seq, seq), F32),
            sds((8, seq), jnp.int32),
            sds((seq, LANES), F32),
            sds((slots, width + LANES), BF16),
        ],
        grid=(heads,),
        in_specs=[
            whole((2, seq)), whole((1, seq)), whole((seq, 1)), whole((1, seq)),
            whole((hp, buckets)), whole((seq, width)),
        ],
        out_specs=[
            pl.BlockSpec((1, seq, seq), lambda h: (h, 0, 0)),
            whole((8, seq)),
            whole((seq, LANES)),
            pl.BlockSpec((per, width + LANES), lambda h: (jnp.minimum(h, 7), 0)),
        ],
        scratch_shapes=[
            pltpu.VMEM((seq, seq), F32),
            pltpu.VMEM((hp, seq), F32),
            pltpu.VMEM((2, seq, LANES), BF16),
        ],
        flops=2 * slots * seq * width,
        moved=heads * seq * seq * 4 + 4 * seq * width,
        name="prep",
    )(routes_t, segments[None, :], segments[:, None], rev_buckets[None, :], bias_t, cotangent)


def pack_kernel(qkv_ref, proj_ref, router_ref, gain_a, gain_b, out_ref):
    rows, width = proj_ref.shape
    experts = router_ref.shape[0]
    out_ref[:, : 3 * width] = qkv_ref[...]
    out_ref[:, 3 * width : 4 * width] = proj_ref[...]
    place = iota((LANES, rows), 0)
    a = gain_a[...].astype(F32).reshape(1, rows)
    b = gain_b[...].astype(F32).reshape(1, rows)
    gains = jnp.where(place == experts, a, jnp.where(place == experts + 1, b, 0.0))
    if rows < LANES:
        gains = jnp.concatenate([gains, jnp.zeros((LANES, LANES - rows), F32)], axis=1)
    spread = (iota((experts, LANES), 0) == iota((experts, LANES), 1)).astype(BF16)
    out_ref[:, 4 * width :] = (dot_tn(router_ref[...], spread) + gains.T[:rows, :]).astype(BF16)


def pack_weights(qkv, proj, router, gain_a, gain_b):
    rows, width = proj.shape
    ins = (qkv, proj, router, gain_a, gain_b)
    return call(
        pack_kernel,
        sds((rows, 4 * width + LANES), BF16),
        grid=(1,),
        in_specs=[whole(x.shape) for x in ins],
        out_specs=whole((rows, 4 * width + LANES)),
        name="pack_weights",
    )(*ins)


def front_kernel(
    blocks, experts, me_ref, tokens_ref, table_ref, slot_row_ref, *refs,
):
    w_in = refs[:blocks]
    (q_ref, k_ref, v_ref, lse_ref, att_ref, res_ref, n1_ref, n2_ref, logit_ref,
     small_ref, small_t_ref) = refs[blocks : blocks + 11]
    qkv_ref, proj_ref = refs[-2:]
    sent_refs = refs[blocks + 11 : -2]
    step = pl.program_id(0)
    last = pl.num_programs(0) - 1
    seq, width = tokens_ref.shape
    rows = w_in[0].shape[0]
    scale = HEAD_DIM ** (-0.5)

    @pl.when(step == 0)
    def _():
        me = me_ref[0]
        for j in range(blocks):
            start = pl.multiple_of((me ^ j) * rows, rows) if blocks > 1 else 0
            qkv_ref[pl.ds(start, rows), :] = w_in[j][:, : 3 * width]
            proj_ref[pl.ds(start, rows), :] = w_in[j][:, 3 * width : 4 * width]
            small_ref[pl.ds(start, rows), :] = w_in[j][:, 4 * width :]
        small_t_ref[...] = small_ref[...].astype(F32).T
        x = tokens_ref[...].astype(F32)
        r = lax.rsqrt(jnp.mean(x * x, axis=-1, keepdims=True) + EPS)
        n1_ref[...] = (x * r * small_t_ref[experts : experts + 1, :]).astype(BF16)
        lse_ref[...] = jnp.zeros_like(lse_ref)

    base = pl.multiple_of(step * GROUP, GROUP)
    n1 = n1_ref[...]
    q_ref[...] = dot(n1, qkv_ref[:, pl.ds(base, GROUP)]).astype(BF16)
    k_ref[...] = dot(n1, qkv_ref[:, pl.ds(width + base, GROUP)]).astype(BF16)
    v_ref[...] = dot(n1, qkv_ref[:, pl.ds(2 * width + base, GROUP)]).astype(BF16)

    half = seq // 2
    lane = iota((half, LANES), 1)
    for pair in range(GROUP // LANES):
        cols = slice(pair * LANES, (pair + 1) * LANES)
        for rb in range(2):
            span = (rb + 1) * half
            qrows = slice(rb * half, (rb + 1) * half)
            qp = q_ref[qrows, cols]
            kp = k_ref[:span, cols]
            vp = v_ref[:span, cols]
            mixed = []
            for parity in range(2):
                mine = (lane // HEAD_DIM) == parity
                qm = jnp.where(mine, qp, jnp.zeros_like(qp))
                s = dot_nt(qm, kp) * scale + table_ref[2 * pair + parity, qrows, :span]
                top = jnp.max(s, axis=-1, keepdims=True)
                e = jnp.exp(s - top)
                total = jnp.sum(e, axis=-1, keepdims=True)
                p = (e * (1.0 / total)).astype(BF16)
                mixed.append(dot(p, vp))
                head = step * (GROUP // HEAD_DIM) + 2 * pair + parity
                lse_ref[qrows, :] = jnp.where(lane == head, top + jnp.log(total), lse_ref[qrows, :])
            at = pl.multiple_of(base + pair * LANES, LANES)
            att_ref[qrows, pl.ds(at, LANES)] = jnp.where(lane < HEAD_DIM, mixed[0], mixed[1]).astype(BF16)

    @pl.when(step == last)
    def _():
        x = tokens_ref[...].astype(F32) + dot(att_ref[...], proj_ref[...])
        res_ref[...] = x
        r = lax.rsqrt(jnp.mean(x * x, axis=-1, keepdims=True) + EPS)
        n2 = (x * r * small_t_ref[experts + 1 : experts + 2, :]).astype(BF16)
        n2_ref[...] = n2
        logit_ref[...] = dot(n2, small_ref[...])
        many = len(sent_refs) > 1
        per = sent_refs[0].shape[0] if many else sent_refs[0].shape[0] // 8
        for j in range(8):
            slots = iota((per, seq), 0) + ((me_ref[0] ^ j) * per if many else j * per)
            hit = (slots == slot_row_ref[0:1, :]) | (slots == slot_row_ref[1:2, :])
            rows_j = dot(hit.astype(BF16), n2).astype(BF16)
            if many:
                sent_refs[j][...] = rows_j
            else:
                sent_refs[0][j * per : (j + 1) * per, :] = rows_j


def front(me, tokens, table, slot_row, w_blocks, experts, slots):
    seq, width = tokens.shape
    blocks = len(w_blocks)
    groups = width // GROUP
    per_group = GROUP // HEAD_DIM
    col = pl.BlockSpec((seq, GROUP), lambda g: (0, g))
    return call(
        functools.partial(front_kernel, blocks, experts),
        [
            sds((seq, width), BF16), sds((seq, width), BF16), sds((seq, width), BF16),
            sds((seq, LANES), F32), sds((seq, width), BF16), sds((seq, width), F32),
            sds((seq, width), BF16), sds((seq, width), BF16), sds((seq, LANES), F32),
            sds((width, LANES), BF16), sds((LANES, width), F32),
        ]
        + [sds((slots // blocks, width), BF16)] * blocks,
        grid=(groups,),
        in_specs=[
            smem(), whole((seq, width)),
            pl.BlockSpec((per_group, seq, seq), lambda g: (g, 0, 0)),
            whole((8, seq)),
        ]
        + [whole(b.shape) for b in w_blocks],
        out_specs=[
            col, col, col,
            whole((seq, LANES)), whole((seq, width)), whole((seq, width)),
            whole((seq, width)), whole((seq, width)), whole((seq, LANES)),
            whole((width, LANES)), whole((LANES, width)),
        ]
        + [whole((slots // blocks, width))] * blocks,
        scratch_shapes=[pltpu.VMEM((width, 3 * width), BF16), pltpu.VMEM((width, width), BF16)],
        flops=2 * seq * width * width * 4 + 2 * slots * seq * width + 8 * seq * seq * width,
        moved=30_000_000,
        name="front",
    )(me, tokens, table, slot_row, *w_blocks)


def assemble_kernel(blocks, me_ref, *refs):
    qkv_ref, proj_ref = refs[-2:]
    wide = qkv_ref.shape[1]
    high = proj_ref.shape[1]
    for j in range(blocks):
        rows = refs[j].shape[0]
        start = pl.multiple_of((me_ref[0] ^ j) * rows, rows) if blocks > 1 else 0
        qkv_ref[pl.ds(start, rows), :] = refs[j][:, :wide]
        proj_ref[pl.ds(start, rows), :] = refs[j][:, wide : wide + high]


def assemble(me, w_blocks, width):
    return call(
        functools.partial(assemble_kernel, len(w_blocks)),
        [sds((width, 3 * width), BF16), sds((width, width), BF16)],
        grid=(1,),
        in_specs=[smem()] + [whole(b.shape) for b in w_blocks],
        out_specs=[whole((width, 3 * width)), whole((width, width))],
        name="assemble",
    )(me, *w_blocks)


def gelu_parts(v):
    size = jnp.abs(v) * (2.0 ** -0.5)
    t = 1.0 / (1.0 + 0.3275911 * size)
    bell = jnp.exp(-0.5 * v * v)
    poly = t * (
        0.5 * 0.254829592
        + t * (0.5 * -0.284496736 + t * (0.5 * 1.421413741 + t * (0.5 * -1.453152027 + t * (0.5 * 1.061405429))))
    )
    tail = poly * bell
    below = jnp.where(v < 0, tail, 1.0 - tail)
    return v * below, below + v * bell * (1.0 / math.sqrt(2.0 * math.pi))


def join_rows(blocks, rows_ref):
    per = blocks[0].shape[0]
    for j, block in enumerate(blocks):
        rows_ref[j * per : (j + 1) * per, :] = block[...]


def gated_rows(me, parts, rows_ref, cotx_ref, small_ref, sg_ref):
    total, width = rows_ref.shape
    tile = total // 8
    for j in range(8):
        here = slice(j * tile, (j + 1) * tile)
        there = pl.ds(pl.multiple_of((me ^ j) * tile, tile), tile) if parts > 1 else here
        logits = dot(rows_ref[here, :], small_ref[...])
        lane = iota((tile, LANES), 1)
        other_id = cotx_ref[there, width:].astype(F32)[:, 0:1].astype(jnp.int32)
        own = jnp.sum(jnp.where(lane == me, logits, 0.0), axis=1, keepdims=True)
        other = jnp.sum(jnp.where(lane == other_id, logits, 0.0), axis=1, keepdims=True)
        top = jnp.maximum(own, other)
        a, b = jnp.exp(own - top), jnp.exp(other - top)
        gate = a / (a + b)
        sg_ref[here, :] = (gate * cotx_ref[there, :width].astype(F32)).astype(BF16)


def expert_acts(w1, w2, rows_ref, sg_ref, act_ref, gp_ref, d_ref, tile):
    for at in range(0, rows_ref.shape[0], tile):
        here = slice(at, at + tile)
        pre = dot(rows_ref[here, :], w1)
        ga = dot_nt(sg_ref[here, :], w2)
        act, slope = gelu_parts(pre)
        low = act.astype(BF16)
        act_ref[here, :] = low
        gp_ref[here, :] = (ga * slope).astype(BF16)
        d_ref[here, :] += jnp.sum(low.astype(F32) * ga, axis=1, keepdims=True)


def expert_weights(rows_t, sg_t, act_ref, gp_ref, buf_ref, cb, pair, ranks):
    width = rows_t.shape[0]
    block = BLOCK
    part = width // ranks
    piece = block // ranks
    gwin = dot(rows_t[...], gp_ref[...]).astype(BF16)
    lane0 = pl.multiple_of(pair * 2 * block, block)
    for dest in range(ranks):
        buf_ref[dest, cb, 0:part, pl.ds(lane0, 2 * block)] = gwin[dest * part : (dest + 1) * part, :]
    gwout = dot(sg_t[...], act_ref[...]).T.astype(BF16)
    for half in range(2):
        rank = 2 * pair + half
        for i in range(ranks):
            for j in range(width // block):
                buf_ref[rank, cb, part + j * piece : part + (j + 1) * piece, i * block : (i + 1) * block] = gwout[
                    half * block + i * piece : half * block + (i + 1) * piece, j * block : (j + 1) * block
                ]


def expert_first_kernel(
    ranks, tile, parts, me_ref, cotx_ref, small_ref, w1a, w1b, w2a, w2b, *refs,
):
    blocks = refs[:parts]
    act_ref, gp_ref, d_ref, buf_ref, sg_ref, rows_t, sg_t, rows_ref = refs[parts:]
    step = pl.program_id(0)

    @pl.when(step == 0)
    def _():
        join_rows(blocks, rows_ref)
        gated_rows(me_ref[0], parts, rows_ref, cotx_ref, small_ref, sg_ref)
        rows_t[...] = rows_ref[...].T
        sg_t[...] = sg_ref[...].T
        d_ref[...] = jnp.zeros_like(d_ref)

    w1 = jnp.concatenate([w1a[...], w1b[...]], axis=1)
    w2 = jnp.concatenate([w2a[...], w2b[...]], axis=0)
    expert_acts(w1, w2, rows_ref, sg_ref, act_ref, gp_ref, d_ref, tile)
    expert_weights(rows_t, sg_t, act_ref, gp_ref, buf_ref, 0, step, ranks)


def expert_rest_kernel(
    ranks, per_rank, start, tile, parts, sg_ref, win_ref, w2a, w2b, gp0_ref, d0_ref, *refs,
):
    blocks = refs[:parts]
    act_ref, gp_ref = refs[parts : parts + 2]
    back_refs = refs[parts + 2 : -3]
    gp_scr, d_scr, rows_ref = refs[-3:]
    step = pl.program_id(0)
    total, width = rows_ref.shape
    block = BLOCK

    @pl.when(step == 0)
    def _():
        join_rows(blocks, rows_ref)
        d_scr[...] = d0_ref[...]
        for c in range(start):
            for r in range(ranks):
                to = (r * per_rank + c) * block
                gp_scr[:, to : to + block] = gp0_ref[:, (c * ranks + r) * block : (c * ranks + r + 1) * block]

    pairs = ranks // 2
    cb, pair = lax.div(step, pairs), lax.rem(step, pairs)
    at_a = pl.multiple_of((2 * pair * per_rank + start + cb) * block, block)
    at_b = pl.multiple_of(((2 * pair + 1) * per_rank + start + cb) * block, block)
    w1 = jnp.concatenate([win_ref[:, pl.ds(at_a, block)], win_ref[:, pl.ds(at_b, block)]], axis=1)
    w2 = jnp.concatenate([w2a[...], w2b[...]], axis=0)
    expert_acts(w1, w2, rows_ref, sg_ref, act_ref, gp_ref, d_scr, tile)
    gp_scr[:, pl.ds(at_a, block)] = gp_ref[:, :block]
    gp_scr[:, pl.ds(at_b, block)] = gp_ref[:, block:]

    @pl.when(step == pl.num_programs(0) - 1)
    def _():
        per = total // 8
        join = 2
        for at in range(0, 8, join):
            here = slice(at * per, (at + join) * per)
            back = dot_nt(gp_scr[here, :], win_ref[...]).astype(BF16)
            d = d_scr[here, :]
            high = d.astype(BF16).astype(F32)
            lane = iota(d.shape, 1)
            side = jnp.where(lane == 0, high, jnp.where(lane == 1, d - high, 0.0)).astype(BF16)
            for i in range(join):
                inner = slice(i * per, (i + 1) * per)
                if parts > 1:
                    ref, to = back_refs[at + i], slice(0, per)
                else:
                    ref, to = back_refs[0], slice((at + i) * per, (at + i + 1) * per)
                ref[to, :width] = back[inner, :]
                ref[to, width:] = side[inner, :]


def expert_weights_kernel(ranks, parts, sg_ref, act_ref, gp_ref, *refs):
    blocks = refs[:parts]
    buf_ref, rows_t, sg_t = refs[parts:]
    step = pl.program_id(0)
    pairs = ranks // 2
    per = blocks[0].shape[0]

    @pl.when(step == 0)
    def _():
        if per % LANES and parts > 1:
            for j in range(0, parts, 2):
                pair = jnp.concatenate([blocks[j][...], blocks[j + 1][...]], axis=0)
                rows_t[:, j * per : (j + 2) * per] = pair.T
        else:
            for j, block in enumerate(blocks):
                rows_t[:, j * per : (j + 1) * per] = block[...].T
        sg_t[...] = sg_ref[...].T

    expert_weights(rows_t, sg_t, act_ref, gp_ref, buf_ref, lax.div(step, pairs), lax.rem(step, pairs), ranks)


def expert_weight_grads(blocks, sg, act, gp, hidden, ranks):
    total, width = sg.shape
    high, wide, per_rank = expert_sizes(width, hidden, ranks)
    count = act.shape[1] // wide
    buf = (ranks, count, high, wide)
    col = pl.BlockSpec((total, 2 * BLOCK), lambda s: (0, s))
    return call(
        functools.partial(expert_weights_kernel, ranks, len(blocks)),
        sds(buf, BF16),
        grid=(count * ranks // 2,),
        in_specs=[once((total, width)), col, col] + [once(b.shape) for b in blocks],
        out_specs=whole(buf),
        scratch_shapes=[pltpu.VMEM((width, total), BF16), pltpu.VMEM((width, total), BF16)],
        flops=4 * total * width * wide * count,
        moved=20_000_000,
        name="experts_weights",
    )(sg, act, gp, *blocks)


def once(shape):
    rank = len(shape)
    return pl.BlockSpec(shape, lambda *_: (0,) * rank, pipeline_mode=pl.Buffered(1))


def expert_sizes(width, hidden, ranks):
    high = width // ranks + (width // BLOCK) * (BLOCK // ranks)
    return high, ranks * BLOCK, hidden // ranks // BLOCK


def expert_first(me, blocks, cotx, small, win, wout, ranks):
    total = cotx.shape[0]
    width, hidden = win.shape
    high, wide, per_rank = expert_sizes(width, hidden, ranks)
    buf = (ranks, 1, high, wide)
    col = pl.BlockSpec((total, 2 * BLOCK), lambda s: (0, s))

    def win_spec(half):
        return pl.BlockSpec((width, BLOCK), lambda s: (0, (2 * s + half) * per_rank))

    def wout_spec(half):
        return pl.BlockSpec((BLOCK, width), lambda s: ((2 * s + half) * per_rank, 0))

    return call(
        functools.partial(expert_first_kernel, ranks, 256, len(blocks)),
        [
            sds((total, wide), BF16), sds((total, wide), BF16), sds((total, LANES), F32), sds(buf, BF16),
            sds((total, width), BF16),
        ],
        grid=(ranks // 2,),
        in_specs=[
            smem(), once((total, width + LANES)), once((width, LANES)),
            win_spec(0), win_spec(1), wout_spec(0), wout_spec(1),
        ]
        + [once(b.shape) for b in blocks],
        out_specs=[
            col, col, whole((total, LANES)), whole(buf), whole((total, width)),
        ],
        scratch_shapes=[
            pltpu.VMEM((width, total), BF16), pltpu.VMEM((width, total), BF16), pltpu.VMEM((total, width), BF16),
        ],
        flops=8 * total * width * wide,
        moved=20_000_000,
        name="experts_first",
    )(me, cotx, small, win, win, wout, wout, *blocks)


def expert_rest(blocks, sg, win, wout, gp0, d0, ranks):
    total, width = sg.shape
    hidden = win.shape[1]
    high, wide, per_rank = expert_sizes(width, hidden, ranks)
    start = 1
    count = per_rank - start
    pairs = ranks // 2
    parts = len(blocks)
    col = pl.BlockSpec((total, 2 * BLOCK), lambda s: (0, s))
    out = (total // parts, width + LANES)

    def wout_spec(half):
        return pl.BlockSpec(
            (BLOCK, width), lambda s: ((2 * lax.rem(s, pairs) + half) * per_rank + start + lax.div(s, pairs), 0)
        )

    return call(
        functools.partial(expert_rest_kernel, ranks, per_rank, start, 256, parts),
        [sds((total, count * wide), BF16), sds((total, count * wide), BF16)] + [sds(out, BF16)] * parts,
        grid=(count * pairs,),
        in_specs=[
            once((total, width)), once((width, hidden)), wout_spec(0), wout_spec(1),
            once((total, start * wide)), once((total, LANES)),
        ]
        + [once(b.shape) for b in blocks],
        out_specs=[col, col] + [whole(out)] * parts,
        scratch_shapes=[
            pltpu.VMEM((total, hidden), BF16), pltpu.VMEM((total, LANES), F32), pltpu.VMEM((total, width), BF16),
        ],
        flops=4 * total * width * wide * count + 2 * total * width * hidden,
        moved=30_000_000,
        name="experts_rest",
    )(sg, win, wout, wout, gp0, d0, *blocks)


def expert_rows_kernel(ranks, per_rank, parts, count, me_ref, *refs):
    acts, w_ref, o_ref, w_scr = refs[:count], refs[count], refs[count + 1], refs[count + 2]

    @pl.when(pl.program_id(0) == 0)
    def _():
        for c in range(per_rank):
            for r in range(ranks):
                to, src = (c * ranks + r) * BLOCK, (r * per_rank + c) * BLOCK
                w_scr[to : to + BLOCK, :] = w_ref[src : src + BLOCK, :]

    at, total = 0, None
    for act in acts:
        wide = act.shape[1]
        more = dot(act[...], w_scr[at : at + wide, :])
        total = more if total is None else total + more
        at += wide
    low = total.astype(BF16)
    if parts == 1:
        o_ref[...] = low
    else:
        per = low.shape[0] // 2
        flip = me_ref[0] % 2
        o_ref[pl.ds(pl.multiple_of(flip * per, per), per), :] = low[:per, :]
        o_ref[pl.ds(pl.multiple_of((1 - flip) * per, per), per), :] = low[per:, :]


def expert_rows(me, acts, wout, parts, ranks):
    total = acts[0].shape[0]
    hidden, width = wout.shape
    tile = total // 4

    def place(i, m):
        return ((m[0] // 2) ^ i if parts > 1 else i, 0)

    return pl.pallas_call(
        functools.partial(expert_rows_kernel, ranks, hidden // ranks // BLOCK, parts, len(acts)),
        sds((total, width), BF16),
        grid_spec=pltpu.PrefetchScalarGridSpec(
            num_scalar_prefetch=1,
            grid=(4,),
            in_specs=[pl.BlockSpec((tile, a.shape[1]), lambda i, m: (i, 0)) for a in acts] + [once(wout.shape)],
            out_specs=pl.BlockSpec((tile, width), place),
            scratch_shapes=[pltpu.VMEM(wout.shape, BF16)],
        ),
        compiler_params=pltpu.CompilerParams(vmem_limit_bytes=VMEM_LIMIT),
        name="expert_rows",
    )(me, *acts, wout)


def norm_back(x, grad, gain):
    r = lax.rsqrt(jnp.mean(x * x, axis=-1, keepdims=True) + EPS)
    u = grad * gain
    inner = jnp.mean(u * x, axis=-1, keepdims=True)
    xr = x * r
    return r * u - (r * r * r) * x * inner, jnp.sum(grad * xr, axis=0, keepdims=True)


def pair_gates(slot_ref, logit_ref):
    logits = logit_ref[...]
    lane = iota(logits.shape, 1)
    hot0 = lane == slot_ref[:, 2:3].astype(jnp.int32)
    hot1 = lane == slot_ref[:, 3:4].astype(jnp.int32)
    c0 = jnp.sum(jnp.where(hot0, logits, 0.0), axis=1, keepdims=True)
    c1 = jnp.sum(jnp.where(hot1, logits, 0.0), axis=1, keepdims=True)
    top = jnp.maximum(c0, c1)
    e0, e1 = jnp.exp(c0 - top), jnp.exp(c1 - top)
    return e0 / (e0 + e1), e1 / (e0 + e1), hot0, hot1


def pair_hits(slot_ref, slots):
    spot = iota((slot_ref.shape[0], slots), 1)
    h0 = (spot == slot_ref[:, 0:1].astype(jnp.int32)).astype(BF16)
    h1 = (spot == slot_ref[:, 1:2].astype(jnp.int32)).astype(BF16)
    return h0, h1


def output_kernel(ret_ref, slot_ref, res_ref, logit_ref, out_ref):
    h0, h1 = pair_hits(slot_ref, ret_ref.shape[0])
    g0, g1, _, _ = pair_gates(slot_ref, logit_ref)
    ret = ret_ref[...]
    out_ref[...] = (res_ref[...] + (g0 * dot(h0, ret) + g1 * dot(h1, ret))).astype(BF16)


def output_rows(returned, slot_col, res, logits):
    ins = (returned, slot_col, res, logits)
    return call(
        output_kernel,
        sds(res.shape, BF16),
        grid=(1,),
        in_specs=[whole(x.shape) for x in ins],
        out_specs=whole(res.shape),
        flops=4 * returned.shape[0] * res.size,
        moved=6_000_000,
        name="output_rows",
    )(*ins)


def heads_back(group, table_ref, q_ref, k_ref, v_ref, gatt_ref, lse_ref, g_scr, diag_ref):
    seq = q_ref.shape[0]
    half = seq // 2
    scale = HEAD_DIM ** (-0.5)
    lane = iota((half, LANES), 1)
    full_lane = iota((seq, LANES), 1)
    for pair in range(GROUP // LANES):
        cols = slice(pair * LANES, (pair + 1) * LANES)
        dk = [jnp.zeros((seq, LANES), F32)] * 2
        dv = [jnp.zeros((seq, LANES), F32)] * 2
        skew = [jnp.zeros((LANES, seq), F32)] * 2
        for rb in range(2):
            span = (rb + 1) * half
            qrows = slice(rb * half, (rb + 1) * half)
            qp = q_ref[qrows, cols]
            gp = gatt_ref[qrows, cols]
            kp = k_ref[:span, cols]
            vp = v_ref[:span, cols]
            dq = []
            for parity in range(2):
                mine = (lane // HEAD_DIM) == parity
                head = group * (GROUP // HEAD_DIM) + 2 * pair + parity
                level = jnp.sum(jnp.where(lane == head, lse_ref[qrows, :], 0.0), axis=1, keepdims=True)
                qm = jnp.where(mine, qp, jnp.zeros_like(qp))
                gm = jnp.where(mine, gp, jnp.zeros_like(gp))
                s = dot_nt(qm, kp) * scale + table_ref[2 * pair + parity, qrows, :span]
                p = jnp.exp(s - level)
                dp = dot_nt(gm, vp)
                d = jnp.sum(p * dp, axis=1, keepdims=True)
                ds = p * (dp - d)
                low = ds.astype(BF16)
                dq.append(dot(low, kp) * scale)
                add_k = dot_tn(low, qp) * scale
                add_v = dot_tn(p.astype(BF16), gp)
                if span < seq:
                    zero = jnp.zeros((seq - span, LANES), F32)
                    add_k = jnp.concatenate([add_k, zero], axis=0)
                    add_v = jnp.concatenate([add_v, zero], axis=0)
                dk[parity] = dk[parity] + add_k
                dv[parity] = dv[parity] + add_v
                wide = low.astype(F32)
                if span < seq:
                    wide = jnp.concatenate([wide, jnp.zeros((half, seq - span), F32)], axis=1)
                for b in range(half // LANES):
                    shift = rb * half + b * LANES
                    rows = wide[b * LANES : (b + 1) * LANES, :]
                    if shift:
                        rows = jnp.concatenate([rows[:, shift:], rows[:, :shift]], axis=1)
                    skew[parity] = skew[parity] + rows
            g_scr[0, qrows, cols] = jnp.where(lane < HEAD_DIM, dq[0], dq[1]).astype(BF16)
        g_scr[1, :, cols] = jnp.where(full_lane < HEAD_DIM, dk[0], dk[1]).astype(BF16)
        g_scr[2, :, cols] = jnp.where(full_lane < HEAD_DIM, dv[0], dv[1]).astype(BF16)
        for parity in range(2):
            acc = skew[parity][0:8, :]
            for i in range(1, LANES // 8):
                acc = acc + pltpu.roll(skew[parity][i * 8 : (i + 1) * 8, :], seq - i * 8, 1)
            at = 8 * (2 * pair + parity)
            diag_ref[at : at + 8, :] = acc


class Parted:
    def __init__(self, size, rows, refs, scratch):
        self.size, self.rows, self.refs, self.scratch = size, rows, refs, scratch

    def put(self, core, value, lanes):
        if self.size != 8:
            self.refs[0][:, lanes] = value
            return
        for b in range(8):
            self.scratch[(b % 2) ^ core, b // 2, :, lanes] = value[b * self.rows : (b + 1) * self.rows, :]

    def done(self):
        if self.size == 8:
            self.refs[0][...] = self.scratch[0]
            self.refs[1][...] = self.scratch[1]


def parted_shapes(size, rows, width, wide):
    if size != 8:
        return [(width, wide)], []
    return [(4, rows, wide)] * 2, [pltpu.VMEM((2, 4, rows, wide), BF16)]


def weights_back(group_at, n1_ref, g_scr, w_refs, core, parted):
    acc = None
    for i, w_ref in enumerate(w_refs):
        g = g_scr[i]
        at = group_at + i * GROUP
        if not isinstance(at, int):
            at = pl.multiple_of(at, GROUP)
        parted.put(core, dot_tn(n1_ref[...], g).astype(BF16), pl.ds(at, GROUP))
        more = dot_nt(g, w_ref[...])
        acc = more if acc is None else acc + more
    return acc


def token_kernel(
    experts, size, own_rows, outs, parts_in, me_ref, slot_ref, res_ref, logit_ref, cot_ref, n2_ref, att_ref,
    proj_ref, small_ref, small_t_ref, table_ref, q_ref, k_ref, v_ref, lse_ref, n1_ref, wq_ref, wk_ref, wv_ref, *refs,
):
    blocks, refs = refs[:parts_in], refs[parts_in:]
    gres_ref, gatt_ref, acc_ref, diag_ref = refs[:4]
    parts = refs[4 : 4 + outs]
    g_scr, gatt_scr, back_ref = refs[4 + outs : 7 + outs]
    parted = Parted(size, own_rows, parts, refs[7 + outs] if size == 8 else None)
    step = pl.program_id(0)
    seq, width = res_ref.shape
    core = me_ref[0] % 2
    groups = width // GROUP
    extra = (groups - 1) * 3 * GROUP

    @pl.when(step == 0)
    def _():
        per = blocks[0].shape[0]
        for j, block in enumerate(blocks):
            to = pl.multiple_of((me_ref[0] ^ j) * per, per) if parts_in > 1 else 0
            back_ref[pl.ds(to, per), :] = block[...]
        h0, h1 = pair_hits(slot_ref, back_ref.shape[0])
        g0, g1, hot0, hot1 = pair_gates(slot_ref, logit_ref)
        back = back_ref[:, :width]
        sides = back_ref[:, width:]
        d0 = jnp.sum(dot(h0, sides), axis=1, keepdims=True)
        d1 = jnp.sum(dot(h1, sides), axis=1, keepdims=True)
        glog = jnp.where(hot0, d0 - g0 * (d0 + d1), 0.0) + jnp.where(hot1, d1 - g1 * (d0 + d1), 0.0)
        glog = glog.astype(BF16)
        x = res_ref[...]
        small = small_ref[...]
        router = jnp.where(iota((width, LANES), 1) < experts, small, jnp.zeros_like(small))
        grad = dot(h0 + h1, back) + dot_nt(glog, router)
        gx, ggain = norm_back(x, grad, small_t_ref[experts + 1 : experts + 2, :])
        gres = gx + cot_ref[...].astype(F32)
        gres_ref[...] = gres
        branch = gres.astype(BF16)
        gatt = dot_nt(branch, proj_ref[...]).astype(BF16)
        for g in range(groups):
            gatt_scr[g] = gatt[:, g * GROUP : (g + 1) * GROUP]
        gatt_ref[...] = gatt[:, (groups - 1) * GROUP :]
        parted.put(core, dot_tn(att_ref[...], branch).astype(BF16), slice(extra, extra + width))
        gain_rows = jnp.where(iota((LANES, width), 0) == experts + 1, ggain, 0.0)
        more = (dot_tn(n2_ref[...], glog) + gain_rows.T).astype(BF16)
        parted.put(core, more, slice(extra + width, extra + width + LANES))

    @pl.when(step > 0)
    def _():
        group = step - 1
        heads_back(group, table_ref, q_ref, k_ref, v_ref, gatt_scr.at[group], lse_ref, g_scr, diag_ref)
        more = weights_back(group * 3 * GROUP, n1_ref, g_scr, (wq_ref, wk_ref, wv_ref), core, parted)

        @pl.when(step == 1)
        def _():
            acc_ref[...] = more

        @pl.when(step > 1)
        def _():
            acc_ref[...] += more

    @pl.when(step == pl.num_programs(0) - 1)
    def _():
        parted.done()


def token_side(
    experts, size, own_rows, me, back, slot_col, res, logits, cot, n2, att, proj, small, small_t,
    table, q, k, v, lse, n1, qkv,
):
    seq, width = res.shape
    groups = width // GROUP
    per_group = GROUP // HEAD_DIM
    wide = (groups - 1) * 3 * GROUP + width + LANES
    shapes, scratch = parted_shapes(size, own_rows, width, wide)

    def at(s):
        return jnp.maximum(s - 1, 0)

    col = pl.BlockSpec((seq, GROUP), lambda s: (0, at(s)))

    def wcol(i):
        return pl.BlockSpec((width, GROUP), lambda s: (0, i * groups + at(s)))

    first = (slot_col, res, logits, cot, n2, att, proj, small, small_t)
    return call(
        functools.partial(token_kernel, experts, size, own_rows, len(shapes), len(back)),
        [
            sds((seq, width), F32), sds((seq, GROUP), BF16), sds((seq, width), F32),
            sds(((groups - 1) * 8 * per_group, seq), F32),
        ]
        + [sds(x, BF16) for x in shapes],
        grid=(groups,),
        in_specs=[smem()] + [once(a.shape) for a in first]
        + [pl.BlockSpec((per_group, seq, seq), lambda s: (at(s), 0, 0)), col, col, col]
        + [once((seq, LANES)), once((seq, width)), wcol(0), wcol(1), wcol(2)]
        + [once(b.shape) for b in back],
        out_specs=[
            whole((seq, width)), whole((seq, GROUP)), whole((seq, width)),
            pl.BlockSpec((8 * per_group, seq), lambda s: (at(s), 0)),
        ]
        + [whole(x) for x in shapes],
        scratch_shapes=[
            pltpu.VMEM((3, seq, GROUP), BF16), pltpu.VMEM((groups, seq, GROUP), BF16),
            pltpu.VMEM((len(back) * back[0].shape[0], width + LANES), BF16),
        ]
        + scratch,
        flops=3072 * seq * width + 12 * seq * width * width + 14 * seq * seq * width,
        moved=30_000_000,
        name="token_side",
    )(me, *first, table, q, k, v, lse, n1, qkv, qkv, qkv, *back)


def tail_kernel(
    experts, size, own_rows, group, outs, me_ref, table_ref, q_ref, k_ref, v_ref, gatt_ref, lse_ref, n1_ref,
    wq_ref, wk_ref, wv_ref, acc_ref, diag_in, tokens_ref, gres_ref, small_t_ref, rev_ref, gtok_ref, *refs,
):
    parts = refs[:outs]
    g_scr, diag_scr = refs[outs : outs + 2]
    parted = Parted(size, own_rows, parts, refs[outs + 2] if size == 8 else None)
    seq, width = tokens_ref.shape
    core = me_ref[0] % 2
    heads_back(group, table_ref, q_ref, k_ref, v_ref, gatt_ref, lse_ref, g_scr, diag_scr)
    acc = acc_ref[...] + weights_back(0, n1_ref, g_scr, (wq_ref, wk_ref, wv_ref), core, parted)
    x = tokens_ref[...].astype(F32)
    gx, ggain = norm_back(x, acc, small_t_ref[experts : experts + 1, :])
    gtok_ref[...] = (gx + gres_ref[...]).astype(BF16)
    gain_rows = jnp.where(iota((LANES, width), 0) == experts, ggain, 0.0)
    diag = jnp.concatenate([diag_in[...], diag_scr[...]], axis=0)
    count = diag.shape[0]
    place = lax.rem(iota((count, seq), 0), 8)
    total = jnp.where(place == 0, diag, 0.0)
    for r in range(1, 8):
        total = total + jnp.where(place == r, pltpu.roll(diag, seq - r, 1), 0.0)
    hot = (iota((LANES, seq), 0) - (experts + 2) == rev_ref[...]).astype(F32)
    per_row = lax.dot_general(
        total, hot, (((1,), (1,)), ((), ())), precision=lax.Precision.HIGHEST, preferred_element_type=F32
    )
    copies = (lax.rem(iota((width, count), 0), own_rows) == lax.div(iota((width, count), 1), 8)).astype(F32)
    spread = jnp.dot(copies, per_row, precision=lax.Precision.HIGHEST, preferred_element_type=F32)
    parted.put(core, (gain_rows.T + spread).astype(BF16), slice(3 * GROUP, 3 * GROUP + LANES))
    parted.done()


def tail(experts, size, own_rows, me, table, q, k, v, gatt, lse, n1, qkv, acc, diag, tokens, gres, small_t, rev_buckets):
    seq, width = n1.shape
    groups = width // GROUP
    group = groups - 1
    per_group = GROUP // HEAD_DIM
    col = pl.BlockSpec((seq, GROUP), lambda _: (0, group))
    shapes, scratch = parted_shapes(size, own_rows, width, 3 * GROUP + LANES)

    def wcol(i):
        return pl.BlockSpec((width, GROUP), lambda _: (0, i * groups + group))

    rest = (acc, diag, tokens, gres, small_t, rev_buckets[None, :])
    return call(
        functools.partial(tail_kernel, experts, size, own_rows, group, len(shapes)),
        [sds((seq, width), BF16)] + [sds(x, BF16) for x in shapes],
        grid=(1,),
        in_specs=[
            smem(), pl.BlockSpec((per_group, seq, seq), lambda _: (group, 0, 0)),
            col, col, col, whole((seq, GROUP)),
            whole((seq, LANES)), whole((seq, width)),
            wcol(0), wcol(1), wcol(2),
        ]
        + [whole(x.shape) for x in rest],
        out_specs=[whole((seq, width))] + [whole(x) for x in shapes],
        scratch_shapes=[pltpu.VMEM((3, seq, GROUP), BF16), pltpu.VMEM((8 * per_group, seq), F32)] + scratch,
        flops=4 * seq * width * width + 7 * seq * seq * width,
        moved=10_000_000,
        name="tail",
    )(me, table, q, k, v, gatt, lse, n1, qkv, qkv, qkv, *rest)


def swap(value, mask, size):
    return lax.ppermute(value, "shard", [(i, i ^ mask) for i in range(size)])


def gather_blocks(value, size, beside):
    if size != 8:
        return [lax.all_gather(value, "shard", axis=0, tiled=True)], beside
    one, six, two, four = (swap(value, j, size) for j in (1, 6, 2, 4))
    one, six, two, four, *beside = lax.optimization_barrier((one, six, two, four, *beside))
    far = {0: value, 1: one, 6: six, 2: two, 4: four}
    near = {j ^ 1: swap(far[j], 1, size) for j in (6, 2, 4)}
    return [far[j] if j in far else near[j] for j in range(8)], beside


def tie(*values):
    return lax.optimization_barrier(values)


def across(value, mask, ranks):
    return lax.ppermute(value, "rep", [(i, i ^ mask) for i in range(ranks)])


def add(*values):
    total = values[0].astype(F32)
    for value in values[1:]:
        total = total + value.astype(F32)
    return total.astype(BF16)


def spread_kernel(terms, rank_ref, *refs):
    outs, total = refs[terms:-1], refs[-1]
    value = refs[0][...].astype(F32)
    for ref in refs[1:terms]:
        value = value + ref[...].astype(F32)
    wide = value.shape[1]
    total[:, :wide] = value
    if total.shape[1] > wide:
        total[:, wide:] = jnp.zeros((value.shape[0], total.shape[1] - wide), F32)
    part = outs[0].shape[1]
    for j, out in enumerate(outs):
        at = pl.multiple_of((rank_ref[0] ^ j) * part, LANES)
        out[...] = total[:, pl.ds(at, part)].astype(BF16)


def line_total(terms, rank, ranks):
    rows, wide = terms[0].shape
    part = -(-wide // (ranks * LANES)) * LANES
    parts = call(
        functools.partial(spread_kernel, len(terms)),
        [sds((rows, part), BF16)] * ranks,
        grid=(1,),
        in_specs=[smem()] + [whole((rows, wide))] * len(terms),
        out_specs=[whole((rows, part))] * ranks,
        scratch_shapes=[pltpu.VMEM((rows, part * ranks), F32)],
        name="spread",
    )(rank, *terms)
    own = add(parts[0], *[across(parts[j], j, ranks) for j in range(1, ranks)])
    return [own] + [across(own, j, ranks) for j in range(1, ranks)]


def finish_kernel(width, src_ref, *refs):
    in_ref, out_ref = refs[-2:]
    total = src_ref[0].astype(F32)
    part, block = in_ref.shape
    piece = out_ref.shape[0]
    in_ref[...] = total[:part, :]
    for j in range(width // block):
        out_ref[:, j * block : (j + 1) * block] = total[part + j * piece : part + (j + 1) * piece, :]


def finish(src, start, earlier, width, hidden, ranks):
    count, high, wide = src.shape
    block = wide // ranks
    part = width // ranks
    piece = block // ranks
    per_rank = hidden // ranks // block
    return call(
        functools.partial(finish_kernel, width),
        [sds((part, hidden), F32), sds((hidden // ranks, width), F32)],
        grid=(count, ranks),
        in_specs=[pl.BlockSpec((1, high, block), lambda c, r: (c, 0, r))]
        + [pl.BlockSpec(memory_space=pl.ANY)] * len(earlier),
        out_specs=[
            pl.BlockSpec((part, block), lambda c, r: (0, r * per_rank + start + c)),
            pl.BlockSpec((piece, width), lambda c, r: ((start + c) * ranks + r, 0)),
        ],
        input_output_aliases={1: 0, 2: 1} if earlier else {},
        name="finish",
    )(src, *earlier)


def pick_kernel(chip_ref, keep_ref, got_ref, six_ref, two_ref, four_ref, own_ref):
    chip = chip_ref[0]
    for ref, other in ((six_ref, 3), (two_ref, 1), (four_ref, 2), (own_ref, 0)):
        at = chip ^ other
        ref[...] = (keep_ref[at].astype(F32) + got_ref[at].astype(F32)).astype(BF16)


def core_sum(parts, me, size):
    if size != 8:
        return [parts[0]]
    keep, send = parts
    got = swap(send, 1, size)
    block = keep.shape[1:]
    return call(
        pick_kernel,
        [sds(block, BF16)] * 4,
        grid=(1,),
        in_specs=[smem(), whole(keep.shape), whole(keep.shape)],
        out_specs=[whole(block)] * 4,
        name="pick",
    )((me // 2).reshape(1), keep, got)


def chips_sum(blocks, size):
    if size != 8:
        return [lax.psum_scatter(blocks[0], "shard", scatter_dimension=0, tiled=True)]
    return [blocks[3]] + [swap(block, j, size) for block, j in zip(blocks, (6, 2, 4))]


def layout_kernel(width, experts, ranks, rank_ref, *refs):
    a_parts, b_parts = refs[:ranks], refs[ranks : 2 * ranks]
    qkv_ref, proj_ref, router_ref, gain_a, gain_b, bias_ref, a, b = refs[2 * ranks :]
    for parts, total in ((a_parts, a), (b_parts, b)):
        part = parts[0].shape[1]
        for j, ref in enumerate(parts):
            at = pl.multiple_of((rank_ref[0] ^ j) * part, LANES)
            total[:, pl.ds(at, part)] = ref[...].astype(F32)
    groups = width // GROUP
    for g in range(groups):
        src, base = (a, g * 3 * GROUP) if g < groups - 1 else (b, 0)
        for i in range(3):
            qkv_ref[:, i * width + g * GROUP : i * width + (g + 1) * GROUP] = src[:, base + i * GROUP : base + (i + 1) * GROUP]
    extra = (groups - 1) * 3 * GROUP
    proj_ref[...] = a[:, extra : extra + width]
    small_a = a[:, extra + width : extra + width + LANES]
    small_b = b[:, 3 * GROUP : 3 * GROUP + LANES]
    rows = small_a.shape[0]
    pad = jnp.zeros((LANES - rows, LANES), F32)
    turned_a = jnp.concatenate([small_a, pad], axis=0).T
    turned_b = jnp.concatenate([small_b, pad], axis=0).T
    router_ref[...] = turned_a[:experts, :rows]
    gain_b[...] = turned_a[experts + 1, :rows]
    gain_a[...] = turned_b[experts, :rows]
    heads, buckets = bias_ref.shape
    bias_ref[...] = small_b[:heads, experts + 2 : experts + 2 + buckets]


def layout(rank, a, b, width, experts, bias_shape):
    rows = a[0].shape[0]
    ranks = len(a)
    ins = (*a, *b)
    shapes = [(rows, 3 * width), (rows, width), (experts, rows), (rows,), (rows,), bias_shape]
    return call(
        functools.partial(layout_kernel, width, experts, ranks),
        [sds(x, F32) for x in shapes],
        grid=(1,),
        in_specs=[smem()] + [whole(x.shape) for x in ins],
        out_specs=[whole(x) for x in shapes],
        scratch_shapes=[pltpu.VMEM((rows, ranks * a[0].shape[1]), F32), pltpu.VMEM((rows, ranks * b[0].shape[1]), F32)],
        name="layout",
    )(rank, *ins)


def body(
    tokens, cotangent, segments, buckets, routes, attn_gain, qkv_weight, proj_weight,
    rel_bias, moe_gain, router, expert_in, expert_out,
):
    seq, width = tokens.shape
    size = lax.axis_size("shard")
    ranks = lax.axis_size("rep")
    top = routes.shape[1]
    experts = expert_in.shape[0] * size
    hidden = expert_in.shape[2]
    capacity = 3 * seq * top // (2 * experts)
    slots = experts * capacity
    bucket_count = rel_bias.shape[0]
    me = lax.axis_index("shard").astype(jnp.int32)
    me_arr = me.reshape(1)
    own_rows = router.shape[0]

    packed = pack_weights(qkv_weight, proj_weight, router.T, attn_gain, moe_gain)
    rev_buckets = jnp.roll(buckets[::-1], 1)
    w_blocks, (table, slot_row, slot_col, cot_slots) = gather_blocks(
        packed, size, prep(routes.T, segments, rev_buckets, rel_bias, cotangent, experts, capacity)
    )
    (q, k, v, lse, att, res, n1, n2, logits, small_full, small_t, *sent) = front(
        me_arr, tokens, table, slot_row, w_blocks, experts, slots
    )
    me_late, logits = tie(me_arr, logits)
    qkv_full, proj_full = assemble(me_late, w_blocks, width)

    def exchange(value):
        wide = value.shape[1]
        moved = lax.all_to_all(
            value.reshape(size, slots // size, wide), "shard", split_axis=0, concat_axis=0, tiled=True
        )
        return moved.reshape(slots, wide)

    cot_rows = exchange(cot_slots)

    def exchange_blocks(blocks):
        if len(blocks) == 1:
            return [exchange(blocks[0])]
        return [blocks[0]] + [swap(block, j, size) for j, block in enumerate(blocks) if j]

    cot_rows, *sent = tie(cot_rows, *sent)
    rows = exchange_blocks(sent)
    win = expert_in[0]
    wout = expert_out[0]
    per_rank = hidden // ranks // 256

    def scatter(buf):
        count, high, wide = buf.shape[1:]
        moved = lax.psum_scatter(buf.reshape(ranks * count * high, wide), "rep", scatter_dimension=0, tiled=True)
        return moved.reshape(count, high, wide)

    qkv_full, proj_full, *rows = tie(qkv_full, proj_full, *rows)
    act0, gp0, d0, buf0, sg = expert_first(me_arr, rows, cot_rows, small_full, win, wout, ranks)
    part0 = scatter(buf0)
    act1, gp1, *sends = expert_rest(rows, sg, win, wout, gp0, d0, ranks)
    back = exchange_blocks(sends)
    buf1 = expert_weight_grads(rows, sg, act1, gp1, hidden, ranks)
    act1, part0 = tie(act1, part0)
    part1 = scatter(buf1)
    result = expert_rows(me_arr, (act0, act1), wout, len(sends), ranks)
    done = finish(part0, 0, (), width, hidden, ranks)
    *back, result, one, two = tie(*back, result, *done)
    done = (one, two)
    returned = exchange(result)
    gres, gatt, acc, diag, *parts_a = token_side(
        experts, size, own_rows, me_arr, back, slot_col, res, logits, cotangent, n2, att, proj_full, small_full, small_t,
        table, q, k, v, lse, n1, qkv_full,
    )
    returned, *parts_a = tie(returned, *parts_a)
    blocks_a = core_sum(parts_a, me, size)
    gatt, *blocks_a = tie(gatt, *blocks_a)
    terms_a = chips_sum(blocks_a, size)
    grad_tokens, *parts_b = tail(
        experts, size, own_rows, me_arr, table, q, k, v, gatt, lse, n1, qkv_full, acc, diag, tokens, gres, small_t, rev_buckets
    )
    cut = len(parts_b)
    tied = tie(*parts_b, *terms_a)
    parts_b, terms_a = tied[:cut], tied[cut:]
    blocks_b = core_sum(parts_b, me, size)
    rank_arr = lax.axis_index("rep").astype(jnp.int32).reshape(1)
    line_a = line_total(terms_a, rank_arr, ranks)
    terms_b = chips_sum(blocks_b, size)
    output = output_rows(returned, slot_col, res, logits)
    output, *terms_b = tie(output, *terms_b)
    line_b = line_total(terms_b, rank_arr, ranks)
    done = finish(part1, 1, done, width, hidden, ranks)
    line_a[0], *done = tie(line_a[0], *done)
    grad_qkv, grad_proj, grad_router, gain_a, gain_b, grad_bias = layout(
        rank_arr, line_a, line_b, width, experts, rel_bias.shape[::-1]
    )
    return (
        output,
        grad_tokens,
        grad_qkv,
        grad_proj,
        grad_router.T,
        gain_a,
        gain_b,
        grad_bias.T,
        done[0][None],
        done[1][None],
    )


def solution(mesh):
    both = P(("rep", "shard"), None)
    return jax.shard_map(
        body,
        mesh=mesh,
        in_specs=(
            both, both, P(("rep", "shard")), P(), both,
            P("shard"), P("shard", None), P("shard", None), P(), P("shard"), P("shard", None),
            P("shard", None, None), P("shard", None, None),
        ),
        out_specs=(
            both, both, P("shard", None), P("shard", None), P("shard", None), P("shard"), P("shard"), P(),
            P("shard", "rep", None), P("shard", "rep", None),
        ),
        check_vma=False,
    )
```

```python
import functools
import math

import jax
import jax.numpy as jnp
from jax import lax
from jax.experimental import pallas as pl
from jax.experimental.pallas import tpu as pltpu
from jax.sharding import PartitionSpec as P

F32 = jnp.float32
BF16 = jnp.bfloat16
EPS = 1e-06
NEG = -1e30
LANES = 128
HEAD_DIM = 64
GROUP = 256
BLOCK = 256
NEAR = 512
VMEM_LIMIT = 60 * 1024 * 1024


def dot(a, b):
    return jnp.dot(a, b, preferred_element_type=F32)


def dot_nt(a, b):
    return lax.dot_general(a, b, (((1,), (1,)), ((), ())), preferred_element_type=F32)


def dot_tn(a, b):
    return lax.dot_general(a, b, (((0,), (0,)), ((), ())), preferred_element_type=F32)


def call(kernel, out_shape, **kw):
    flops = kw.pop("flops", 0)
    moved = kw.pop("moved", 0)
    return pl.pallas_call(
        kernel,
        out_shape=out_shape,
        compiler_params=pltpu.CompilerParams(vmem_limit_bytes=VMEM_LIMIT),
        cost_estimate=pl.CostEstimate(flops=flops, bytes_accessed=moved, transcendentals=0),
        **kw,
    )


def whole(shape):
    rank = len(shape)
    return pl.BlockSpec(shape, lambda *_: (0,) * rank)


def smem():
    return pl.BlockSpec(memory_space=pltpu.SMEM)


def sds(shape, dtype):
    return jax.ShapeDtypeStruct(shape, dtype)


def iota(shape, dim):
    return lax.broadcasted_iota(jnp.int32, shape, dim)


def prep_kernel(
    experts, capacity, routes_ref, seg_row, seg_col, rev_ref, bias_ref, cot_ref,
    table_ref, slot_row_ref, slot_col_ref, cot_out_ref, other_ref, mask_scr, series_scr,
):
    step = pl.program_id(0)
    seq = cot_ref.shape[0]
    width = cot_ref.shape[1]
    per = cot_out_ref.shape[0]

    @pl.when(step == 0)
    def _():
        keep = (iota((seq, seq), 0) >= iota((seq, seq), 1)) & (seg_col[...] == seg_row[...])
        mask_scr[...] = jnp.where(keep, 0.0, NEG)
        rev = rev_ref[...]
        bias = bias_ref[...]
        series = jnp.zeros((bias.shape[0], seq), F32)
        for bucket in range(bias.shape[1]):
            series = jnp.where(rev == bucket, bias[:, bucket : bucket + 1], series)
        series_scr[...] = series
        first, second = routes_ref[0:1, :], routes_ref[1:2, :]
        ids = iota((experts, seq), 0)
        m0 = (ids == first).astype(F32)
        m1 = (ids == second).astype(F32)
        before = (iota((seq, seq), 0) < iota((seq, seq), 1)).astype(BF16)
        count = dot((m0 + m1).astype(BF16), before)
        rank0 = jnp.sum(count * m0, axis=0, keepdims=True)
        rank1 = jnp.sum(count * m1, axis=0, keepdims=True)
        r0, r1 = first.astype(F32), second.astype(F32)
        slot0 = jnp.where(rank0 < capacity, r0 * capacity + rank0, -1.0)
        slot1 = jnp.where(rank1 < capacity, r1 * capacity + rank1, -1.0)
        place = iota((LANES, seq), 0)
        rows = jnp.where(place == 0, slot0, -1.0)
        rows = jnp.where(place == 1, slot1, rows)
        rows = jnp.where(place == 2, r0, rows)
        rows = jnp.where(place == 3, r1, rows)
        slot_row_ref[...] = rows[0:8, :].astype(jnp.int32)
        cols = rows.T
        slot_col_ref[...] = cols

    row = series_scr[pl.ds(step, 1), :]
    table_ref[0] = pltpu.roll(jnp.broadcast_to(row, (seq, seq)), 0, 1, stride=1, stride_axis=0) + mask_scr[...]

    @pl.when(step < 8)
    def _():
        slots = iota((per, seq), 0) + step * per
        hit0 = (slots == slot_row_ref[0:1, :]).astype(F32)
        hit1 = (slots == slot_row_ref[1:2, :]).astype(F32)
        cot_out_ref[...] = dot((hit0 + hit1).astype(BF16), cot_ref[...]).astype(BF16)
        first = jnp.broadcast_to(slot_row_ref[2:3, :].astype(F32), (8, seq)).astype(BF16)
        second = jnp.broadcast_to(slot_row_ref[3:4, :].astype(F32), (8, seq)).astype(BF16)
        other = dot_nt(second, hit0.astype(BF16)) + dot_nt(first, hit1.astype(BF16))
        other_ref[0] = other.astype(jnp.int32)


def prep(routes_t, segments, rev_buckets, rel_bias, cotangent, experts, capacity):
    seq, width = cotangent.shape
    heads = rel_bias.shape[1]
    buckets = rel_bias.shape[0]
    slots = experts * capacity
    per = slots // 8
    hp = -(-heads // 8) * 8
    bias_t = jnp.zeros((hp, buckets), F32).at[:heads].set(rel_bias.T)
    return call(
        functools.partial(prep_kernel, experts, capacity),
        [
            sds((heads, seq, seq), F32),
            sds((8, seq), jnp.int32),
            sds((seq, LANES), F32),
            sds((slots, width), BF16),
            sds((8, 8, per), jnp.int32),
        ],
        grid=(heads,),
        in_specs=[
            whole((2, seq)), whole((1, seq)), whole((seq, 1)), whole((1, seq)),
            whole((hp, buckets)), whole((seq, width)),
        ],
        out_specs=[
            pl.BlockSpec((1, seq, seq), lambda h: (h, 0, 0)),
            whole((8, seq)),
            whole((seq, LANES)),
            pl.BlockSpec((per, width), lambda h: (jnp.minimum(h, 7), 0)),
            pl.BlockSpec((1, 8, per), lambda h: (jnp.minimum(h, 7), 0, 0)),
        ],
        scratch_shapes=[
            pltpu.VMEM((seq, seq), F32),
            pltpu.VMEM((hp, seq), F32),
        ],
        flops=2 * slots * seq * width,
        moved=heads * seq * seq * 4 + 4 * seq * width,
        name="prep",
    )(routes_t, segments[None, :], segments[:, None], rev_buckets[None, :], bias_t, cotangent)


def pack_kernel(qkv_ref, proj_ref, router_ref, gain_a, gain_b, out_ref):
    rows, width = proj_ref.shape
    experts = router_ref.shape[0]
    out_ref[:, : 3 * width] = qkv_ref[...]
    out_ref[:, 3 * width : 4 * width] = proj_ref[...]
    place = iota((LANES, rows), 0)
    a = gain_a[...].astype(F32).reshape(1, rows)
    b = gain_b[...].astype(F32).reshape(1, rows)
    gains = jnp.where(place == experts, a, jnp.where(place == experts + 1, b, 0.0))
    if rows < LANES:
        gains = jnp.concatenate([gains, jnp.zeros((LANES, LANES - rows), F32)], axis=1)
    spread = (iota((experts, LANES), 0) == iota((experts, LANES), 1)).astype(BF16)
    out_ref[:, 4 * width :] = (dot_tn(router_ref[...], spread) + gains.T[:rows, :]).astype(BF16)


def pack_weights(qkv, proj, router, gain_a, gain_b):
    rows, width = proj.shape
    ins = (qkv, proj, router, gain_a, gain_b)
    return call(
        pack_kernel,
        sds((rows, 4 * width + LANES), BF16),
        grid=(1,),
        in_specs=[whole(x.shape) for x in ins],
        out_specs=whole((rows, 4 * width + LANES)),
        name="pack_weights",
    )(*ins)


def front_kernel(
    blocks, experts, me_ref, tokens_ref, table_ref, slot_row_ref, *refs,
):
    w_in = refs[:blocks]
    (q_ref, k_ref, v_ref, prob_ref, att_ref, res_ref, n1_ref, n2_ref, logit_ref,
     small_ref, small_t_ref) = refs[blocks : blocks + 11]
    qkv_ref, proj_ref = refs[-2:]
    sent_refs = refs[blocks + 11 : -2]
    step = pl.program_id(0)
    last = pl.num_programs(0) - 1
    seq, width = tokens_ref.shape
    rows = w_in[0].shape[0]
    scale = HEAD_DIM ** (-0.5)

    @pl.when(step == 0)
    def _():
        me = me_ref[0]
        for j in range(blocks):
            start = pl.multiple_of((me ^ j) * rows, rows) if blocks > 1 else 0
            qkv_ref[pl.ds(start, rows), :] = w_in[j][:, : 3 * width]
            proj_ref[pl.ds(start, rows), :] = w_in[j][:, 3 * width : 4 * width]
            small_ref[pl.ds(start, rows), :] = w_in[j][:, 4 * width :]
        small_t_ref[...] = small_ref[...].astype(F32).T
        x = tokens_ref[...].astype(F32)
        r = lax.rsqrt(jnp.mean(x * x, axis=-1, keepdims=True) + EPS)
        n1_ref[...] = (x * r * small_t_ref[experts : experts + 1, :]).astype(BF16)

    base = pl.multiple_of(step * GROUP, GROUP)
    n1 = n1_ref[...]
    q_ref[...] = dot(n1, qkv_ref[:, pl.ds(base, GROUP)]).astype(BF16)
    k_ref[...] = dot(n1, qkv_ref[:, pl.ds(width + base, GROUP)]).astype(BF16)
    v_ref[...] = dot(n1, qkv_ref[:, pl.ds(2 * width + base, GROUP)]).astype(BF16)

    half = seq // 2
    lane = iota((half, LANES), 1)
    for pair in range(GROUP // LANES):
        cols = slice(pair * LANES, (pair + 1) * LANES)
        for rb in range(2):
            span = (rb + 1) * half
            qrows = slice(rb * half, (rb + 1) * half)
            qp = q_ref[qrows, cols]
            kp = k_ref[:span, cols]
            vp = v_ref[:span, cols]
            mixed = []
            for parity in range(2):
                mine = (lane // HEAD_DIM) == parity
                qm = jnp.where(mine, qp, jnp.zeros_like(qp))
                s = dot_nt(qm, kp) * scale + table_ref[2 * pair + parity, qrows, :span]
                top = jnp.max(s, axis=-1, keepdims=True)
                e = jnp.exp(s - top)
                total = jnp.sum(e, axis=-1, keepdims=True)
                p = (e * (1.0 / total)).astype(BF16)
                mixed.append(dot(p, vp))
                prob_ref[2 * pair + parity, qrows, :span] = p
            at = pl.multiple_of(base + pair * LANES, LANES)
            att_ref[qrows, pl.ds(at, LANES)] = jnp.where(lane < HEAD_DIM, mixed[0], mixed[1]).astype(BF16)

    @pl.when(step == last)
    def _():
        x = tokens_ref[...].astype(F32) + dot(att_ref[...], proj_ref[...])
        res_ref[...] = x
        r = lax.rsqrt(jnp.mean(x * x, axis=-1, keepdims=True) + EPS)
        n2 = (x * r * small_t_ref[experts + 1 : experts + 2, :]).astype(BF16)
        n2_ref[...] = n2
        logit_ref[...] = dot(n2, small_ref[...])
        many = len(sent_refs) > 1
        per = sent_refs[0].shape[0] if many else sent_refs[0].shape[0] // 8
        for j in range(8):
            slots = iota((per, seq), 0) + ((me_ref[0] ^ j) * per if many else j * per)
            hit = (slots == slot_row_ref[0:1, :]) | (slots == slot_row_ref[1:2, :])
            rows_j = dot(hit.astype(BF16), n2).astype(BF16)
            if many:
                sent_refs[j][...] = rows_j
            else:
                sent_refs[0][j * per : (j + 1) * per, :] = rows_j


def front(me, tokens, table, slot_row, w_blocks, experts, slots):
    seq, width = tokens.shape
    blocks = len(w_blocks)
    groups = width // GROUP
    per_group = GROUP // HEAD_DIM
    col = pl.BlockSpec((seq, GROUP), lambda g: (0, g))
    return call(
        functools.partial(front_kernel, blocks, experts),
        [
            sds((seq, width), BF16), sds((seq, width), BF16), sds((seq, width), BF16),
            sds((width // HEAD_DIM, seq, seq), BF16), sds((seq, width), BF16), sds((seq, width), F32),
            sds((seq, width), BF16), sds((seq, width), BF16), sds((seq, LANES), F32),
            sds((width, LANES), BF16), sds((LANES, width), F32),
        ]
        + [sds((slots // blocks, width), BF16)] * blocks,
        grid=(groups,),
        in_specs=[
            smem(), whole((seq, width)),
            pl.BlockSpec((per_group, seq, seq), lambda g: (g, 0, 0)),
            whole((8, seq)),
        ]
        + [whole(b.shape) for b in w_blocks],
        out_specs=[
            col, col, col,
            pl.BlockSpec((per_group, seq, seq), lambda g: (g, 0, 0)), whole((seq, width)), whole((seq, width)),
            whole((seq, width)), whole((seq, width)), whole((seq, LANES)),
            whole((width, LANES)), whole((LANES, width)),
        ]
        + [whole((slots // blocks, width))] * blocks,
        scratch_shapes=[pltpu.VMEM((width, 3 * width), BF16), pltpu.VMEM((width, width), BF16)],
        flops=2 * seq * width * width * 4 + 2 * slots * seq * width + 8 * seq * seq * width,
        moved=30_000_000,
        name="front",
    )(me, tokens, table, slot_row, *w_blocks)


def assemble_kernel(blocks, me_ref, *refs):
    qkv_ref, proj_ref = refs[-2:]
    wide = qkv_ref.shape[1]
    high = proj_ref.shape[1]
    for j in range(blocks):
        rows = refs[j].shape[0]
        start = pl.multiple_of((me_ref[0] ^ j) * rows, rows) if blocks > 1 else 0
        qkv_ref[pl.ds(start, rows), :] = refs[j][:, :wide]
        proj_ref[pl.ds(start, rows), :] = refs[j][:, wide : wide + high]


def assemble(me, w_blocks, width):
    return call(
        functools.partial(assemble_kernel, len(w_blocks)),
        [sds((width, 3 * width), BF16), sds((width, width), BF16)],
        grid=(1,),
        in_specs=[smem()] + [whole(b.shape) for b in w_blocks],
        out_specs=[whole((width, 3 * width)), whole((width, width))],
        name="assemble",
    )(me, *w_blocks)


def gelu_parts(v):
    size = jnp.abs(v) * (2.0 ** -0.5)
    t = 1.0 / (1.0 + 0.3275911 * size)
    bell = jnp.exp(-0.5 * v * v)
    poly = t * (
        0.5 * 0.254829592
        + t * (0.5 * -0.284496736 + t * (0.5 * 1.421413741 + t * (0.5 * -1.453152027 + t * (0.5 * 1.061405429))))
    )
    tail = poly * bell
    below = jnp.where(v < 0, tail, 1.0 - tail)
    return v * below, below + v * bell * (1.0 / math.sqrt(2.0 * math.pi))


def join_rows(blocks, rows_ref):
    per = blocks[0].shape[0]
    for j, block in enumerate(blocks):
        rows_ref[j * per : (j + 1) * per, :] = block[...]


def gated_rows(me, parts, rows_ref, cot_ref, other_ref, small_ref, sg_ref):
    total, width = rows_ref.shape
    tile = total // 8
    for j in range(8):
        here = slice(j * tile, (j + 1) * tile)
        there = pl.ds(pl.multiple_of((me ^ j) * tile, tile), tile) if parts > 1 else here
        logits = dot(rows_ref[here, :], small_ref[...])
        lane = iota((tile, LANES), 1)
        line = other_ref[pl.ds(me ^ j if parts > 1 else j, 1), :].astype(F32)
        fill = -tile % LANES
        if fill:
            line = jnp.concatenate([line, jnp.zeros((1, fill), F32)], axis=1)
        other_id = jnp.broadcast_to(line, (8, tile + fill)).T[:tile, 0:1].astype(jnp.int32)
        own = jnp.sum(jnp.where(lane == me, logits, 0.0), axis=1, keepdims=True)
        other = jnp.sum(jnp.where(lane == other_id, logits, 0.0), axis=1, keepdims=True)
        top = jnp.maximum(own, other)
        a, b = jnp.exp(own - top), jnp.exp(other - top)
        gate = a / (a + b)
        sg_ref[here, :] = (gate * cot_ref[there, :].astype(F32)).astype(BF16)


def expert_acts(w1, w2, rows_ref, sg_ref, act_ref, gp_ref, d_ref, tile):
    for at in range(0, rows_ref.shape[0], tile):
        here = slice(at, at + tile)
        pre = dot(rows_ref[here, :], w1)
        ga = dot_nt(sg_ref[here, :], w2)
        act, slope = gelu_parts(pre)
        low = act.astype(BF16)
        act_ref[here, :] = low
        gp_ref[here, :] = (ga * slope).astype(BF16)
        d_ref[here, :] += jnp.sum(low.astype(F32) * ga, axis=1, keepdims=True)


def expert_weights(rows_t, sg_t, act_ref, gp_ref, buf_ref, cb, pair, ranks):
    width = rows_t.shape[0]
    block = BLOCK
    part = width // ranks
    piece = block // ranks
    gwin = dot(rows_t[...], gp_ref[...]).astype(BF16)
    lane0 = pl.multiple_of(pair * 2 * block, block)
    for dest in range(ranks):
        buf_ref[dest, cb, 0:part, pl.ds(lane0, 2 * block)] = gwin[dest * part : (dest + 1) * part, :]
    gwout = dot(sg_t[...], act_ref[...]).T.astype(BF16)
    for half in range(2):
        rank = 2 * pair + half
        for i in range(ranks):
            for j in range(width // block):
                buf_ref[rank, cb, part + j * piece : part + (j + 1) * piece, i * block : (i + 1) * block] = gwout[
                    half * block + i * piece : half * block + (i + 1) * piece, j * block : (j + 1) * block
                ]


def expert_first_kernel(
    ranks, tile, parts, me_ref, cot_ref, other_ref, small_ref, w1a, w1b, w2a, w2b, *refs,
):
    blocks = refs[:parts]
    act_ref, gp_ref, d_ref, buf_ref, sg_ref, rows_t, sg_t, rows_ref = refs[parts:]
    step = pl.program_id(0)

    @pl.when(step == 0)
    def _():
        join_rows(blocks, rows_ref)
        gated_rows(me_ref[0], parts, rows_ref, cot_ref, other_ref, small_ref, sg_ref)
        rows_t[...] = rows_ref[...].T
        sg_t[...] = sg_ref[...].T
        d_ref[...] = jnp.zeros_like(d_ref)

    w1 = jnp.concatenate([w1a[...], w1b[...]], axis=1)
    w2 = jnp.concatenate([w2a[...], w2b[...]], axis=0)
    expert_acts(w1, w2, rows_ref, sg_ref, act_ref, gp_ref, d_ref, tile)
    expert_weights(rows_t, sg_t, act_ref, gp_ref, buf_ref, 0, step, ranks)


def expert_rest_kernel(
    ranks, per_rank, start, tile, parts, me_ref, sg_ref, win_ref, w2a, w2b, gp0_ref, d0_ref, *refs,
):
    blocks = refs[:parts]
    act_ref, gp_ref, back_ref, side_ref = refs[parts : parts + 4]
    gp_scr, d_scr, rows_ref = refs[-3:]
    step = pl.program_id(0)
    total, width = rows_ref.shape
    block = BLOCK

    @pl.when(step == 0)
    def _():
        join_rows(blocks, rows_ref)
        d_scr[...] = d0_ref[...]
        for c in range(start):
            for r in range(ranks):
                to = (r * per_rank + c) * block
                gp_scr[:, to : to + block] = gp0_ref[:, (c * ranks + r) * block : (c * ranks + r + 1) * block]

    pairs = ranks // 2
    cb, pair = lax.div(step, pairs), lax.rem(step, pairs)
    at_a = pl.multiple_of((2 * pair * per_rank + start + cb) * block, block)
    at_b = pl.multiple_of(((2 * pair + 1) * per_rank + start + cb) * block, block)
    w1 = jnp.concatenate([win_ref[:, pl.ds(at_a, block)], win_ref[:, pl.ds(at_b, block)]], axis=1)
    w2 = jnp.concatenate([w2a[...], w2b[...]], axis=0)
    expert_acts(w1, w2, rows_ref, sg_ref, act_ref, gp_ref, d_scr, tile)
    gp_scr[:, pl.ds(at_a, block)] = gp_ref[:, :block]
    gp_scr[:, pl.ds(at_b, block)] = gp_ref[:, block:]

    @pl.when(step == pl.num_programs(0) - 1)
    def _():
        per = total // 8
        join = 2
        for at in range(0, 8, join):
            here = slice(at * per, (at + join) * per)
            back = dot_nt(gp_scr[here, :], win_ref[...]).astype(BF16)
            d = d_scr[here, :]
            high = d.astype(BF16).astype(F32)
            lane = iota(d.shape, 1)
            side = jnp.where(lane == 0, high, jnp.where(lane == 1, d - high, 0.0)).astype(BF16)
            for i in range(join):
                inner = slice(i * per, (i + 1) * per)
                if parts > 1:
                    to = pl.ds(pl.multiple_of((me_ref[0] ^ (at + i)) * per, per), per)
                else:
                    to = slice((at + i) * per, (at + i + 1) * per)
                back_ref[to, :] = back[inner, :NEAR]
                side_ref[to, : width - NEAR] = back[inner, NEAR:]
                side_ref[to, width - NEAR :] = side[inner, :]


def expert_weights_kernel(ranks, parts, sg_ref, act_ref, gp_ref, *refs):
    blocks = refs[:parts]
    buf_ref, rows_t, sg_t = refs[parts:]
    step = pl.program_id(0)
    pairs = ranks // 2
    per = blocks[0].shape[0]

    @pl.when(step == 0)
    def _():
        if per % LANES and parts > 1:
            for j in range(0, parts, 2):
                pair = jnp.concatenate([blocks[j][...], blocks[j + 1][...]], axis=0)
                rows_t[:, j * per : (j + 2) * per] = pair.T
        else:
            for j, block in enumerate(blocks):
                rows_t[:, j * per : (j + 1) * per] = block[...].T
        sg_t[...] = sg_ref[...].T

    expert_weights(rows_t, sg_t, act_ref, gp_ref, buf_ref, lax.div(step, pairs), lax.rem(step, pairs), ranks)


def expert_weight_grads(blocks, sg, act, gp, hidden, ranks):
    total, width = sg.shape
    high, wide, per_rank = expert_sizes(width, hidden, ranks)
    count = act.shape[1] // wide
    buf = (ranks, count, high, wide)
    col = pl.BlockSpec((total, 2 * BLOCK), lambda s: (0, s))
    return call(
        functools.partial(expert_weights_kernel, ranks, len(blocks)),
        sds(buf, BF16),
        grid=(count * ranks // 2,),
        in_specs=[once((total, width)), col, col] + [once(b.shape) for b in blocks],
        out_specs=whole(buf),
        scratch_shapes=[pltpu.VMEM((width, total), BF16), pltpu.VMEM((width, total), BF16)],
        flops=4 * total * width * wide * count,
        moved=20_000_000,
        name="experts_weights",
    )(sg, act, gp, *blocks)


def once(shape):
    rank = len(shape)
    return pl.BlockSpec(shape, lambda *_: (0,) * rank, pipeline_mode=pl.Buffered(1))


def expert_sizes(width, hidden, ranks):
    high = width // ranks + (width // BLOCK) * (BLOCK // ranks)
    return high, ranks * BLOCK, hidden // ranks // BLOCK


def expert_first(me, blocks, cot, other, small, win, wout, ranks):
    total = cot.shape[0]
    width, hidden = win.shape
    high, wide, per_rank = expert_sizes(width, hidden, ranks)
    buf = (ranks, 1, high, wide)
    col = pl.BlockSpec((total, 2 * BLOCK), lambda s: (0, s))

    def win_spec(half):
        return pl.BlockSpec((width, BLOCK), lambda s: (0, (2 * s + half) * per_rank))

    def wout_spec(half):
        return pl.BlockSpec((BLOCK, width), lambda s: ((2 * s + half) * per_rank, 0))

    return call(
        functools.partial(expert_first_kernel, ranks, 256, len(blocks)),
        [
            sds((total, wide), BF16), sds((total, wide), BF16), sds((total, LANES), F32), sds(buf, BF16),
            sds((total, width), BF16),
        ],
        grid=(ranks // 2,),
        in_specs=[
            smem(), once((total, width)), once(other.shape), once((width, LANES)),
            win_spec(0), win_spec(1), wout_spec(0), wout_spec(1),
        ]
        + [once(b.shape) for b in blocks],
        out_specs=[
            col, col, whole((total, LANES)), whole(buf), whole((total, width)),
        ],
        scratch_shapes=[
            pltpu.VMEM((width, total), BF16), pltpu.VMEM((width, total), BF16), pltpu.VMEM((total, width), BF16),
        ],
        flops=8 * total * width * wide,
        moved=20_000_000,
        name="experts_first",
    )(me, cot, other, small, win, win, wout, wout, *blocks)


def expert_rest(me, blocks, sg, win, wout, gp0, d0, ranks):
    total, width = sg.shape
    hidden = win.shape[1]
    high, wide, per_rank = expert_sizes(width, hidden, ranks)
    start = 1
    count = per_rank - start
    pairs = ranks // 2
    parts = len(blocks)
    col = pl.BlockSpec((total, 2 * BLOCK), lambda s: (0, s))
    out_near, out_far = (total, NEAR), (total, width + LANES - NEAR)

    def wout_spec(half):
        return pl.BlockSpec(
            (BLOCK, width), lambda s: ((2 * lax.rem(s, pairs) + half) * per_rank + start + lax.div(s, pairs), 0)
        )

    return call(
        functools.partial(expert_rest_kernel, ranks, per_rank, start, 256, parts),
        [sds((total, count * wide), BF16), sds((total, count * wide), BF16)]
        + [sds(out_near, BF16), sds(out_far, BF16)],
        grid=(count * pairs,),
        in_specs=[
            smem(), once((total, width)), once((width, hidden)), wout_spec(0), wout_spec(1),
            once((total, start * wide)), once((total, LANES)),
        ]
        + [once(b.shape) for b in blocks],
        out_specs=[col, col, whole(out_near), whole(out_far)],
        scratch_shapes=[
            pltpu.VMEM((total, hidden), BF16), pltpu.VMEM((total, LANES), F32), pltpu.VMEM((total, width), BF16),
        ],
        flops=4 * total * width * wide * count + 2 * total * width * hidden,
        moved=30_000_000,
        name="experts_rest",
    )(me, sg, win, wout, wout, gp0, d0, *blocks)


def expert_rows_kernel(ranks, per_rank, parts, count, me_ref, *refs):
    acts, w_ref, o_ref, w_scr = refs[:count], refs[count], refs[count + 1], refs[count + 2]

    @pl.when(pl.program_id(0) == 0)
    def _():
        for c in range(per_rank):
            for r in range(ranks):
                to, src = (c * ranks + r) * BLOCK, (r * per_rank + c) * BLOCK
                w_scr[to : to + BLOCK, :] = w_ref[src : src + BLOCK, :]

    at, total = 0, None
    for act in acts:
        wide = act.shape[1]
        more = dot(act[...], w_scr[at : at + wide, :])
        total = more if total is None else total + more
        at += wide
    low = total.astype(BF16)
    if parts == 1:
        o_ref[...] = low
    else:
        per = low.shape[0] // 2
        flip = me_ref[0] % 2
        o_ref[pl.ds(pl.multiple_of(flip * per, per), per), :] = low[:per, :]
        o_ref[pl.ds(pl.multiple_of((1 - flip) * per, per), per), :] = low[per:, :]


def expert_rows(me, acts, wout, parts, ranks):
    total = acts[0].shape[0]
    hidden, width = wout.shape
    tile = total // 4

    def place(i, m):
        return ((m[0] // 2) ^ i if parts > 1 else i, 0)

    return pl.pallas_call(
        functools.partial(expert_rows_kernel, ranks, hidden // ranks // BLOCK, parts, len(acts)),
        sds((total, width), BF16),
        grid_spec=pltpu.PrefetchScalarGridSpec(
            num_scalar_prefetch=1,
            grid=(4,),
            in_specs=[pl.BlockSpec((tile, a.shape[1]), lambda i, m: (i, 0)) for a in acts] + [once(wout.shape)],
            out_specs=pl.BlockSpec((tile, width), place),
            scratch_shapes=[pltpu.VMEM(wout.shape, BF16)],
        ),
        compiler_params=pltpu.CompilerParams(vmem_limit_bytes=VMEM_LIMIT),
        name="expert_rows",
    )(me, *acts, wout)


def norm_back(x, grad, gain):
    r = lax.rsqrt(jnp.mean(x * x, axis=-1, keepdims=True) + EPS)
    u = grad * gain
    inner = jnp.mean(u * x, axis=-1, keepdims=True)
    xr = x * r
    return r * u - (r * r * r) * x * inner, jnp.sum(grad * xr, axis=0, keepdims=True)


def pair_gates(slot_ref, logit_ref):
    logits = logit_ref[...]
    lane = iota(logits.shape, 1)
    hot0 = lane == slot_ref[:, 2:3].astype(jnp.int32)
    hot1 = lane == slot_ref[:, 3:4].astype(jnp.int32)
    c0 = jnp.sum(jnp.where(hot0, logits, 0.0), axis=1, keepdims=True)
    c1 = jnp.sum(jnp.where(hot1, logits, 0.0), axis=1, keepdims=True)
    top = jnp.maximum(c0, c1)
    e0, e1 = jnp.exp(c0 - top), jnp.exp(c1 - top)
    return e0 / (e0 + e1), e1 / (e0 + e1), hot0, hot1


def pair_hits(slot_ref, slots):
    spot = iota((slot_ref.shape[0], slots), 1)
    h0 = (spot == slot_ref[:, 0:1].astype(jnp.int32)).astype(BF16)
    h1 = (spot == slot_ref[:, 1:2].astype(jnp.int32)).astype(BF16)
    return h0, h1


def output_kernel(ret_ref, slot_ref, res_ref, logit_ref, out_ref):
    h0, h1 = pair_hits(slot_ref, ret_ref.shape[0])
    g0, g1, _, _ = pair_gates(slot_ref, logit_ref)
    ret = ret_ref[...]
    out_ref[...] = (res_ref[...] + (g0 * dot(h0, ret) + g1 * dot(h1, ret))).astype(BF16)


def output_rows(returned, slot_col, res, logits):
    ins = (returned, slot_col, res, logits)
    return call(
        output_kernel,
        sds(res.shape, BF16),
        grid=(1,),
        in_specs=[whole(x.shape) for x in ins],
        out_specs=whole(res.shape),
        flops=4 * returned.shape[0] * res.size,
        moved=6_000_000,
        name="output_rows",
    )(*ins)


def heads_back(prob_ref, q_ref, k_ref, v_ref, gatt_ref, g_scr, diag_ref):
    seq = q_ref.shape[0]
    half = seq // 2
    scale = HEAD_DIM ** (-0.5)
    lane = iota((half, LANES), 1)
    full_lane = iota((seq, LANES), 1)
    for pair in range(GROUP // LANES):
        cols = slice(pair * LANES, (pair + 1) * LANES)
        dk = [jnp.zeros((seq, LANES), F32)] * 2
        dv = [jnp.zeros((seq, LANES), F32)] * 2
        skew = [jnp.zeros((LANES, seq), F32)] * 2
        for rb in range(2):
            span = (rb + 1) * half
            qrows = slice(rb * half, (rb + 1) * half)
            qp = q_ref[qrows, cols]
            gp = gatt_ref[qrows, cols]
            kp = k_ref[:span, cols]
            vp = v_ref[:span, cols]
            dq = []
            for parity in range(2):
                mine = (lane // HEAD_DIM) == parity
                gm = jnp.where(mine, gp, jnp.zeros_like(gp))
                low_p = prob_ref[2 * pair + parity, qrows, :span]
                p = low_p.astype(F32)
                dp = dot_nt(gm, vp)
                d = jnp.sum(p * dp, axis=1, keepdims=True)
                ds = p * (dp - d)
                low = ds.astype(BF16)
                dq.append(dot(low, kp) * scale)
                add_k = dot_tn(low, qp) * scale
                add_v = dot_tn(low_p, gp)
                if span < seq:
                    zero = jnp.zeros((seq - span, LANES), F32)
                    add_k = jnp.concatenate([add_k, zero], axis=0)
                    add_v = jnp.concatenate([add_v, zero], axis=0)
                dk[parity] = dk[parity] + add_k
                dv[parity] = dv[parity] + add_v
                wide = low.astype(F32)
                if span < seq:
                    wide = jnp.concatenate([wide, jnp.zeros((half, seq - span), F32)], axis=1)
                for b in range(half // LANES):
                    shift = rb * half + b * LANES
                    rows = wide[b * LANES : (b + 1) * LANES, :]
                    if shift:
                        rows = jnp.concatenate([rows[:, shift:], rows[:, :shift]], axis=1)
                    skew[parity] = skew[parity] + rows
            g_scr[0, qrows, cols] = jnp.where(lane < HEAD_DIM, dq[0], dq[1]).astype(BF16)
        g_scr[1, :, cols] = jnp.where(full_lane < HEAD_DIM, dk[0], dk[1]).astype(BF16)
        g_scr[2, :, cols] = jnp.where(full_lane < HEAD_DIM, dv[0], dv[1]).astype(BF16)
        for parity in range(2):
            acc = skew[parity][0:8, :]
            for i in range(1, LANES // 8):
                acc = acc + pltpu.roll(skew[parity][i * 8 : (i + 1) * 8, :], seq - i * 8, 1)
            at = 8 * (2 * pair + parity)
            diag_ref[at : at + 8, :] = acc


class Parted:
    def __init__(self, size, rows, refs, scratch):
        self.size, self.rows, self.refs, self.scratch = size, rows, refs, scratch

    def put(self, core, value, lanes):
        if self.size != 8:
            self.refs[0][:, lanes] = value
            return
        for b in range(8):
            self.scratch[(b % 2) ^ core, b // 2, :, lanes] = value[b * self.rows : (b + 1) * self.rows, :]

    def done(self):
        if self.size == 8:
            self.refs[0][...] = self.scratch[0]
            self.refs[1][...] = self.scratch[1]


def parted_shapes(size, rows, width, wide):
    if size != 8:
        return [(width, wide)], []
    return [(4, rows, wide)] * 2, [pltpu.VMEM((2, 4, rows, wide), BF16)]


def weights_back(group_at, n1_ref, g_scr, w_refs, core, parted):
    acc = None
    for i, w_ref in enumerate(w_refs):
        g = g_scr[i]
        at = group_at + i * GROUP
        if not isinstance(at, int):
            at = pl.multiple_of(at, GROUP)
        parted.put(core, dot_tn(n1_ref[...], g).astype(BF16), pl.ds(at, GROUP))
        more = dot_nt(g, w_ref[...])
        acc = more if acc is None else acc + more
    return acc


def token_kernel(
    experts, size, own_rows, outs, parts_in, me_ref, slot_ref, res_ref, logit_ref, cot_ref, n2_ref, att_ref,
    proj_ref, small_ref, small_t_ref, prob_ref, q_ref, k_ref, v_ref, n1_ref, wq_ref, wk_ref, wv_ref, *refs,
):
    blocks, refs = refs[:parts_in], refs[parts_in:]
    gres_ref, gatt_ref, acc_ref, diag_ref = refs[:4]
    parts = refs[4 : 4 + outs]
    g_scr, gatt_scr, back_ref = refs[4 + outs : 7 + outs]
    parted = Parted(size, own_rows, parts, refs[7 + outs] if size == 8 else None)
    step = pl.program_id(0)
    seq, width = res_ref.shape
    core = me_ref[0] % 2
    groups = width // GROUP
    extra = (groups - 1) * 3 * GROUP

    @pl.when(step == 0)
    def _():
        at = 0
        for block in blocks:
            back_ref[:, at : at + block.shape[1]] = block[...]
            at += block.shape[1]
        h0, h1 = pair_hits(slot_ref, back_ref.shape[0])
        g0, g1, hot0, hot1 = pair_gates(slot_ref, logit_ref)
        back = back_ref[:, :width]
        sides = back_ref[:, width:]
        d0 = jnp.sum(dot(h0, sides), axis=1, keepdims=True)
        d1 = jnp.sum(dot(h1, sides), axis=1, keepdims=True)
        glog = jnp.where(hot0, d0 - g0 * (d0 + d1), 0.0) + jnp.where(hot1, d1 - g1 * (d0 + d1), 0.0)
        glog = glog.astype(BF16)
        x = res_ref[...]
        small = small_ref[...]
        router = jnp.where(iota((width, LANES), 1) < experts, small, jnp.zeros_like(small))
        grad = dot(h0 + h1, back) + dot_nt(glog, router)
        gx, ggain = norm_back(x, grad, small_t_ref[experts + 1 : experts + 2, :])
        gres = gx + cot_ref[...].astype(F32)
        gres_ref[...] = gres
        branch = gres.astype(BF16)
        gatt = dot_nt(branch, proj_ref[...]).astype(BF16)
        for g in range(groups):
            gatt_scr[g] = gatt[:, g * GROUP : (g + 1) * GROUP]
        gatt_ref[...] = gatt[:, (groups - 1) * GROUP :]
        parted.put(core, dot_tn(att_ref[...], branch).astype(BF16), slice(extra, extra + width))
        gain_rows = jnp.where(iota((LANES, width), 0) == experts + 1, ggain, 0.0)
        more = (dot_tn(n2_ref[...], glog) + gain_rows.T).astype(BF16)
        parted.put(core, more, slice(extra + width, extra + width + LANES))

    @pl.when(step > 0)
    def _():
        group = step - 1
        heads_back(prob_ref, q_ref, k_ref, v_ref, gatt_scr.at[group], g_scr, diag_ref)
        more = weights_back(group * 3 * GROUP, n1_ref, g_scr, (wq_ref, wk_ref, wv_ref), core, parted)

        @pl.when(step == 1)
        def _():
            acc_ref[...] = more

        @pl.when(step > 1)
        def _():
            acc_ref[...] += more

    @pl.when(step == pl.num_programs(0) - 1)
    def _():
        parted.done()


def token_side(
    experts, size, own_rows, me, back, slot_col, res, logits, cot, n2, att, proj, small, small_t,
    probs, q, k, v, n1, qkv,
):
    seq, width = res.shape
    groups = width // GROUP
    per_group = GROUP // HEAD_DIM
    wide = (groups - 1) * 3 * GROUP + width + LANES
    shapes, scratch = parted_shapes(size, own_rows, width, wide)

    def at(s):
        return jnp.maximum(s - 1, 0)

    col = pl.BlockSpec((seq, GROUP), lambda s: (0, at(s)))

    def wcol(i):
        return pl.BlockSpec((width, GROUP), lambda s: (0, i * groups + at(s)))

    first = (slot_col, res, logits, cot, n2, att, proj, small, small_t)
    return call(
        functools.partial(token_kernel, experts, size, own_rows, len(shapes), len(back)),
        [
            sds((seq, width), F32), sds((seq, GROUP), BF16), sds((seq, width), F32),
            sds(((groups - 1) * 8 * per_group, seq), F32),
        ]
        + [sds(x, BF16) for x in shapes],
        grid=(groups,),
        in_specs=[smem()] + [once(a.shape) for a in first]
        + [pl.BlockSpec((per_group, seq, seq), lambda s: (at(s), 0, 0)), col, col, col]
        + [once((seq, width)), wcol(0), wcol(1), wcol(2)]
        + [once(b.shape) for b in back],
        out_specs=[
            whole((seq, width)), whole((seq, GROUP)), whole((seq, width)),
            pl.BlockSpec((8 * per_group, seq), lambda s: (at(s), 0)),
        ]
        + [whole(x) for x in shapes],
        scratch_shapes=[
            pltpu.VMEM((3, seq, GROUP), BF16), pltpu.VMEM((groups, seq, GROUP), BF16),
            pltpu.VMEM((back[0].shape[0], width + LANES), BF16),
        ]
        + scratch,
        flops=3072 * seq * width + 12 * seq * width * width + 14 * seq * seq * width,
        moved=30_000_000,
        name="token_side",
    )(me, *first, probs, q, k, v, n1, qkv, qkv, qkv, *back)


def tail_kernel(
    experts, size, own_rows, outs, me_ref, prob_ref, q_ref, k_ref, v_ref, gatt_ref, n1_ref,
    wq_ref, wk_ref, wv_ref, acc_ref, diag_in, tokens_ref, gres_ref, small_t_ref, rev_ref, gtok_ref, *refs,
):
    parts = refs[:outs]
    g_scr, diag_scr = refs[outs : outs + 2]
    parted = Parted(size, own_rows, parts, refs[outs + 2] if size == 8 else None)
    seq, width = tokens_ref.shape
    core = me_ref[0] % 2
    heads_back(prob_ref, q_ref, k_ref, v_ref, gatt_ref, g_scr, diag_scr)
    acc = acc_ref[...] + weights_back(0, n1_ref, g_scr, (wq_ref, wk_ref, wv_ref), core, parted)
    x = tokens_ref[...].astype(F32)
    gx, ggain = norm_back(x, acc, small_t_ref[experts : experts + 1, :])
    gtok_ref[...] = (gx + gres_ref[...]).astype(BF16)
    gain_rows = jnp.where(iota((LANES, width), 0) == experts, ggain, 0.0)
    diag = jnp.concatenate([diag_in[...], diag_scr[...]], axis=0)
    count = diag.shape[0]
    place = lax.rem(iota((count, seq), 0), 8)
    total = jnp.where(place == 0, diag, 0.0)
    for r in range(1, 8):
        total = total + jnp.where(place == r, pltpu.roll(diag, seq - r, 1), 0.0)
    hot = (iota((LANES, seq), 0) - (experts + 2) == rev_ref[...]).astype(F32)
    per_row = lax.dot_general(
        total, hot, (((1,), (1,)), ((), ())), precision=lax.Precision.HIGHEST, preferred_element_type=F32
    )
    copies = (lax.rem(iota((width, count), 0), own_rows) == lax.div(iota((width, count), 1), 8)).astype(F32)
    spread = jnp.dot(copies, per_row, precision=lax.Precision.HIGHEST, preferred_element_type=F32)
    parted.put(core, (gain_rows.T + spread).astype(BF16), slice(3 * GROUP, 3 * GROUP + LANES))
    parted.done()


def tail(experts, size, own_rows, me, probs, q, k, v, gatt, n1, qkv, acc, diag, tokens, gres, small_t, rev_buckets):
    seq, width = n1.shape
    groups = width // GROUP
    group = groups - 1
    per_group = GROUP // HEAD_DIM
    col = pl.BlockSpec((seq, GROUP), lambda _: (0, group))
    shapes, scratch = parted_shapes(size, own_rows, width, 3 * GROUP + LANES)

    def wcol(i):
        return pl.BlockSpec((width, GROUP), lambda _: (0, i * groups + group))

    rest = (acc, diag, tokens, gres, small_t, rev_buckets[None, :])
    return call(
        functools.partial(tail_kernel, experts, size, own_rows, len(shapes)),
        [sds((seq, width), BF16)] + [sds(x, BF16) for x in shapes],
        grid=(1,),
        in_specs=[
            smem(), pl.BlockSpec((per_group, seq, seq), lambda _: (group, 0, 0)),
            col, col, col, whole((seq, GROUP)),
            whole((seq, width)),
            wcol(0), wcol(1), wcol(2),
        ]
        + [whole(x.shape) for x in rest],
        out_specs=[whole((seq, width))] + [whole(x) for x in shapes],
        scratch_shapes=[pltpu.VMEM((3, seq, GROUP), BF16), pltpu.VMEM((8 * per_group, seq), F32)] + scratch,
        flops=4 * seq * width * width + 7 * seq * seq * width,
        moved=10_000_000,
        name="tail",
    )(me, probs, q, k, v, gatt, n1, qkv, qkv, qkv, *rest)


def swap(value, mask, size):
    return lax.ppermute(value, "shard", [(i, i ^ mask) for i in range(size)])


def gather_blocks(value, size, beside):
    if size != 8:
        return [lax.all_gather(value, "shard", axis=0, tiled=True)], beside
    one, six, two, four = (swap(value, j, size) for j in (1, 6, 2, 4))
    one, six, two, four, *beside = lax.optimization_barrier((one, six, two, four, *beside))
    far = {0: value, 1: one, 6: six, 2: two, 4: four}
    near = {j ^ 1: swap(far[j], 1, size) for j in (6, 2, 4)}
    return [far[j] if j in far else near[j] for j in range(8)], beside


def tie(*values):
    return lax.optimization_barrier(values)


def across(value, mask, ranks):
    return lax.ppermute(value, "rep", [(i, i ^ mask) for i in range(ranks)])


def add(*values):
    total = values[0].astype(F32)
    for value in values[1:]:
        total = total + value.astype(F32)
    return total.astype(BF16)


def spread_kernel(terms, rank_ref, *refs):
    outs, total = refs[terms:-1], refs[-1]
    value = refs[0][...].astype(F32)
    for ref in refs[1:terms]:
        value = value + ref[...].astype(F32)
    wide = value.shape[1]
    total[:, :wide] = value
    if total.shape[1] > wide:
        total[:, wide:] = jnp.zeros((value.shape[0], total.shape[1] - wide), F32)
    part = outs[0].shape[1]
    for j, out in enumerate(outs):
        at = pl.multiple_of((rank_ref[0] ^ j) * part, LANES)
        out[...] = total[:, pl.ds(at, part)].astype(BF16)


def line_total(terms, rank, ranks):
    rows, wide = terms[0].shape
    part = -(-wide // (ranks * LANES)) * LANES
    parts = call(
        functools.partial(spread_kernel, len(terms)),
        [sds((rows, part), BF16)] * ranks,
        grid=(1,),
        in_specs=[smem()] + [whole((rows, wide))] * len(terms),
        out_specs=[whole((rows, part))] * ranks,
        scratch_shapes=[pltpu.VMEM((rows, part * ranks), F32)],
        name="spread",
    )(rank, *terms)
    own = add(parts[0], *[across(parts[j], j, ranks) for j in range(1, ranks)])
    return [own] + [across(own, j, ranks) for j in range(1, ranks)]


def finish_kernel(width, src_ref, *refs):
    in_ref, out_ref = refs[-2:]
    total = src_ref[0].astype(F32)
    part, block = in_ref.shape
    piece = out_ref.shape[0]
    in_ref[...] = total[:part, :]
    for j in range(width // block):
        out_ref[:, j * block : (j + 1) * block] = total[part + j * piece : part + (j + 1) * piece, :]


def finish(src, start, earlier, width, hidden, ranks):
    count, high, wide = src.shape
    block = wide // ranks
    part = width // ranks
    piece = block // ranks
    per_rank = hidden // ranks // block
    return call(
        functools.partial(finish_kernel, width),
        [sds((part, hidden), F32), sds((hidden // ranks, width), F32)],
        grid=(count, ranks),
        in_specs=[pl.BlockSpec((1, high, block), lambda c, r: (c, 0, r))]
        + [pl.BlockSpec(memory_space=pl.ANY)] * len(earlier),
        out_specs=[
            pl.BlockSpec((part, block), lambda c, r: (0, r * per_rank + start + c)),
            pl.BlockSpec((piece, width), lambda c, r: ((start + c) * ranks + r, 0)),
        ],
        input_output_aliases={1: 0, 2: 1} if earlier else {},
        name="finish",
    )(src, *earlier)


def pick_kernel(chip_ref, keep_ref, got_ref, six_ref, two_ref, four_ref, own_ref):
    chip = chip_ref[0]
    for ref, other in ((six_ref, 3), (two_ref, 1), (four_ref, 2), (own_ref, 0)):
        at = chip ^ other
        ref[...] = (keep_ref[at].astype(F32) + got_ref[at].astype(F32)).astype(BF16)


def core_sum(parts, me, size):
    if size != 8:
        return [parts[0]]
    keep, send = parts
    got = swap(send, 1, size)
    block = keep.shape[1:]
    return call(
        pick_kernel,
        [sds(block, BF16)] * 4,
        grid=(1,),
        in_specs=[smem(), whole(keep.shape), whole(keep.shape)],
        out_specs=[whole(block)] * 4,
        name="pick",
    )((me // 2).reshape(1), keep, got)


def chips_sum(blocks, size):
    if size != 8:
        return [lax.psum_scatter(blocks[0], "shard", scatter_dimension=0, tiled=True)]
    return [blocks[3]] + [swap(block, j, size) for block, j in zip(blocks, (6, 2, 4))]


def layout_kernel(width, experts, ranks, rank_ref, *refs):
    a_parts, b_parts = refs[:ranks], refs[ranks : 2 * ranks]
    qkv_ref, proj_ref, router_ref, gain_a, gain_b, bias_ref, a, b = refs[2 * ranks :]
    for parts, total in ((a_parts, a), (b_parts, b)):
        part = parts[0].shape[1]
        for j, ref in enumerate(parts):
            at = pl.multiple_of((rank_ref[0] ^ j) * part, LANES)
            total[:, pl.ds(at, part)] = ref[...].astype(F32)
    groups = width // GROUP
    for g in range(groups):
        src, base = (a, g * 3 * GROUP) if g < groups - 1 else (b, 0)
        for i in range(3):
            qkv_ref[:, i * width + g * GROUP : i * width + (g + 1) * GROUP] = src[:, base + i * GROUP : base + (i + 1) * GROUP]
    extra = (groups - 1) * 3 * GROUP
    proj_ref[...] = a[:, extra : extra + width]
    small_a = a[:, extra + width : extra + width + LANES]
    small_b = b[:, 3 * GROUP : 3 * GROUP + LANES]
    rows = small_a.shape[0]
    pad = jnp.zeros((LANES - rows, LANES), F32)
    turned_a = jnp.concatenate([small_a, pad], axis=0).T
    turned_b = jnp.concatenate([small_b, pad], axis=0).T
    router_ref[...] = turned_a[:experts, :rows]
    gain_b[...] = turned_a[experts + 1, :rows]
    gain_a[...] = turned_b[experts, :rows]
    heads, buckets = bias_ref.shape
    bias_ref[...] = small_b[:heads, experts + 2 : experts + 2 + buckets]


def layout(rank, a, b, width, experts, bias_shape):
    rows = a[0].shape[0]
    ranks = len(a)
    ins = (*a, *b)
    shapes = [(rows, 3 * width), (rows, width), (experts, rows), (rows,), (rows,), bias_shape]
    return call(
        functools.partial(layout_kernel, width, experts, ranks),
        [sds(x, F32) for x in shapes],
        grid=(1,),
        in_specs=[smem()] + [whole(x.shape) for x in ins],
        out_specs=[whole(x) for x in shapes],
        scratch_shapes=[pltpu.VMEM((rows, ranks * a[0].shape[1]), F32), pltpu.VMEM((rows, ranks * b[0].shape[1]), F32)],
        name="layout",
    )(rank, *ins)


def body(
    tokens, cotangent, segments, buckets, routes, attn_gain, qkv_weight, proj_weight,
    rel_bias, moe_gain, router, expert_in, expert_out,
):
    seq, width = tokens.shape
    size = lax.axis_size("shard")
    ranks = lax.axis_size("rep")
    top = routes.shape[1]
    experts = expert_in.shape[0] * size
    hidden = expert_in.shape[2]
    capacity = 3 * seq * top // (2 * experts)
    slots = experts * capacity
    bucket_count = rel_bias.shape[0]
    me = lax.axis_index("shard").astype(jnp.int32)
    me_arr = me.reshape(1)
    own_rows = router.shape[0]

    packed = pack_weights(qkv_weight, proj_weight, router.T, attn_gain, moe_gain)
    rev_buckets = jnp.roll(buckets[::-1], 1)
    *tables, other = prep(routes.T, segments, rev_buckets, rel_bias, cotangent, experts, capacity)
    other = lax.all_to_all(
        other[:, 0, :].reshape(size, slots // size), "shard", split_axis=0, concat_axis=0, tiled=True
    )
    w_blocks, (table, slot_row, slot_col, cot_slots, other) = gather_blocks(packed, size, (*tables, other))
    other = other.reshape(8, slots // 8)
    (q, k, v, probs, att, res, n1, n2, logits, small_full, small_t, *sent) = front(
        me_arr, tokens, table, slot_row, w_blocks, experts, slots
    )
    me_late, logits = tie(me_arr, logits)
    qkv_full, proj_full = assemble(me_late, w_blocks, width)

    def exchange(value):
        wide = value.shape[1]
        moved = lax.all_to_all(
            value.reshape(size, slots // size, wide), "shard", split_axis=0, concat_axis=0, tiled=True
        )
        return moved.reshape(slots, wide)

    cot_rows = exchange(cot_slots)

    def exchange_blocks(blocks):
        if len(blocks) == 1:
            return [exchange(blocks[0])]
        return [blocks[0]] + [swap(block, j, size) for j, block in enumerate(blocks) if j]

    cot_rows, *sent = tie(cot_rows, *sent)
    rows = exchange_blocks(sent)
    win = expert_in[0]
    wout = expert_out[0]
    per_rank = hidden // ranks // 256

    def scatter(buf):
        count, high, wide = buf.shape[1:]
        moved = lax.psum_scatter(buf.reshape(ranks * count * high, wide), "rep", scatter_dimension=0, tiled=True)
        return moved.reshape(count, high, wide)

    qkv_full, proj_full, *rows = tie(qkv_full, proj_full, *rows)
    act0, gp0, d0, buf0, sg = expert_first(me_arr, rows, cot_rows, other, small_full, win, wout, ranks)
    part0 = scatter(buf0)
    act1, gp1, send_near, send_far = expert_rest(me_arr, rows, sg, win, wout, gp0, d0, ranks)
    near = exchange(send_near)
    buf1 = expert_weight_grads(rows, sg, act1, gp1, hidden, ranks)
    buf1, part0, near, act1, send_far = tie(buf1, part0, near, act1, send_far)
    part1 = scatter(buf1)
    far = exchange(send_far)
    result = expert_rows(me_arr, (act0, act1), wout, len(rows), ranks)
    near, far, result = tie(near, far, result)
    returned = exchange(result)
    gres, gatt, acc, diag, *parts_a = token_side(
        experts, size, own_rows, me_arr, [near, far], slot_col, res, logits, cotangent, n2, att, proj_full, small_full, small_t,
        probs, q, k, v, n1, qkv_full,
    )
    returned, *parts_a = tie(returned, *parts_a)
    blocks_a = core_sum(parts_a, me, size)
    gatt, *blocks_a = tie(gatt, *blocks_a)
    terms_a = chips_sum(blocks_a, size)
    grad_tokens, *parts_b = tail(
        experts, size, own_rows, me_arr, probs, q, k, v, gatt, n1, qkv_full, acc, diag, tokens, gres, small_t, rev_buckets
    )
    cut = len(parts_b)
    tied = tie(*parts_b, *terms_a)
    parts_b, terms_a = tied[:cut], tied[cut:]
    blocks_b = core_sum(parts_b, me, size)
    rank_arr = lax.axis_index("rep").astype(jnp.int32).reshape(1)
    done = finish(part0, 0, (), width, hidden, ranks)
    one, two, *terms_a = tie(*done, *terms_a)
    done = (one, two)
    line_a = line_total(terms_a, rank_arr, ranks)
    terms_b = chips_sum(blocks_b, size)
    output = output_rows(returned, slot_col, res, logits)
    output, *terms_b = tie(output, *terms_b)
    line_b = line_total(terms_b, rank_arr, ranks)
    done = finish(part1, 1, done, width, hidden, ranks)
    line_a[0], *done = tie(line_a[0], *done)
    grad_qkv, grad_proj, grad_router, gain_a, gain_b, grad_bias = layout(
        rank_arr, line_a, line_b, width, experts, rel_bias.shape[::-1]
    )
    return (
        output,
        grad_tokens,
        grad_qkv,
        grad_proj,
        grad_router.T,
        gain_a,
        gain_b,
        grad_bias.T,
        done[0][None],
        done[1][None],
    )


def solution(mesh):
    both = P(("rep", "shard"), None)
    return jax.shard_map(
        body,
        mesh=mesh,
        in_specs=(
            both, both, P(("rep", "shard")), P(), both,
            P("shard"), P("shard", None), P("shard", None), P(), P("shard"), P("shard", None),
            P("shard", None, None), P("shard", None, None),
        ),
        out_specs=(
            both, both, P("shard", None), P("shard", None), P("shard", None), P("shard"), P("shard"), P(),
            P("shard", "rep", None), P("shard", "rep", None),
        ),
        check_vma=False,
    )
```

```python
import functools
import math

import jax
import jax.numpy as jnp
from jax import lax
from jax.experimental import pallas as pl
from jax.experimental.pallas import tpu as pltpu
from jax.sharding import PartitionSpec as P

F32 = jnp.float32
BF16 = jnp.bfloat16
EPS = 1e-06
NEG = -1e30
LANES = 128
HEAD_DIM = 64
GROUP = 256
BLOCK = 256
NEAR = 512
VMEM_LIMIT = 60 * 1024 * 1024


def dot(a, b):
    return jnp.dot(a, b, preferred_element_type=F32)


def dot_nt(a, b):
    return lax.dot_general(a, b, (((1,), (1,)), ((), ())), preferred_element_type=F32)


def dot_tn(a, b):
    return lax.dot_general(a, b, (((0,), (0,)), ((), ())), preferred_element_type=F32)


def call(kernel, out_shape, **kw):
    flops = kw.pop("flops", 0)
    moved = kw.pop("moved", 0)
    return pl.pallas_call(
        kernel,
        out_shape=out_shape,
        compiler_params=pltpu.CompilerParams(vmem_limit_bytes=VMEM_LIMIT),
        cost_estimate=pl.CostEstimate(flops=flops, bytes_accessed=moved, transcendentals=0),
        **kw,
    )


def whole(shape):
    rank = len(shape)
    return pl.BlockSpec(shape, lambda *_: (0,) * rank)


def smem():
    return pl.BlockSpec(memory_space=pltpu.SMEM)


def sds(shape, dtype):
    return jax.ShapeDtypeStruct(shape, dtype)


def iota(shape, dim):
    return lax.broadcasted_iota(jnp.int32, shape, dim)


def prep_kernel(
    experts, capacity, routes_ref, seg_row, seg_col, rev_ref, bias_ref, cot_ref,
    table_ref, slot_row_ref, slot_col_ref, cot_out_ref, other_ref, mask_scr, series_scr,
):
    step = pl.program_id(0)
    seq = cot_ref.shape[0]
    width = cot_ref.shape[1]
    per = cot_out_ref.shape[0]

    @pl.when(step == 0)
    def _():
        keep = (iota((seq, seq), 0) >= iota((seq, seq), 1)) & (seg_col[...] == seg_row[...])
        mask_scr[...] = jnp.where(keep, 0.0, NEG)
        rev = rev_ref[...]
        bias = bias_ref[...]
        series = jnp.zeros((bias.shape[0], seq), F32)
        for bucket in range(bias.shape[1]):
            series = jnp.where(rev == bucket, bias[:, bucket : bucket + 1], series)
        series_scr[...] = series
        first, second = routes_ref[0:1, :], routes_ref[1:2, :]
        ids = iota((experts, seq), 0)
        m0 = (ids == first).astype(F32)
        m1 = (ids == second).astype(F32)
        before = (iota((seq, seq), 0) < iota((seq, seq), 1)).astype(BF16)
        count = dot((m0 + m1).astype(BF16), before)
        rank0 = jnp.sum(count * m0, axis=0, keepdims=True)
        rank1 = jnp.sum(count * m1, axis=0, keepdims=True)
        r0, r1 = first.astype(F32), second.astype(F32)
        slot0 = jnp.where(rank0 < capacity, r0 * capacity + rank0, -1.0)
        slot1 = jnp.where(rank1 < capacity, r1 * capacity + rank1, -1.0)
        place = iota((LANES, seq), 0)
        rows = jnp.where(place == 0, slot0, -1.0)
        rows = jnp.where(place == 1, slot1, rows)
        rows = jnp.where(place == 2, r0, rows)
        rows = jnp.where(place == 3, r1, rows)
        slot_row_ref[...] = rows[0:8, :].astype(jnp.int32)
        cols = rows.T
        slot_col_ref[...] = cols

    row = series_scr[pl.ds(step, 1), :]
    table_ref[0] = pltpu.roll(jnp.broadcast_to(row, (seq, seq)), 0, 1, stride=1, stride_axis=0) + mask_scr[...]

    @pl.when(step < 8)
    def _():
        slots = iota((per, seq), 0) + step * per
        hit0 = (slots == slot_row_ref[0:1, :]).astype(F32)
        hit1 = (slots == slot_row_ref[1:2, :]).astype(F32)
        cot_out_ref[...] = dot((hit0 + hit1).astype(BF16), cot_ref[...]).astype(BF16)
        first = jnp.broadcast_to(slot_row_ref[2:3, :].astype(F32), (8, seq)).astype(BF16)
        second = jnp.broadcast_to(slot_row_ref[3:4, :].astype(F32), (8, seq)).astype(BF16)
        other = dot_nt(second, hit0.astype(BF16)) + dot_nt(first, hit1.astype(BF16))
        other_ref[0] = other.astype(jnp.int32)


def prep(routes_t, segments, rev_buckets, rel_bias, cotangent, experts, capacity):
    seq, width = cotangent.shape
    heads = rel_bias.shape[1]
    buckets = rel_bias.shape[0]
    slots = experts * capacity
    per = slots // 8
    hp = -(-heads // 8) * 8
    bias_t = jnp.zeros((hp, buckets), F32).at[:heads].set(rel_bias.T)
    return call(
        functools.partial(prep_kernel, experts, capacity),
        [
            sds((heads, seq, seq), F32),
            sds((8, seq), jnp.int32),
            sds((seq, LANES), F32),
            sds((slots, width), BF16),
            sds((8, 8, per), jnp.int32),
        ],
        grid=(heads,),
        in_specs=[
            whole((2, seq)), whole((1, seq)), whole((seq, 1)), whole((1, seq)),
            whole((hp, buckets)), whole((seq, width)),
        ],
        out_specs=[
            pl.BlockSpec((1, seq, seq), lambda h: (h, 0, 0)),
            whole((8, seq)),
            whole((seq, LANES)),
            pl.BlockSpec((per, width), lambda h: (jnp.minimum(h, 7), 0)),
            pl.BlockSpec((1, 8, per), lambda h: (jnp.minimum(h, 7), 0, 0)),
        ],
        scratch_shapes=[
            pltpu.VMEM((seq, seq), F32),
            pltpu.VMEM((hp, seq), F32),
        ],
        flops=2 * slots * seq * width,
        moved=heads * seq * seq * 4 + 4 * seq * width,
        name="prep",
    )(routes_t, segments[None, :], segments[:, None], rev_buckets[None, :], bias_t, cotangent)


def pack_kernel(qkv_ref, proj_ref, router_ref, gain_a, gain_b, out_ref):
    rows, width = proj_ref.shape
    experts = router_ref.shape[0]
    out_ref[:, : 3 * width] = qkv_ref[...]
    out_ref[:, 3 * width : 4 * width] = proj_ref[...]
    place = iota((LANES, rows), 0)
    a = gain_a[...].astype(F32).reshape(1, rows)
    b = gain_b[...].astype(F32).reshape(1, rows)
    gains = jnp.where(place == experts, a, jnp.where(place == experts + 1, b, 0.0))
    if rows < LANES:
        gains = jnp.concatenate([gains, jnp.zeros((LANES, LANES - rows), F32)], axis=1)
    spread = (iota((experts, LANES), 0) == iota((experts, LANES), 1)).astype(BF16)
    out_ref[:, 4 * width :] = (dot_tn(router_ref[...], spread) + gains.T[:rows, :]).astype(BF16)


def pack_weights(qkv, proj, router, gain_a, gain_b):
    rows, width = proj.shape
    ins = (qkv, proj, router, gain_a, gain_b)
    return call(
        pack_kernel,
        sds((rows, 4 * width + LANES), BF16),
        grid=(1,),
        in_specs=[whole(x.shape) for x in ins],
        out_specs=whole((rows, 4 * width + LANES)),
        name="pack_weights",
    )(*ins)


def front_kernel(
    blocks, experts, me_ref, tokens_ref, table_ref, slot_row_ref, *refs,
):
    w_in = refs[:blocks]
    (q_ref, k_ref, v_ref, prob_ref, att_ref, res_ref, n1_ref, n2_ref, logit_ref,
     small_ref, small_t_ref) = refs[blocks : blocks + 11]
    qkv_ref, proj_ref = refs[-2:]
    sent_refs = refs[blocks + 11 : -2]
    step = pl.program_id(0)
    last = pl.num_programs(0) - 1
    seq, width = tokens_ref.shape
    rows = w_in[0].shape[0]
    scale = HEAD_DIM ** (-0.5)

    @pl.when(step == 0)
    def _():
        me = me_ref[0]
        for j in range(blocks):
            start = pl.multiple_of((me ^ j) * rows, rows) if blocks > 1 else 0
            qkv_ref[pl.ds(start, rows), :] = w_in[j][:, : 3 * width]
            proj_ref[pl.ds(start, rows), :] = w_in[j][:, 3 * width : 4 * width]
            small_ref[pl.ds(start, rows), :] = w_in[j][:, 4 * width :]
        small_t_ref[...] = small_ref[...].astype(F32).T
        x = tokens_ref[...].astype(F32)
        r = lax.rsqrt(jnp.mean(x * x, axis=-1, keepdims=True) + EPS)
        n1_ref[...] = (x * r * small_t_ref[experts : experts + 1, :]).astype(BF16)

    base = pl.multiple_of(step * GROUP, GROUP)
    n1 = n1_ref[...]
    q_ref[...] = dot(n1, qkv_ref[:, pl.ds(base, GROUP)]).astype(BF16)
    k_ref[...] = dot(n1, qkv_ref[:, pl.ds(width + base, GROUP)]).astype(BF16)
    v_ref[...] = dot(n1, qkv_ref[:, pl.ds(2 * width + base, GROUP)]).astype(BF16)

    half = seq // 2
    lane = iota((half, LANES), 1)
    for pair in range(GROUP // LANES):
        cols = slice(pair * LANES, (pair + 1) * LANES)
        for rb in range(2):
            span = (rb + 1) * half
            qrows = slice(rb * half, (rb + 1) * half)
            qp = q_ref[qrows, cols]
            kp = k_ref[:span, cols]
            vp = v_ref[:span, cols]
            mixed = []
            for parity in range(2):
                mine = (lane // HEAD_DIM) == parity
                qm = jnp.where(mine, qp, jnp.zeros_like(qp))
                s = dot_nt(qm, kp) * scale + table_ref[2 * pair + parity, qrows, :span]
                top = jnp.max(s, axis=-1, keepdims=True)
                e = jnp.exp(s - top)
                total = jnp.sum(e, axis=-1, keepdims=True)
                p = (e * (1.0 / total)).astype(BF16)
                mixed.append(dot(p, vp))
                prob_ref[2 * pair + parity, qrows, :span] = p
            at = pl.multiple_of(base + pair * LANES, LANES)
            att_ref[qrows, pl.ds(at, LANES)] = jnp.where(lane < HEAD_DIM, mixed[0], mixed[1]).astype(BF16)

    @pl.when(step == last)
    def _():
        x = tokens_ref[...].astype(F32) + dot(att_ref[...], proj_ref[...])
        res_ref[...] = x
        r = lax.rsqrt(jnp.mean(x * x, axis=-1, keepdims=True) + EPS)
        n2 = (x * r * small_t_ref[experts + 1 : experts + 2, :]).astype(BF16)
        n2_ref[...] = n2
        logit_ref[...] = dot(n2, small_ref[...])
        many = len(sent_refs) > 1
        per = sent_refs[0].shape[0] if many else sent_refs[0].shape[0] // 8
        for j in range(8):
            slots = iota((per, seq), 0) + ((me_ref[0] ^ j) * per if many else j * per)
            hit = (slots == slot_row_ref[0:1, :]) | (slots == slot_row_ref[1:2, :])
            rows_j = dot(hit.astype(BF16), n2).astype(BF16)
            if many:
                sent_refs[j][...] = rows_j
            else:
                sent_refs[0][j * per : (j + 1) * per, :] = rows_j


def front(me, tokens, table, slot_row, w_blocks, experts, slots):
    seq, width = tokens.shape
    blocks = len(w_blocks)
    groups = width // GROUP
    per_group = GROUP // HEAD_DIM
    col = pl.BlockSpec((seq, GROUP), lambda g: (0, g))
    return call(
        functools.partial(front_kernel, blocks, experts),
        [
            sds((seq, width), BF16), sds((seq, width), BF16), sds((seq, width), BF16),
            sds((width // HEAD_DIM, seq, seq), BF16), sds((seq, width), BF16), sds((seq, width), F32),
            sds((seq, width), BF16), sds((seq, width), BF16), sds((seq, LANES), F32),
            sds((width, LANES), BF16), sds((LANES, width), F32),
        ]
        + [sds((slots // blocks, width), BF16)] * blocks,
        grid=(groups,),
        in_specs=[
            smem(), whole((seq, width)),
            pl.BlockSpec((per_group, seq, seq), lambda g: (g, 0, 0)),
            whole((8, seq)),
        ]
        + [whole(b.shape) for b in w_blocks],
        out_specs=[
            col, col, col,
            pl.BlockSpec((per_group, seq, seq), lambda g: (g, 0, 0)), whole((seq, width)), whole((seq, width)),
            whole((seq, width)), whole((seq, width)), whole((seq, LANES)),
            whole((width, LANES)), whole((LANES, width)),
        ]
        + [whole((slots // blocks, width))] * blocks,
        scratch_shapes=[pltpu.VMEM((width, 3 * width), BF16), pltpu.VMEM((width, width), BF16)],
        flops=2 * seq * width * width * 4 + 2 * slots * seq * width + 8 * seq * seq * width,
        moved=30_000_000,
        name="front",
    )(me, tokens, table, slot_row, *w_blocks)


def assemble_kernel(blocks, me_ref, *refs):
    qkv_ref, proj_ref = refs[-2:]
    wide = qkv_ref.shape[1]
    high = proj_ref.shape[1]
    for j in range(blocks):
        rows = refs[j].shape[0]
        start = pl.multiple_of((me_ref[0] ^ j) * rows, rows) if blocks > 1 else 0
        qkv_ref[pl.ds(start, rows), :] = refs[j][:, :wide]
        proj_ref[pl.ds(start, rows), :] = refs[j][:, wide : wide + high]


def assemble(me, w_blocks, width):
    return call(
        functools.partial(assemble_kernel, len(w_blocks)),
        [sds((width, 3 * width), BF16), sds((width, width), BF16)],
        grid=(1,),
        in_specs=[smem()] + [whole(b.shape) for b in w_blocks],
        out_specs=[whole((width, 3 * width)), whole((width, width))],
        name="assemble",
    )(me, *w_blocks)


def gelu_parts(v):
    size = jnp.abs(v) * (2.0 ** -0.5)
    t = 1.0 / (1.0 + 0.3275911 * size)
    bell = jnp.exp(-0.5 * v * v)
    poly = t * (
        0.5 * 0.254829592
        + t * (0.5 * -0.284496736 + t * (0.5 * 1.421413741 + t * (0.5 * -1.453152027 + t * (0.5 * 1.061405429))))
    )
    tail = poly * bell
    below = jnp.where(v < 0, tail, 1.0 - tail)
    return v * below, below + v * bell * (1.0 / math.sqrt(2.0 * math.pi))


def join_rows(blocks, rows_ref):
    per = blocks[0].shape[0]
    for j, block in enumerate(blocks):
        rows_ref[j * per : (j + 1) * per, :] = block[...]


def gated_rows(me, parts, rows_ref, cot_ref, other_ref, small_ref, sg_ref):
    total, width = rows_ref.shape
    tile = total // 8
    for j in range(8):
        here = slice(j * tile, (j + 1) * tile)
        there = pl.ds(pl.multiple_of((me ^ j) * tile, tile), tile) if parts > 1 else here
        logits = dot(rows_ref[here, :], small_ref[...])
        lane = iota((tile, LANES), 1)
        line = other_ref[pl.ds(me ^ j if parts > 1 else j, 1), :].astype(F32)
        fill = -tile % LANES
        if fill:
            line = jnp.concatenate([line, jnp.zeros((1, fill), F32)], axis=1)
        other_id = jnp.broadcast_to(line, (8, tile + fill)).T[:tile, 0:1].astype(jnp.int32)
        own = jnp.sum(jnp.where(lane == me, logits, 0.0), axis=1, keepdims=True)
        other = jnp.sum(jnp.where(lane == other_id, logits, 0.0), axis=1, keepdims=True)
        top = jnp.maximum(own, other)
        a, b = jnp.exp(own - top), jnp.exp(other - top)
        gate = a / (a + b)
        sg_ref[here, :] = (gate * cot_ref[there, :].astype(F32)).astype(BF16)


def expert_acts(w1, w2, rows_ref, sg_ref, act_ref, gp_ref, d_ref, tile):
    for at in range(0, rows_ref.shape[0], tile):
        here = slice(at, at + tile)
        pre = dot(rows_ref[here, :], w1)
        ga = dot_nt(sg_ref[here, :], w2)
        act, slope = gelu_parts(pre)
        low = act.astype(BF16)
        act_ref[here, :] = low
        gp_ref[here, :] = (ga * slope).astype(BF16)
        d_ref[here, :] += jnp.sum(low.astype(F32) * ga, axis=1, keepdims=True)


def expert_weights(rows_t, sg_t, act_ref, gp_ref, buf_ref, cb, pair, ranks):
    width = rows_t.shape[0]
    block = BLOCK
    part = width // ranks
    piece = block // ranks
    gwin = dot(rows_t[...], gp_ref[...]).astype(BF16)
    lane0 = pl.multiple_of(pair * 2 * block, block)
    for dest in range(ranks):
        buf_ref[dest, cb, 0:part, pl.ds(lane0, 2 * block)] = gwin[dest * part : (dest + 1) * part, :]
    gwout = dot(sg_t[...], act_ref[...]).T.astype(BF16)
    for half in range(2):
        rank = 2 * pair + half
        for i in range(ranks):
            for j in range(width // block):
                buf_ref[rank, cb, part + j * piece : part + (j + 1) * piece, i * block : (i + 1) * block] = gwout[
                    half * block + i * piece : half * block + (i + 1) * piece, j * block : (j + 1) * block
                ]


def expert_first_kernel(
    ranks, tile, parts, me_ref, cot_ref, other_ref, small_ref, w1a, w1b, w2a, w2b, *refs,
):
    blocks = refs[:parts]
    act_ref, gp_ref, d_ref, buf_ref, sg_ref, rows_t, sg_t, rows_ref = refs[parts:]
    step = pl.program_id(0)

    @pl.when(step == 0)
    def _():
        join_rows(blocks, rows_ref)
        gated_rows(me_ref[0], parts, rows_ref, cot_ref, other_ref, small_ref, sg_ref)
        rows_t[...] = rows_ref[...].T
        sg_t[...] = sg_ref[...].T
        d_ref[...] = jnp.zeros_like(d_ref)

    w1 = jnp.concatenate([w1a[...], w1b[...]], axis=1)
    w2 = jnp.concatenate([w2a[...], w2b[...]], axis=0)
    expert_acts(w1, w2, rows_ref, sg_ref, act_ref, gp_ref, d_ref, tile)
    expert_weights(rows_t, sg_t, act_ref, gp_ref, buf_ref, 0, step, ranks)


def expert_rest_kernel(
    ranks, per_rank, start, tile, parts, me_ref, sg_ref, win_ref, w2a, w2b, gp0_ref, d0_ref, *refs,
):
    blocks = refs[:parts]
    act_ref, gp_ref, back_ref, side_ref = refs[parts : parts + 4]
    gp_scr, d_scr, rows_ref = refs[-3:]
    step = pl.program_id(0)
    total, width = rows_ref.shape
    block = BLOCK

    @pl.when(step == 0)
    def _():
        join_rows(blocks, rows_ref)
        d_scr[...] = d0_ref[...]
        for c in range(start):
            for r in range(ranks):
                to = (r * per_rank + c) * block
                gp_scr[:, to : to + block] = gp0_ref[:, (c * ranks + r) * block : (c * ranks + r + 1) * block]

    pairs = ranks // 2
    cb, pair = lax.div(step, pairs), lax.rem(step, pairs)
    at_a = pl.multiple_of((2 * pair * per_rank + start + cb) * block, block)
    at_b = pl.multiple_of(((2 * pair + 1) * per_rank + start + cb) * block, block)
    w1 = jnp.concatenate([win_ref[:, pl.ds(at_a, block)], win_ref[:, pl.ds(at_b, block)]], axis=1)
    w2 = jnp.concatenate([w2a[...], w2b[...]], axis=0)
    expert_acts(w1, w2, rows_ref, sg_ref, act_ref, gp_ref, d_scr, tile)
    gp_scr[:, pl.ds(at_a, block)] = gp_ref[:, :block]
    gp_scr[:, pl.ds(at_b, block)] = gp_ref[:, block:]

    @pl.when(step == pl.num_programs(0) - 1)
    def _():
        per = total // 8
        join = 2
        for at in range(0, 8, join):
            here = slice(at * per, (at + join) * per)
            back = dot_nt(gp_scr[here, :], win_ref[...]).astype(BF16)
            d = d_scr[here, :]
            high = d.astype(BF16).astype(F32)
            lane = iota(d.shape, 1)
            side = jnp.where(lane == 0, high, jnp.where(lane == 1, d - high, 0.0)).astype(BF16)
            for i in range(join):
                inner = slice(i * per, (i + 1) * per)
                if parts > 1:
                    to = pl.ds(pl.multiple_of((me_ref[0] ^ (at + i)) * per, per), per)
                else:
                    to = slice((at + i) * per, (at + i + 1) * per)
                back_ref[to, :] = back[inner, :NEAR]
                side_ref[to, : width - NEAR] = back[inner, NEAR:]
                side_ref[to, width - NEAR :] = side[inner, :]


def expert_weights_kernel(ranks, parts, sg_ref, act_ref, gp_ref, *refs):
    blocks = refs[:parts]
    buf_ref, rows_t, sg_t = refs[parts:]
    step = pl.program_id(0)
    pairs = ranks // 2
    per = blocks[0].shape[0]

    @pl.when(step == 0)
    def _():
        if per % LANES and parts > 1:
            for j in range(0, parts, 2):
                pair = jnp.concatenate([blocks[j][...], blocks[j + 1][...]], axis=0)
                rows_t[:, j * per : (j + 2) * per] = pair.T
        else:
            for j, block in enumerate(blocks):
                rows_t[:, j * per : (j + 1) * per] = block[...].T
        sg_t[...] = sg_ref[...].T

    expert_weights(rows_t, sg_t, act_ref, gp_ref, buf_ref, lax.div(step, pairs), lax.rem(step, pairs), ranks)


def expert_weight_grads(blocks, sg, act, gp, hidden, ranks):
    total, width = sg.shape
    high, wide, per_rank = expert_sizes(width, hidden, ranks)
    count = act.shape[1] // wide
    buf = (ranks, count, high, wide)
    col = pl.BlockSpec((total, 2 * BLOCK), lambda s: (0, s))
    return call(
        functools.partial(expert_weights_kernel, ranks, len(blocks)),
        sds(buf, BF16),
        grid=(count * ranks // 2,),
        in_specs=[once((total, width)), col, col] + [once(b.shape) for b in blocks],
        out_specs=whole(buf),
        scratch_shapes=[pltpu.VMEM((width, total), BF16), pltpu.VMEM((width, total), BF16)],
        flops=4 * total * width * wide * count,
        moved=20_000_000,
        name="experts_weights",
    )(sg, act, gp, *blocks)


def once(shape):
    rank = len(shape)
    return pl.BlockSpec(shape, lambda *_: (0,) * rank, pipeline_mode=pl.Buffered(1))


def expert_sizes(width, hidden, ranks):
    high = width // ranks + (width // BLOCK) * (BLOCK // ranks)
    return high, ranks * BLOCK, hidden // ranks // BLOCK


def expert_first(me, blocks, cot, other, small, win, wout, ranks):
    total = cot.shape[0]
    width, hidden = win.shape
    high, wide, per_rank = expert_sizes(width, hidden, ranks)
    buf = (ranks, 1, high, wide)
    col = pl.BlockSpec((total, 2 * BLOCK), lambda s: (0, s))

    def win_spec(half):
        return pl.BlockSpec((width, BLOCK), lambda s: (0, (2 * s + half) * per_rank))

    def wout_spec(half):
        return pl.BlockSpec((BLOCK, width), lambda s: ((2 * s + half) * per_rank, 0))

    return call(
        functools.partial(expert_first_kernel, ranks, 256, len(blocks)),
        [
            sds((total, wide), BF16), sds((total, wide), BF16), sds((total, LANES), F32), sds(buf, BF16),
            sds((total, width), BF16),
        ],
        grid=(ranks // 2,),
        in_specs=[
            smem(), once((total, width)), once(other.shape), once((width, LANES)),
            win_spec(0), win_spec(1), wout_spec(0), wout_spec(1),
        ]
        + [once(b.shape) for b in blocks],
        out_specs=[
            col, col, whole((total, LANES)), whole(buf), whole((total, width)),
        ],
        scratch_shapes=[
            pltpu.VMEM((width, total), BF16), pltpu.VMEM((width, total), BF16), pltpu.VMEM((total, width), BF16),
        ],
        flops=8 * total * width * wide,
        moved=20_000_000,
        name="experts_first",
    )(me, cot, other, small, win, win, wout, wout, *blocks)


def expert_rest(me, blocks, sg, win, wout, gp0, d0, ranks):
    total, width = sg.shape
    hidden = win.shape[1]
    high, wide, per_rank = expert_sizes(width, hidden, ranks)
    start = 1
    count = per_rank - start
    pairs = ranks // 2
    parts = len(blocks)
    col = pl.BlockSpec((total, 2 * BLOCK), lambda s: (0, s))
    out_near, out_far = (total, NEAR), (total, width + LANES - NEAR)

    def wout_spec(half):
        return pl.BlockSpec(
            (BLOCK, width), lambda s: ((2 * lax.rem(s, pairs) + half) * per_rank + start + lax.div(s, pairs), 0)
        )

    return call(
        functools.partial(expert_rest_kernel, ranks, per_rank, start, 256, parts),
        [sds((total, count * wide), BF16), sds((total, count * wide), BF16)]
        + [sds(out_near, BF16), sds(out_far, BF16)],
        grid=(count * pairs,),
        in_specs=[
            smem(), once((total, width)), once((width, hidden)), wout_spec(0), wout_spec(1),
            once((total, start * wide)), once((total, LANES)),
        ]
        + [once(b.shape) for b in blocks],
        out_specs=[col, col, whole(out_near), whole(out_far)],
        scratch_shapes=[
            pltpu.VMEM((total, hidden), BF16), pltpu.VMEM((total, LANES), F32), pltpu.VMEM((total, width), BF16),
        ],
        flops=4 * total * width * wide * count + 2 * total * width * hidden,
        moved=30_000_000,
        name="experts_rest",
    )(me, sg, win, wout, wout, gp0, d0, *blocks)


def expert_rows_kernel(ranks, per_rank, parts, count, me_ref, *refs):
    acts, w_ref, o_ref, w_scr = refs[:count], refs[count], refs[count + 1], refs[count + 2]

    @pl.when(pl.program_id(0) == 0)
    def _():
        for c in range(per_rank):
            for r in range(ranks):
                to, src = (c * ranks + r) * BLOCK, (r * per_rank + c) * BLOCK
                w_scr[to : to + BLOCK, :] = w_ref[src : src + BLOCK, :]

    at, total = 0, None
    for act in acts:
        wide = act.shape[1]
        more = dot(act[...], w_scr[at : at + wide, :])
        total = more if total is None else total + more
        at += wide
    low = total.astype(BF16)
    if parts == 1:
        o_ref[...] = low
    else:
        per = low.shape[0] // 2
        flip = me_ref[0] % 2
        o_ref[pl.ds(pl.multiple_of(flip * per, per), per), :] = low[:per, :]
        o_ref[pl.ds(pl.multiple_of((1 - flip) * per, per), per), :] = low[per:, :]


def expert_rows(me, acts, wout, parts, ranks):
    total = acts[0].shape[0]
    hidden, width = wout.shape
    tile = total // 4

    def place(i, m):
        return ((m[0] // 2) ^ i if parts > 1 else i, 0)

    return pl.pallas_call(
        functools.partial(expert_rows_kernel, ranks, hidden // ranks // BLOCK, parts, len(acts)),
        sds((total, width), BF16),
        grid_spec=pltpu.PrefetchScalarGridSpec(
            num_scalar_prefetch=1,
            grid=(4,),
            in_specs=[pl.BlockSpec((tile, a.shape[1]), lambda i, m: (i, 0)) for a in acts] + [once(wout.shape)],
            out_specs=pl.BlockSpec((tile, width), place),
            scratch_shapes=[pltpu.VMEM(wout.shape, BF16)],
        ),
        compiler_params=pltpu.CompilerParams(vmem_limit_bytes=VMEM_LIMIT),
        name="expert_rows",
    )(me, *acts, wout)


def norm_back(x, grad, gain):
    r = lax.rsqrt(jnp.mean(x * x, axis=-1, keepdims=True) + EPS)
    u = grad * gain
    inner = jnp.mean(u * x, axis=-1, keepdims=True)
    xr = x * r
    return r * u - (r * r * r) * x * inner, jnp.sum(grad * xr, axis=0, keepdims=True)


def pair_gates(slot_ref, logit_ref):
    logits = logit_ref[...]
    lane = iota(logits.shape, 1)
    hot0 = lane == slot_ref[:, 2:3].astype(jnp.int32)
    hot1 = lane == slot_ref[:, 3:4].astype(jnp.int32)
    c0 = jnp.sum(jnp.where(hot0, logits, 0.0), axis=1, keepdims=True)
    c1 = jnp.sum(jnp.where(hot1, logits, 0.0), axis=1, keepdims=True)
    top = jnp.maximum(c0, c1)
    e0, e1 = jnp.exp(c0 - top), jnp.exp(c1 - top)
    return e0 / (e0 + e1), e1 / (e0 + e1), hot0, hot1


def pair_hits(slot_ref, slots):
    spot = iota((slot_ref.shape[0], slots), 1)
    h0 = (spot == slot_ref[:, 0:1].astype(jnp.int32)).astype(BF16)
    h1 = (spot == slot_ref[:, 1:2].astype(jnp.int32)).astype(BF16)
    return h0, h1


def output_kernel(ret_ref, slot_ref, res_ref, logit_ref, out_ref):
    h0, h1 = pair_hits(slot_ref, ret_ref.shape[0])
    g0, g1, _, _ = pair_gates(slot_ref, logit_ref)
    ret = ret_ref[...]
    out_ref[...] = (res_ref[...] + (g0 * dot(h0, ret) + g1 * dot(h1, ret))).astype(BF16)


def output_rows(returned, slot_col, res, logits):
    ins = (returned, slot_col, res, logits)
    return call(
        output_kernel,
        sds(res.shape, BF16),
        grid=(1,),
        in_specs=[whole(x.shape) for x in ins],
        out_specs=whole(res.shape),
        flops=4 * returned.shape[0] * res.size,
        moved=6_000_000,
        name="output_rows",
    )(*ins)


def heads_back(prob_ref, q_ref, k_ref, v_ref, gatt_ref, g_scr, diag_ref):
    seq = q_ref.shape[0]
    half = seq // 2
    scale = HEAD_DIM ** (-0.5)
    lane = iota((half, LANES), 1)
    full_lane = iota((seq, LANES), 1)
    for pair in range(GROUP // LANES):
        cols = slice(pair * LANES, (pair + 1) * LANES)
        dk = [jnp.zeros((seq, LANES), F32)] * 2
        dv = [jnp.zeros((seq, LANES), F32)] * 2
        skew = [jnp.zeros((LANES, seq), F32)] * 2
        for rb in range(2):
            span = (rb + 1) * half
            qrows = slice(rb * half, (rb + 1) * half)
            qp = q_ref[qrows, cols]
            gp = gatt_ref[qrows, cols]
            kp = k_ref[:span, cols]
            vp = v_ref[:span, cols]
            dq = []
            for parity in range(2):
                mine = (lane // HEAD_DIM) == parity
                gm = jnp.where(mine, gp, jnp.zeros_like(gp))
                low_p = prob_ref[2 * pair + parity, qrows, :span]
                p = low_p.astype(F32)
                dp = dot_nt(gm, vp)
                d = jnp.sum(p * dp, axis=1, keepdims=True)
                ds = p * (dp - d)
                low = ds.astype(BF16)
                dq.append(dot(low, kp) * scale)
                add_k = dot_tn(low, qp) * scale
                add_v = dot_tn(low_p, gp)
                if span < seq:
                    zero = jnp.zeros((seq - span, LANES), F32)
                    add_k = jnp.concatenate([add_k, zero], axis=0)
                    add_v = jnp.concatenate([add_v, zero], axis=0)
                dk[parity] = dk[parity] + add_k
                dv[parity] = dv[parity] + add_v
                wide = low.astype(F32)
                if span < seq:
                    wide = jnp.concatenate([wide, jnp.zeros((half, seq - span), F32)], axis=1)
                for b in range(half // LANES):
                    shift = rb * half + b * LANES
                    rows = wide[b * LANES : (b + 1) * LANES, :]
                    if shift:
                        rows = jnp.concatenate([rows[:, shift:], rows[:, :shift]], axis=1)
                    skew[parity] = skew[parity] + rows
            g_scr[0, qrows, cols] = jnp.where(lane < HEAD_DIM, dq[0], dq[1]).astype(BF16)
        g_scr[1, :, cols] = jnp.where(full_lane < HEAD_DIM, dk[0], dk[1]).astype(BF16)
        g_scr[2, :, cols] = jnp.where(full_lane < HEAD_DIM, dv[0], dv[1]).astype(BF16)
        for parity in range(2):
            acc = skew[parity][0:8, :]
            for i in range(1, LANES // 8):
                acc = acc + pltpu.roll(skew[parity][i * 8 : (i + 1) * 8, :], seq - i * 8, 1)
            at = 8 * (2 * pair + parity)
            diag_ref[at : at + 8, :] = acc


class Parted:
    def __init__(self, size, rows, refs, scratch):
        self.size, self.rows, self.refs, self.scratch = size, rows, refs, scratch

    def put(self, core, value, lanes):
        if self.size != 8:
            self.refs[0][:, lanes] = value
            return
        for b in range(8):
            self.scratch[(b % 2) ^ core, b // 2, :, lanes] = value[b * self.rows : (b + 1) * self.rows, :]

    def done(self):
        if self.size == 8:
            self.refs[0][...] = self.scratch[0]
            self.refs[1][...] = self.scratch[1]


def parted_shapes(size, rows, width, wide):
    if size != 8:
        return [(width, wide)], []
    return [(4, rows, wide)] * 2, [pltpu.VMEM((2, 4, rows, wide), BF16)]


def weights_back(group_at, n1_ref, g_scr, w_refs, core, parted):
    acc = None
    for i, w_ref in enumerate(w_refs):
        g = g_scr[i]
        at = group_at + i * GROUP
        if not isinstance(at, int):
            at = pl.multiple_of(at, GROUP)
        parted.put(core, dot_tn(n1_ref[...], g).astype(BF16), pl.ds(at, GROUP))
        more = dot_nt(g, w_ref[...])
        acc = more if acc is None else acc + more
    return acc


def token_kernel(
    experts, size, own_rows, outs, parts_in, me_ref, slot_ref, res_ref, logit_ref, cot_ref, n2_ref, att_ref,
    proj_ref, small_ref, small_t_ref, prob_ref, q_ref, k_ref, v_ref, n1_ref, wq_ref, wk_ref, wv_ref, *refs,
):
    blocks, refs = refs[:parts_in], refs[parts_in:]
    gres_ref, gatt_ref, acc_ref, diag_ref = refs[:4]
    parts = refs[4 : 4 + outs]
    g_scr, gatt_scr, back_ref = refs[4 + outs : 7 + outs]
    parted = Parted(size, own_rows, parts, refs[7 + outs] if size == 8 else None)
    step = pl.program_id(0)
    seq, width = res_ref.shape
    core = me_ref[0] % 2
    groups = width // GROUP
    extra = (groups - 1) * 3 * GROUP

    @pl.when(step == 0)
    def _():
        at = 0
        for block in blocks:
            back_ref[:, at : at + block.shape[1]] = block[...]
            at += block.shape[1]
        h0, h1 = pair_hits(slot_ref, back_ref.shape[0])
        g0, g1, hot0, hot1 = pair_gates(slot_ref, logit_ref)
        back = back_ref[:, :width]
        sides = back_ref[:, width:]
        d0 = jnp.sum(dot(h0, sides), axis=1, keepdims=True)
        d1 = jnp.sum(dot(h1, sides), axis=1, keepdims=True)
        glog = jnp.where(hot0, d0 - g0 * (d0 + d1), 0.0) + jnp.where(hot1, d1 - g1 * (d0 + d1), 0.0)
        glog = glog.astype(BF16)
        x = res_ref[...]
        small = small_ref[...]
        router = jnp.where(iota((width, LANES), 1) < experts, small, jnp.zeros_like(small))
        grad = dot(h0 + h1, back) + dot_nt(glog, router)
        gx, ggain = norm_back(x, grad, small_t_ref[experts + 1 : experts + 2, :])
        gres = gx + cot_ref[...].astype(F32)
        gres_ref[...] = gres
        branch = gres.astype(BF16)
        gatt = dot_nt(branch, proj_ref[...]).astype(BF16)
        for g in range(groups):
            gatt_scr[g] = gatt[:, g * GROUP : (g + 1) * GROUP]
        gatt_ref[...] = gatt[:, (groups - 1) * GROUP :]
        parted.put(core, dot_tn(att_ref[...], branch).astype(BF16), slice(extra, extra + width))
        gain_rows = jnp.where(iota((LANES, width), 0) == experts + 1, ggain, 0.0)
        more = (dot_tn(n2_ref[...], glog) + gain_rows.T).astype(BF16)
        parted.put(core, more, slice(extra + width, extra + width + LANES))

    @pl.when(step > 0)
    def _():
        group = step - 1
        heads_back(prob_ref, q_ref, k_ref, v_ref, gatt_scr.at[group], g_scr, diag_ref)
        more = weights_back(group * 3 * GROUP, n1_ref, g_scr, (wq_ref, wk_ref, wv_ref), core, parted)

        @pl.when(step == 1)
        def _():
            acc_ref[...] = more

        @pl.when(step > 1)
        def _():
            acc_ref[...] += more

    @pl.when(step == pl.num_programs(0) - 1)
    def _():
        parted.done()


def token_side(
    experts, size, own_rows, me, back, slot_col, res, logits, cot, n2, att, proj, small, small_t,
    probs, q, k, v, n1, qkv,
):
    seq, width = res.shape
    groups = width // GROUP
    per_group = GROUP // HEAD_DIM
    wide = (groups - 1) * 3 * GROUP + width + LANES
    shapes, scratch = parted_shapes(size, own_rows, width, wide)

    def at(s):
        return jnp.maximum(s - 1, 0)

    col = pl.BlockSpec((seq, GROUP), lambda s: (0, at(s)))

    def wcol(i):
        return pl.BlockSpec((width, GROUP), lambda s: (0, i * groups + at(s)))

    first = (slot_col, res, logits, cot, n2, att, proj, small, small_t)
    return call(
        functools.partial(token_kernel, experts, size, own_rows, len(shapes), len(back)),
        [
            sds((seq, width), F32), sds((seq, GROUP), BF16), sds((seq, width), F32),
            sds(((groups - 1) * 8 * per_group, seq), F32),
        ]
        + [sds(x, BF16) for x in shapes],
        grid=(groups,),
        in_specs=[smem()] + [once(a.shape) for a in first]
        + [pl.BlockSpec((per_group, seq, seq), lambda s: (at(s), 0, 0)), col, col, col]
        + [once((seq, width)), wcol(0), wcol(1), wcol(2)]
        + [once(b.shape) for b in back],
        out_specs=[
            whole((seq, width)), whole((seq, GROUP)), whole((seq, width)),
            pl.BlockSpec((8 * per_group, seq), lambda s: (at(s), 0)),
        ]
        + [whole(x) for x in shapes],
        scratch_shapes=[
            pltpu.VMEM((3, seq, GROUP), BF16), pltpu.VMEM((groups, seq, GROUP), BF16),
            pltpu.VMEM((back[0].shape[0], width + LANES), BF16),
        ]
        + scratch,
        flops=3072 * seq * width + 12 * seq * width * width + 14 * seq * seq * width,
        moved=30_000_000,
        name="token_side",
    )(me, *first, probs, q, k, v, n1, qkv, qkv, qkv, *back)


def tail_kernel(
    experts, size, own_rows, outs, me_ref, prob_ref, q_ref, k_ref, v_ref, gatt_ref, n1_ref,
    wq_ref, wk_ref, wv_ref, acc_ref, diag_in, tokens_ref, gres_ref, small_t_ref, rev_ref, gtok_ref, *refs,
):
    parts = refs[:outs]
    g_scr, diag_scr = refs[outs : outs + 2]
    parted = Parted(size, own_rows, parts, refs[outs + 2] if size == 8 else None)
    seq, width = tokens_ref.shape
    core = me_ref[0] % 2
    heads_back(prob_ref, q_ref, k_ref, v_ref, gatt_ref, g_scr, diag_scr)
    acc = acc_ref[...] + weights_back(0, n1_ref, g_scr, (wq_ref, wk_ref, wv_ref), core, parted)
    x = tokens_ref[...].astype(F32)
    gx, ggain = norm_back(x, acc, small_t_ref[experts : experts + 1, :])
    gtok_ref[...] = (gx + gres_ref[...]).astype(BF16)
    gain_rows = jnp.where(iota((LANES, width), 0) == experts, ggain, 0.0)
    diag = jnp.concatenate([diag_in[...], diag_scr[...]], axis=0)
    count = diag.shape[0]
    place = lax.rem(iota((count, seq), 0), 8)
    total = jnp.where(place == 0, diag, 0.0)
    for r in range(1, 8):
        total = total + jnp.where(place == r, pltpu.roll(diag, seq - r, 1), 0.0)
    hot = (iota((LANES, seq), 0) - (experts + 2) == rev_ref[...]).astype(F32)
    per_row = lax.dot_general(
        total, hot, (((1,), (1,)), ((), ())), precision=lax.Precision.HIGHEST, preferred_element_type=F32
    )
    copies = (lax.rem(iota((width, count), 0), own_rows) == lax.div(iota((width, count), 1), 8)).astype(F32)
    spread = jnp.dot(copies, per_row, precision=lax.Precision.HIGHEST, preferred_element_type=F32)
    parted.put(core, (gain_rows.T + spread).astype(BF16), slice(3 * GROUP, 3 * GROUP + LANES))
    parted.done()


def tail(experts, size, own_rows, me, probs, q, k, v, gatt, n1, qkv, acc, diag, tokens, gres, small_t, rev_buckets):
    seq, width = n1.shape
    groups = width // GROUP
    group = groups - 1
    per_group = GROUP // HEAD_DIM
    col = pl.BlockSpec((seq, GROUP), lambda _: (0, group))
    shapes, scratch = parted_shapes(size, own_rows, width, 3 * GROUP + LANES)

    def wcol(i):
        return pl.BlockSpec((width, GROUP), lambda _: (0, i * groups + group))

    rest = (acc, diag, tokens, gres, small_t, rev_buckets[None, :])
    return call(
        functools.partial(tail_kernel, experts, size, own_rows, len(shapes)),
        [sds((seq, width), BF16)] + [sds(x, BF16) for x in shapes],
        grid=(1,),
        in_specs=[
            smem(), pl.BlockSpec((per_group, seq, seq), lambda _: (group, 0, 0)),
            col, col, col, whole((seq, GROUP)),
            whole((seq, width)),
            wcol(0), wcol(1), wcol(2),
        ]
        + [whole(x.shape) for x in rest],
        out_specs=[whole((seq, width))] + [whole(x) for x in shapes],
        scratch_shapes=[pltpu.VMEM((3, seq, GROUP), BF16), pltpu.VMEM((8 * per_group, seq), F32)] + scratch,
        flops=4 * seq * width * width + 7 * seq * seq * width,
        moved=10_000_000,
        name="tail",
    )(me, probs, q, k, v, gatt, n1, qkv, qkv, qkv, *rest)


def swap(value, mask, size):
    return lax.ppermute(value, "shard", [(i, i ^ mask) for i in range(size)])


def gather_blocks(value, size, beside):
    if size != 8:
        return [lax.all_gather(value, "shard", axis=0, tiled=True)], beside
    one, six, two, four = (swap(value, j, size) for j in (1, 6, 2, 4))
    one, six, two, four, *beside = lax.optimization_barrier((one, six, two, four, *beside))
    far = {0: value, 1: one, 6: six, 2: two, 4: four}
    near = {j ^ 1: swap(far[j], 1, size) for j in (6, 2, 4)}
    return [far[j] if j in far else near[j] for j in range(8)], beside


def tie(*values):
    return lax.optimization_barrier(values)


def across(value, mask, ranks):
    return lax.ppermute(value, "rep", [(i, i ^ mask) for i in range(ranks)])


def add(*values):
    total = values[0].astype(F32)
    for value in values[1:]:
        total = total + value.astype(F32)
    return total.astype(BF16)


def spread_kernel(terms, rank_ref, *refs):
    outs, total = refs[terms:-1], refs[-1]
    value = refs[0][...].astype(F32)
    for ref in refs[1:terms]:
        value = value + ref[...].astype(F32)
    wide = value.shape[1]
    total[:, :wide] = value
    if total.shape[1] > wide:
        total[:, wide:] = jnp.zeros((value.shape[0], total.shape[1] - wide), F32)
    part = outs[0].shape[1]
    for j, out in enumerate(outs):
        at = pl.multiple_of((rank_ref[0] ^ j) * part, LANES)
        out[...] = total[:, pl.ds(at, part)].astype(BF16)


def line_total(terms, rank, ranks):
    rows, wide = terms[0].shape
    part = -(-wide // (ranks * LANES)) * LANES
    parts = call(
        functools.partial(spread_kernel, len(terms)),
        [sds((rows, part), BF16)] * ranks,
        grid=(1,),
        in_specs=[smem()] + [whole((rows, wide))] * len(terms),
        out_specs=[whole((rows, part))] * ranks,
        scratch_shapes=[pltpu.VMEM((rows, part * ranks), F32)],
        name="spread",
    )(rank, *terms)
    own = add(parts[0], *[across(parts[j], j, ranks) for j in range(1, ranks)])
    return [own] + [across(own, j, ranks) for j in range(1, ranks)]


def finish_kernel(width, src_ref, *refs):
    in_ref, out_ref = refs[-2:]
    total = src_ref[0].astype(F32)
    part, block = in_ref.shape
    piece = out_ref.shape[0]
    in_ref[...] = total[:part, :]
    for j in range(width // block):
        out_ref[:, j * block : (j + 1) * block] = total[part + j * piece : part + (j + 1) * piece, :]


def finish(src, start, earlier, width, hidden, ranks):
    count, high, wide = src.shape
    block = wide // ranks
    part = width // ranks
    piece = block // ranks
    per_rank = hidden // ranks // block
    return call(
        functools.partial(finish_kernel, width),
        [sds((part, hidden), F32), sds((hidden // ranks, width), F32)],
        grid=(count, ranks),
        in_specs=[pl.BlockSpec((1, high, block), lambda c, r: (c, 0, r))]
        + [pl.BlockSpec(memory_space=pl.ANY)] * len(earlier),
        out_specs=[
            pl.BlockSpec((part, block), lambda c, r: (0, r * per_rank + start + c)),
            pl.BlockSpec((piece, width), lambda c, r: ((start + c) * ranks + r, 0)),
        ],
        input_output_aliases={1: 0, 2: 1} if earlier else {},
        name="finish",
    )(src, *earlier)


def pick_kernel(chip_ref, keep_ref, got_ref, six_ref, two_ref, four_ref, own_ref):
    chip = chip_ref[0]
    for ref, other in ((six_ref, 3), (two_ref, 1), (four_ref, 2), (own_ref, 0)):
        at = chip ^ other
        ref[...] = (keep_ref[at].astype(F32) + got_ref[at].astype(F32)).astype(BF16)


def core_sum(parts, me, size):
    if size != 8:
        return [parts[0]]
    keep, send = parts
    got = swap(send, 1, size)
    block = keep.shape[1:]
    return call(
        pick_kernel,
        [sds(block, BF16)] * 4,
        grid=(1,),
        in_specs=[smem(), whole(keep.shape), whole(keep.shape)],
        out_specs=[whole(block)] * 4,
        name="pick",
    )((me // 2).reshape(1), keep, got)


def chips_sum(blocks, size):
    if size != 8:
        return [lax.psum_scatter(blocks[0], "shard", scatter_dimension=0, tiled=True)]
    return [blocks[3]] + [swap(block, j, size) for block, j in zip(blocks, (6, 2, 4))]


def layout_kernel(width, experts, ranks, rank_ref, *refs):
    a_parts, b_parts = refs[:ranks], refs[ranks : 2 * ranks]
    qkv_ref, proj_ref, router_ref, gain_a, gain_b, bias_ref, a, b = refs[2 * ranks :]
    for parts, total in ((a_parts, a), (b_parts, b)):
        part = parts[0].shape[1]
        for j, ref in enumerate(parts):
            at = pl.multiple_of((rank_ref[0] ^ j) * part, LANES)
            total[:, pl.ds(at, part)] = ref[...].astype(F32)
    groups = width // GROUP
    for g in range(groups):
        src, base = (a, g * 3 * GROUP) if g < groups - 1 else (b, 0)
        for i in range(3):
            qkv_ref[:, i * width + g * GROUP : i * width + (g + 1) * GROUP] = src[:, base + i * GROUP : base + (i + 1) * GROUP]
    extra = (groups - 1) * 3 * GROUP
    proj_ref[...] = a[:, extra : extra + width]
    small_a = a[:, extra + width : extra + width + LANES]
    small_b = b[:, 3 * GROUP : 3 * GROUP + LANES]
    rows = small_a.shape[0]
    pad = jnp.zeros((LANES - rows, LANES), F32)
    turned_a = jnp.concatenate([small_a, pad], axis=0).T
    turned_b = jnp.concatenate([small_b, pad], axis=0).T
    router_ref[...] = turned_a[:experts, :rows]
    gain_b[...] = turned_a[experts + 1, :rows]
    gain_a[...] = turned_b[experts, :rows]
    heads, buckets = bias_ref.shape
    bias_ref[...] = small_b[:heads, experts + 2 : experts + 2 + buckets]


def layout(rank, a, b, width, experts, bias_shape):
    rows = a[0].shape[0]
    ranks = len(a)
    ins = (*a, *b)
    shapes = [(rows, 3 * width), (rows, width), (experts, rows), (rows,), (rows,), bias_shape]
    return call(
        functools.partial(layout_kernel, width, experts, ranks),
        [sds(x, F32) for x in shapes],
        grid=(1,),
        in_specs=[smem()] + [whole(x.shape) for x in ins],
        out_specs=[whole(x) for x in shapes],
        scratch_shapes=[pltpu.VMEM((rows, ranks * a[0].shape[1]), F32), pltpu.VMEM((rows, ranks * b[0].shape[1]), F32)],
        name="layout",
    )(rank, *ins)


def body(
    tokens, cotangent, segments, buckets, routes, attn_gain, qkv_weight, proj_weight,
    rel_bias, moe_gain, router, expert_in, expert_out,
):
    seq, width = tokens.shape
    size = lax.axis_size("shard")
    ranks = lax.axis_size("rep")
    top = routes.shape[1]
    experts = expert_in.shape[0] * size
    hidden = expert_in.shape[2]
    capacity = 3 * seq * top // (2 * experts)
    slots = experts * capacity
    bucket_count = rel_bias.shape[0]
    me = lax.axis_index("shard").astype(jnp.int32)
    me_arr = me.reshape(1)
    own_rows = router.shape[0]

    packed = pack_weights(qkv_weight, proj_weight, router.T, attn_gain, moe_gain)
    rev_buckets = jnp.roll(buckets[::-1], 1)
    *tables, other = prep(routes.T, segments, rev_buckets, rel_bias, cotangent, experts, capacity)
    other = lax.all_to_all(
        other[:, 0, :].reshape(size, slots // size), "shard", split_axis=0, concat_axis=0, tiled=True
    )
    w_blocks, (table, slot_row, slot_col, cot_slots, other) = gather_blocks(packed, size, (*tables, other))
    other = other.reshape(8, slots // 8)
    (q, k, v, probs, att, res, n1, n2, logits, small_full, small_t, *sent) = front(
        me_arr, tokens, table, slot_row, w_blocks, experts, slots
    )
    me_late, logits = tie(me_arr, logits)
    qkv_full, proj_full = assemble(me_late, w_blocks, width)

    def exchange(value):
        wide = value.shape[1]
        moved = lax.all_to_all(
            value.reshape(size, slots // size, wide), "shard", split_axis=0, concat_axis=0, tiled=True
        )
        return moved.reshape(slots, wide)

    cot_rows = exchange(cot_slots)

    def exchange_blocks(blocks):
        if len(blocks) == 1:
            return [exchange(blocks[0])]
        return [blocks[0]] + [swap(block, j, size) for j, block in enumerate(blocks) if j]

    cot_rows, *sent = tie(cot_rows, *sent)
    rows = exchange_blocks(sent)
    win = expert_in[0]
    wout = expert_out[0]
    per_rank = hidden // ranks // 256

    def scatter(buf):
        count, high, wide = buf.shape[1:]
        moved = lax.psum_scatter(buf.reshape(ranks * count * high, wide), "rep", scatter_dimension=0, tiled=True)
        return moved.reshape(count, high, wide)

    qkv_full, proj_full, *rows = tie(qkv_full, proj_full, *rows)
    act0, gp0, d0, buf0, sg = expert_first(me_arr, rows, cot_rows, other, small_full, win, wout, ranks)
    part0 = scatter(buf0)
    act1, gp1, send_near, send_far = expert_rest(me_arr, rows, sg, win, wout, gp0, d0, ranks)
    near = exchange(send_near)
    buf1 = expert_weight_grads(rows, sg, act1, gp1, hidden, ranks)
    buf1, part0, near, act1, send_far = tie(buf1, part0, near, act1, send_far)
    part1 = scatter(buf1)
    far = exchange(send_far)
    result = expert_rows(me_arr, (act0, act1), wout, len(rows), ranks)
    near, far, result = tie(near, far, result)
    returned = exchange(result)
    gres, gatt, acc, diag, *parts_a = token_side(
        experts, size, own_rows, me_arr, [near, far], slot_col, res, logits, cotangent, n2, att, proj_full, small_full, small_t,
        probs, q, k, v, n1, qkv_full,
    )
    returned, *parts_a = tie(returned, *parts_a)
    blocks_a = core_sum(parts_a, me, size)
    gatt, *blocks_a = tie(gatt, *blocks_a)
    terms_a = chips_sum(blocks_a, size)
    grad_tokens, *parts_b = tail(
        experts, size, own_rows, me_arr, probs, q, k, v, gatt, n1, qkv_full, acc, diag, tokens, gres, small_t, rev_buckets
    )
    cut = len(parts_b)
    done = finish(part0, 0, (), width, hidden, ranks)
    one, two, *tied = tie(*done, *parts_b, *terms_a)
    done = (one, two)
    parts_b, terms_a = tied[:cut], tied[cut:]
    blocks_b = core_sum(parts_b, me, size)
    rank_arr = lax.axis_index("rep").astype(jnp.int32).reshape(1)
    line_a = line_total(terms_a, rank_arr, ranks)
    terms_b = chips_sum(blocks_b, size)
    output = output_rows(returned, slot_col, res, logits)
    output, *terms_b = tie(output, *terms_b)
    line_b = line_total(terms_b, rank_arr, ranks)
    done = finish(part1, 1, done, width, hidden, ranks)
    line_a[0], *done = tie(line_a[0], *done)
    grad_qkv, grad_proj, grad_router, gain_a, gain_b, grad_bias = layout(
        rank_arr, line_a, line_b, width, experts, rel_bias.shape[::-1]
    )
    return (
        output,
        grad_tokens,
        grad_qkv,
        grad_proj,
        grad_router.T,
        gain_a,
        gain_b,
        grad_bias.T,
        done[0][None],
        done[1][None],
    )


def solution(mesh):
    both = P(("rep", "shard"), None)
    return jax.shard_map(
        body,
        mesh=mesh,
        in_specs=(
            both, both, P(("rep", "shard")), P(), both,
            P("shard"), P("shard", None), P("shard", None), P(), P("shard"), P("shard", None),
            P("shard", None, None), P("shard", None, None),
        ),
        out_specs=(
            both, both, P("shard", None), P("shard", None), P("shard", None), P("shard"), P("shard"), P(),
            P("shard", "rep", None), P("shard", "rep", None),
        ),
        check_vma=False,
    )
```

```python
import functools
import math

import jax
import jax.numpy as jnp
from jax import lax
from jax.experimental import pallas as pl
from jax.experimental.pallas import tpu as pltpu
from jax.sharding import PartitionSpec as P

F32 = jnp.float32
BF16 = jnp.bfloat16
EPS = 1e-06
NEG = -1e30
LANES = 128
HEAD_DIM = 64
GROUP = 256
BLOCK = 256
NEAR = 512
VMEM_LIMIT = 60 * 1024 * 1024


def dot(a, b):
    return jnp.dot(a, b, preferred_element_type=F32)


def dot_nt(a, b):
    return lax.dot_general(a, b, (((1,), (1,)), ((), ())), preferred_element_type=F32)


def dot_tn(a, b):
    return lax.dot_general(a, b, (((0,), (0,)), ((), ())), preferred_element_type=F32)


def call(kernel, out_shape, **kw):
    flops = kw.pop("flops", 0)
    moved = kw.pop("moved", 0)
    return pl.pallas_call(
        kernel,
        out_shape=out_shape,
        compiler_params=pltpu.CompilerParams(vmem_limit_bytes=VMEM_LIMIT),
        cost_estimate=pl.CostEstimate(flops=flops, bytes_accessed=moved, transcendentals=0),
        **kw,
    )


def whole(shape):
    rank = len(shape)
    return pl.BlockSpec(shape, lambda *_: (0,) * rank)


def smem():
    return pl.BlockSpec(memory_space=pltpu.SMEM)


def sds(shape, dtype):
    return jax.ShapeDtypeStruct(shape, dtype)


def iota(shape, dim):
    return lax.broadcasted_iota(jnp.int32, shape, dim)


def prep_kernel(
    experts, capacity, routes_ref, seg_row, seg_col, rev_ref, bias_ref, cot_ref,
    table_ref, slot_row_ref, slot_col_ref, cot_out_ref, other_ref, mask_scr, series_scr,
):
    step = pl.program_id(0)
    seq = cot_ref.shape[0]
    width = cot_ref.shape[1]
    per = cot_out_ref.shape[0]

    @pl.when(step == 0)
    def _():
        keep = (iota((seq, seq), 0) >= iota((seq, seq), 1)) & (seg_col[...] == seg_row[...])
        mask_scr[...] = jnp.where(keep, 0.0, NEG)
        rev = rev_ref[...]
        bias = bias_ref[...]
        series = jnp.zeros((bias.shape[0], seq), F32)
        for bucket in range(bias.shape[1]):
            series = jnp.where(rev == bucket, bias[:, bucket : bucket + 1], series)
        series_scr[...] = series
        first, second = routes_ref[0:1, :], routes_ref[1:2, :]
        ids = iota((experts, seq), 0)
        m0 = (ids == first).astype(F32)
        m1 = (ids == second).astype(F32)
        before = (iota((seq, seq), 0) < iota((seq, seq), 1)).astype(BF16)
        count = dot((m0 + m1).astype(BF16), before)
        rank0 = jnp.sum(count * m0, axis=0, keepdims=True)
        rank1 = jnp.sum(count * m1, axis=0, keepdims=True)
        r0, r1 = first.astype(F32), second.astype(F32)
        slot0 = jnp.where(rank0 < capacity, r0 * capacity + rank0, -1.0)
        slot1 = jnp.where(rank1 < capacity, r1 * capacity + rank1, -1.0)
        place = iota((LANES, seq), 0)
        rows = jnp.where(place == 0, slot0, -1.0)
        rows = jnp.where(place == 1, slot1, rows)
        rows = jnp.where(place == 2, r0, rows)
        rows = jnp.where(place == 3, r1, rows)
        slot_row_ref[...] = rows[0:8, :].astype(jnp.int32)
        cols = rows.T
        slot_col_ref[...] = cols

    row = series_scr[pl.ds(step, 1), :]
    table_ref[0] = pltpu.roll(jnp.broadcast_to(row, (seq, seq)), 0, 1, stride=1, stride_axis=0) + mask_scr[...]

    @pl.when(step < 8)
    def _():
        slots = iota((per, seq), 0) + step * per
        hit0 = (slots == slot_row_ref[0:1, :]).astype(F32)
        hit1 = (slots == slot_row_ref[1:2, :]).astype(F32)
        cot_out_ref[...] = dot((hit0 + hit1).astype(BF16), cot_ref[...]).astype(BF16)
        first = jnp.broadcast_to(slot_row_ref[2:3, :].astype(F32), (8, seq)).astype(BF16)
        second = jnp.broadcast_to(slot_row_ref[3:4, :].astype(F32), (8, seq)).astype(BF16)
        other = dot_nt(second, hit0.astype(BF16)) + dot_nt(first, hit1.astype(BF16))
        other_ref[0] = other.astype(jnp.int32)


def prep(routes_t, segments, rev_buckets, rel_bias, cotangent, experts, capacity):
    seq, width = cotangent.shape
    heads = rel_bias.shape[1]
    buckets = rel_bias.shape[0]
    slots = experts * capacity
    per = slots // 8
    hp = -(-heads // 8) * 8
    bias_t = jnp.zeros((hp, buckets), F32).at[:heads].set(rel_bias.T)
    return call(
        functools.partial(prep_kernel, experts, capacity),
        [
            sds((heads, seq, seq), F32),
            sds((8, seq), jnp.int32),
            sds((seq, LANES), F32),
            sds((slots, width), BF16),
            sds((8, 8, per), jnp.int32),
        ],
        grid=(heads,),
        in_specs=[
            whole((2, seq)), whole((1, seq)), whole((seq, 1)), whole((1, seq)),
            whole((hp, buckets)), whole((seq, width)),
        ],
        out_specs=[
            pl.BlockSpec((1, seq, seq), lambda h: (h, 0, 0)),
            whole((8, seq)),
            whole((seq, LANES)),
            pl.BlockSpec((per, width), lambda h: (jnp.minimum(h, 7), 0)),
            pl.BlockSpec((1, 8, per), lambda h: (jnp.minimum(h, 7), 0, 0)),
        ],
        scratch_shapes=[
            pltpu.VMEM((seq, seq), F32),
            pltpu.VMEM((hp, seq), F32),
        ],
        flops=2 * slots * seq * width,
        moved=heads * seq * seq * 4 + 4 * seq * width,
        name="prep",
    )(routes_t, segments[None, :], segments[:, None], rev_buckets[None, :], bias_t, cotangent)


def pack_kernel(qkv_ref, proj_ref, router_ref, gain_a, gain_b, out_ref):
    rows, width = proj_ref.shape
    experts = router_ref.shape[0]
    out_ref[:, : 3 * width] = qkv_ref[...]
    out_ref[:, 3 * width : 4 * width] = proj_ref[...]
    place = iota((LANES, rows), 0)
    a = gain_a[...].astype(F32).reshape(1, rows)
    b = gain_b[...].astype(F32).reshape(1, rows)
    gains = jnp.where(place == experts, a, jnp.where(place == experts + 1, b, 0.0))
    if rows < LANES:
        gains = jnp.concatenate([gains, jnp.zeros((LANES, LANES - rows), F32)], axis=1)
    spread = (iota((experts, LANES), 0) == iota((experts, LANES), 1)).astype(BF16)
    out_ref[:, 4 * width :] = (dot_tn(router_ref[...], spread) + gains.T[:rows, :]).astype(BF16)


def pack_weights(qkv, proj, router, gain_a, gain_b):
    rows, width = proj.shape
    ins = (qkv, proj, router, gain_a, gain_b)
    return call(
        pack_kernel,
        sds((rows, 4 * width + LANES), BF16),
        grid=(1,),
        in_specs=[whole(x.shape) for x in ins],
        out_specs=whole((rows, 4 * width + LANES)),
        name="pack_weights",
    )(*ins)


def front_kernel(
    blocks, experts, me_ref, tokens_ref, table_ref, slot_row_ref, *refs,
):
    w_in = refs[:blocks]
    (q_ref, k_ref, v_ref, prob_ref, att_ref, res_ref, n1_ref, n2_ref, logit_ref,
     small_ref, small_t_ref) = refs[blocks : blocks + 11]
    qkv_ref, proj_ref = refs[-2:]
    sent_refs = refs[blocks + 11 : -2]
    step = pl.program_id(0)
    last = pl.num_programs(0) - 1
    seq, width = tokens_ref.shape
    rows = w_in[0].shape[0]
    scale = HEAD_DIM ** (-0.5)

    @pl.when(step == 0)
    def _():
        me = me_ref[0]
        for j in range(blocks):
            start = pl.multiple_of((me ^ j) * rows, rows) if blocks > 1 else 0
            qkv_ref[pl.ds(start, rows), :] = w_in[j][:, : 3 * width]
            proj_ref[pl.ds(start, rows), :] = w_in[j][:, 3 * width : 4 * width]
            small_ref[pl.ds(start, rows), :] = w_in[j][:, 4 * width :]
        small_t_ref[...] = small_ref[...].astype(F32).T
        x = tokens_ref[...].astype(F32)
        r = lax.rsqrt(jnp.mean(x * x, axis=-1, keepdims=True) + EPS)
        n1_ref[...] = (x * r * small_t_ref[experts : experts + 1, :]).astype(BF16)

    base = pl.multiple_of(step * GROUP, GROUP)
    n1 = n1_ref[...]
    q_ref[...] = dot(n1, qkv_ref[:, pl.ds(base, GROUP)]).astype(BF16)
    k_ref[...] = dot(n1, qkv_ref[:, pl.ds(width + base, GROUP)]).astype(BF16)
    v_ref[...] = dot(n1, qkv_ref[:, pl.ds(2 * width + base, GROUP)]).astype(BF16)

    half = seq // 2
    lane = iota((half, LANES), 1)
    for pair in range(GROUP // LANES):
        cols = slice(pair * LANES, (pair + 1) * LANES)
        for rb in range(2):
            span = (rb + 1) * half
            qrows = slice(rb * half, (rb + 1) * half)
            qp = q_ref[qrows, cols]
            kp = k_ref[:span, cols]
            vp = v_ref[:span, cols]
            mixed = []
            for parity in range(2):
                mine = (lane // HEAD_DIM) == parity
                qm = jnp.where(mine, qp, jnp.zeros_like(qp))
                s = dot_nt(qm, kp) * scale + table_ref[2 * pair + parity, qrows, :span]
                top = jnp.max(s, axis=-1, keepdims=True)
                e = jnp.exp(s - top)
                total = jnp.sum(e, axis=-1, keepdims=True)
                p = (e * (1.0 / total)).astype(BF16)
                mixed.append(dot(p, vp))
                prob_ref[2 * pair + parity, qrows, :span] = p
            at = pl.multiple_of(base + pair * LANES, LANES)
            att_ref[qrows, pl.ds(at, LANES)] = jnp.where(lane < HEAD_DIM, mixed[0], mixed[1]).astype(BF16)

    @pl.when(step == last)
    def _():
        x = tokens_ref[...].astype(F32) + dot(att_ref[...], proj_ref[...])
        res_ref[...] = x
        r = lax.rsqrt(jnp.mean(x * x, axis=-1, keepdims=True) + EPS)
        n2 = (x * r * small_t_ref[experts + 1 : experts + 2, :]).astype(BF16)
        n2_ref[...] = n2
        logit_ref[...] = dot(n2, small_ref[...])
        many = len(sent_refs) > 1
        per = sent_refs[0].shape[0] if many else sent_refs[0].shape[0] // 8
        for j in range(8):
            slots = iota((per, seq), 0) + ((me_ref[0] ^ j) * per if many else j * per)
            hit = (slots == slot_row_ref[0:1, :]) | (slots == slot_row_ref[1:2, :])
            rows_j = dot(hit.astype(BF16), n2).astype(BF16)
            if many:
                sent_refs[j][...] = rows_j
            else:
                sent_refs[0][j * per : (j + 1) * per, :] = rows_j


def front(me, tokens, table, slot_row, w_blocks, experts, slots):
    seq, width = tokens.shape
    blocks = len(w_blocks)
    groups = width // GROUP
    per_group = GROUP // HEAD_DIM
    col = pl.BlockSpec((seq, GROUP), lambda g: (0, g))
    return call(
        functools.partial(front_kernel, blocks, experts),
        [
            sds((seq, width), BF16), sds((seq, width), BF16), sds((seq, width), BF16),
            sds((width // HEAD_DIM, seq, seq), BF16), sds((seq, width), BF16), sds((seq, width), F32),
            sds((seq, width), BF16), sds((seq, width), BF16), sds((seq, LANES), F32),
            sds((width, LANES), BF16), sds((LANES, width), F32),
        ]
        + [sds((slots // blocks, width), BF16)] * blocks,
        grid=(groups,),
        in_specs=[
            smem(), whole((seq, width)),
            pl.BlockSpec((per_group, seq, seq), lambda g: (g, 0, 0)),
            whole((8, seq)),
        ]
        + [whole(b.shape) for b in w_blocks],
        out_specs=[
            col, col, col,
            pl.BlockSpec((per_group, seq, seq), lambda g: (g, 0, 0)), whole((seq, width)), whole((seq, width)),
            whole((seq, width)), whole((seq, width)), whole((seq, LANES)),
            whole((width, LANES)), whole((LANES, width)),
        ]
        + [whole((slots // blocks, width))] * blocks,
        scratch_shapes=[pltpu.VMEM((width, 3 * width), BF16), pltpu.VMEM((width, width), BF16)],
        flops=2 * seq * width * width * 4 + 2 * slots * seq * width + 8 * seq * seq * width,
        moved=30_000_000,
        name="front",
    )(me, tokens, table, slot_row, *w_blocks)


def assemble_kernel(blocks, me_ref, *refs):
    qkv_ref, proj_ref = refs[-2:]
    wide = qkv_ref.shape[1]
    high = proj_ref.shape[1]
    for j in range(blocks):
        rows = refs[j].shape[0]
        start = pl.multiple_of((me_ref[0] ^ j) * rows, rows) if blocks > 1 else 0
        qkv_ref[pl.ds(start, rows), :] = refs[j][:, :wide]
        proj_ref[pl.ds(start, rows), :] = refs[j][:, wide : wide + high]


def assemble(me, w_blocks, width):
    return call(
        functools.partial(assemble_kernel, len(w_blocks)),
        [sds((width, 3 * width), BF16), sds((width, width), BF16)],
        grid=(1,),
        in_specs=[smem()] + [whole(b.shape) for b in w_blocks],
        out_specs=[whole((width, 3 * width)), whole((width, width))],
        name="assemble",
    )(me, *w_blocks)


def gelu_parts(v):
    size = jnp.abs(v) * (2.0 ** -0.5)
    t = 1.0 / (1.0 + 0.3275911 * size)
    bell = jnp.exp(-0.5 * v * v)
    poly = t * (
        0.5 * 0.254829592
        + t * (0.5 * -0.284496736 + t * (0.5 * 1.421413741 + t * (0.5 * -1.453152027 + t * (0.5 * 1.061405429))))
    )
    tail = poly * bell
    below = jnp.where(v < 0, tail, 1.0 - tail)
    return v * below, below + v * bell * (1.0 / math.sqrt(2.0 * math.pi))


def join_rows(blocks, rows_ref):
    per = blocks[0].shape[0]
    for j, block in enumerate(blocks):
        rows_ref[j * per : (j + 1) * per, :] = block[...]


def gated_rows(me, parts, rows_ref, cot_ref, other_ref, small_ref, sg_ref):
    total, width = rows_ref.shape
    tile = total // 8
    for j in range(8):
        here = slice(j * tile, (j + 1) * tile)
        there = pl.ds(pl.multiple_of((me ^ j) * tile, tile), tile) if parts > 1 else here
        logits = dot(rows_ref[here, :], small_ref[...])
        lane = iota((tile, LANES), 1)
        line = other_ref[pl.ds(me ^ j if parts > 1 else j, 1), :].astype(F32)
        fill = -tile % LANES
        if fill:
            line = jnp.concatenate([line, jnp.zeros((1, fill), F32)], axis=1)
        other_id = jnp.broadcast_to(line, (8, tile + fill)).T[:tile, 0:1].astype(jnp.int32)
        own = jnp.sum(jnp.where(lane == me, logits, 0.0), axis=1, keepdims=True)
        other = jnp.sum(jnp.where(lane == other_id, logits, 0.0), axis=1, keepdims=True)
        top = jnp.maximum(own, other)
        a, b = jnp.exp(own - top), jnp.exp(other - top)
        gate = a / (a + b)
        sg_ref[here, :] = (gate * cot_ref[there, :].astype(F32)).astype(BF16)


def expert_acts(w1, w2, rows_ref, sg_ref, act_ref, gp_ref, d_ref, tile):
    for at in range(0, rows_ref.shape[0], tile):
        here = slice(at, at + tile)
        pre = dot(rows_ref[here, :], w1)
        ga = dot_nt(sg_ref[here, :], w2)
        act, slope = gelu_parts(pre)
        low = act.astype(BF16)
        act_ref[here, :] = low
        gp_ref[here, :] = (ga * slope).astype(BF16)
        d_ref[here, :] += jnp.sum(low.astype(F32) * ga, axis=1, keepdims=True)


def expert_weights(rows_t, sg_t, act_ref, gp_ref, buf_ref, cb, pair, ranks):
    width = rows_t.shape[0]
    block = BLOCK
    part = width // ranks
    piece = block // ranks
    gwin = dot(rows_t[...], gp_ref[...]).astype(BF16)
    lane0 = pl.multiple_of(pair * 2 * block, block)
    for dest in range(ranks):
        buf_ref[dest, cb, 0:part, pl.ds(lane0, 2 * block)] = gwin[dest * part : (dest + 1) * part, :]
    gwout = dot(sg_t[...], act_ref[...]).T.astype(BF16)
    for half in range(2):
        rank = 2 * pair + half
        for i in range(ranks):
            for j in range(width // block):
                buf_ref[rank, cb, part + j * piece : part + (j + 1) * piece, i * block : (i + 1) * block] = gwout[
                    half * block + i * piece : half * block + (i + 1) * piece, j * block : (j + 1) * block
                ]


def expert_first_kernel(
    ranks, tile, parts, me_ref, cot_ref, other_ref, small_ref, w1a, w1b, w2a, w2b, *refs,
):
    blocks = refs[:parts]
    act_ref, gp_ref, d_ref, buf_ref, sg_ref, rows_t, sg_t, rows_ref = refs[parts:]
    step = pl.program_id(0)

    @pl.when(step == 0)
    def _():
        join_rows(blocks, rows_ref)
        gated_rows(me_ref[0], parts, rows_ref, cot_ref, other_ref, small_ref, sg_ref)
        rows_t[...] = rows_ref[...].T
        sg_t[...] = sg_ref[...].T
        d_ref[...] = jnp.zeros_like(d_ref)

    w1 = jnp.concatenate([w1a[...], w1b[...]], axis=1)
    w2 = jnp.concatenate([w2a[...], w2b[...]], axis=0)
    expert_acts(w1, w2, rows_ref, sg_ref, act_ref, gp_ref, d_ref, tile)
    expert_weights(rows_t, sg_t, act_ref, gp_ref, buf_ref, 0, step, ranks)


def expert_rest_kernel(
    ranks, per_rank, start, tile, parts, me_ref, sg_ref, win_ref, w2a, w2b, gp0_ref, d0_ref, *refs,
):
    blocks = refs[:parts]
    act_ref, gp_ref, back_ref, side_ref = refs[parts : parts + 4]
    gp_scr, d_scr, rows_ref = refs[-3:]
    step = pl.program_id(0)
    total, width = rows_ref.shape
    block = BLOCK

    @pl.when(step == 0)
    def _():
        join_rows(blocks, rows_ref)
        d_scr[...] = d0_ref[...]
        for c in range(start):
            for r in range(ranks):
                to = (r * per_rank + c) * block
                gp_scr[:, to : to + block] = gp0_ref[:, (c * ranks + r) * block : (c * ranks + r + 1) * block]

    pairs = ranks // 2
    cb, pair = lax.div(step, pairs), lax.rem(step, pairs)
    at_a = pl.multiple_of((2 * pair * per_rank + start + cb) * block, block)
    at_b = pl.multiple_of(((2 * pair + 1) * per_rank + start + cb) * block, block)
    w1 = jnp.concatenate([win_ref[:, pl.ds(at_a, block)], win_ref[:, pl.ds(at_b, block)]], axis=1)
    w2 = jnp.concatenate([w2a[...], w2b[...]], axis=0)
    expert_acts(w1, w2, rows_ref, sg_ref, act_ref, gp_ref, d_scr, tile)
    gp_scr[:, pl.ds(at_a, block)] = gp_ref[:, :block]
    gp_scr[:, pl.ds(at_b, block)] = gp_ref[:, block:]

    @pl.when(step == pl.num_programs(0) - 1)
    def _():
        per = total // 8
        join = 2
        for at in range(0, 8, join):
            here = slice(at * per, (at + join) * per)
            back = dot_nt(gp_scr[here, :], win_ref[...]).astype(BF16)
            d = d_scr[here, :]
            high = d.astype(BF16).astype(F32)
            lane = iota(d.shape, 1)
            side = jnp.where(lane == 0, high, jnp.where(lane == 1, d - high, 0.0)).astype(BF16)
            for i in range(join):
                inner = slice(i * per, (i + 1) * per)
                if parts > 1:
                    to = pl.ds(pl.multiple_of((me_ref[0] ^ (at + i)) * per, per), per)
                else:
                    to = slice((at + i) * per, (at + i + 1) * per)
                back_ref[to, :] = back[inner, :NEAR]
                side_ref[to, : width - NEAR] = back[inner, NEAR:]
                side_ref[to, width - NEAR :] = side[inner, :]


def expert_weights_kernel(ranks, parts, sg_ref, act_ref, gp_ref, *refs):
    blocks = refs[:parts]
    buf_ref, rows_t, sg_t = refs[parts:]
    step = pl.program_id(0)
    pairs = ranks // 2
    per = blocks[0].shape[0]

    @pl.when(step == 0)
    def _():
        if per % LANES and parts > 1:
            for j in range(0, parts, 2):
                pair = jnp.concatenate([blocks[j][...], blocks[j + 1][...]], axis=0)
                rows_t[:, j * per : (j + 2) * per] = pair.T
        else:
            for j, block in enumerate(blocks):
                rows_t[:, j * per : (j + 1) * per] = block[...].T
        sg_t[...] = sg_ref[...].T

    expert_weights(rows_t, sg_t, act_ref, gp_ref, buf_ref, lax.div(step, pairs), lax.rem(step, pairs), ranks)


def expert_weight_grads(blocks, sg, act, gp, hidden, ranks):
    total, width = sg.shape
    high, wide, per_rank = expert_sizes(width, hidden, ranks)
    count = act.shape[1] // wide
    buf = (ranks, count, high, wide)
    col = pl.BlockSpec((total, 2 * BLOCK), lambda s: (0, s))
    return call(
        functools.partial(expert_weights_kernel, ranks, len(blocks)),
        sds(buf, BF16),
        grid=(count * ranks // 2,),
        in_specs=[once((total, width)), col, col] + [once(b.shape) for b in blocks],
        out_specs=whole(buf),
        scratch_shapes=[pltpu.VMEM((width, total), BF16), pltpu.VMEM((width, total), BF16)],
        flops=4 * total * width * wide * count,
        moved=20_000_000,
        name="experts_weights",
    )(sg, act, gp, *blocks)


def once(shape):
    rank = len(shape)
    return pl.BlockSpec(shape, lambda *_: (0,) * rank, pipeline_mode=pl.Buffered(1))


def expert_sizes(width, hidden, ranks):
    high = width // ranks + (width // BLOCK) * (BLOCK // ranks)
    return high, ranks * BLOCK, hidden // ranks // BLOCK


def expert_first(me, blocks, cot, other, small, win, wout, ranks):
    total = cot.shape[0]
    width, hidden = win.shape
    high, wide, per_rank = expert_sizes(width, hidden, ranks)
    buf = (ranks, 1, high, wide)
    col = pl.BlockSpec((total, 2 * BLOCK), lambda s: (0, s))

    def win_spec(half):
        return pl.BlockSpec((width, BLOCK), lambda s: (0, (2 * s + half) * per_rank))

    def wout_spec(half):
        return pl.BlockSpec((BLOCK, width), lambda s: ((2 * s + half) * per_rank, 0))

    return call(
        functools.partial(expert_first_kernel, ranks, 256, len(blocks)),
        [
            sds((total, wide), BF16), sds((total, wide), BF16), sds((total, LANES), F32), sds(buf, BF16),
            sds((total, width), BF16),
        ],
        grid=(ranks // 2,),
        in_specs=[
            smem(), once((total, width)), once(other.shape), once((width, LANES)),
            win_spec(0), win_spec(1), wout_spec(0), wout_spec(1),
        ]
        + [once(b.shape) for b in blocks],
        out_specs=[
            col, col, whole((total, LANES)), whole(buf), whole((total, width)),
        ],
        scratch_shapes=[
            pltpu.VMEM((width, total), BF16), pltpu.VMEM((width, total), BF16), pltpu.VMEM((total, width), BF16),
        ],
        flops=8 * total * width * wide,
        moved=20_000_000,
        name="experts_first",
    )(me, cot, other, small, win, win, wout, wout, *blocks)


def expert_rest(me, blocks, sg, win, wout, gp0, d0, ranks):
    total, width = sg.shape
    hidden = win.shape[1]
    high, wide, per_rank = expert_sizes(width, hidden, ranks)
    start = 1
    count = per_rank - start
    pairs = ranks // 2
    parts = len(blocks)
    col = pl.BlockSpec((total, 2 * BLOCK), lambda s: (0, s))
    out_near, out_far = (total, NEAR), (total, width + LANES - NEAR)

    def wout_spec(half):
        return pl.BlockSpec(
            (BLOCK, width), lambda s: ((2 * lax.rem(s, pairs) + half) * per_rank + start + lax.div(s, pairs), 0)
        )

    return call(
        functools.partial(expert_rest_kernel, ranks, per_rank, start, 256, parts),
        [sds((total, count * wide), BF16), sds((total, count * wide), BF16)]
        + [sds(out_near, BF16), sds(out_far, BF16)],
        grid=(count * pairs,),
        in_specs=[
            smem(), once((total, width)), once((width, hidden)), wout_spec(0), wout_spec(1),
            once((total, start * wide)), once((total, LANES)),
        ]
        + [once(b.shape) for b in blocks],
        out_specs=[col, col, whole(out_near), whole(out_far)],
        scratch_shapes=[
            pltpu.VMEM((total, hidden), BF16), pltpu.VMEM((total, LANES), F32), pltpu.VMEM((total, width), BF16),
        ],
        flops=4 * total * width * wide * count + 2 * total * width * hidden,
        moved=30_000_000,
        name="experts_rest",
    )(me, sg, win, wout, wout, gp0, d0, *blocks)


def expert_rows_kernel(ranks, per_rank, parts, count, me_ref, *refs):
    acts, w_ref, o_ref, w_scr = refs[:count], refs[count], refs[count + 1], refs[count + 2]

    @pl.when(pl.program_id(0) == 0)
    def _():
        for c in range(per_rank):
            for r in range(ranks):
                to, src = (c * ranks + r) * BLOCK, (r * per_rank + c) * BLOCK
                w_scr[to : to + BLOCK, :] = w_ref[src : src + BLOCK, :]

    at, total = 0, None
    for act in acts:
        wide = act.shape[1]
        more = dot(act[...], w_scr[at : at + wide, :])
        total = more if total is None else total + more
        at += wide
    low = total.astype(BF16)
    if parts == 1:
        o_ref[...] = low
    else:
        per = low.shape[0] // 2
        flip = me_ref[0] % 2
        o_ref[pl.ds(pl.multiple_of(flip * per, per), per), :] = low[:per, :]
        o_ref[pl.ds(pl.multiple_of((1 - flip) * per, per), per), :] = low[per:, :]


def expert_rows(me, acts, wout, parts, ranks):
    total = acts[0].shape[0]
    hidden, width = wout.shape
    tile = total // 4

    def place(i, m):
        return ((m[0] // 2) ^ i if parts > 1 else i, 0)

    return pl.pallas_call(
        functools.partial(expert_rows_kernel, ranks, hidden // ranks // BLOCK, parts, len(acts)),
        sds((total, width), BF16),
        grid_spec=pltpu.PrefetchScalarGridSpec(
            num_scalar_prefetch=1,
            grid=(4,),
            in_specs=[pl.BlockSpec((tile, a.shape[1]), lambda i, m: (i, 0)) for a in acts] + [once(wout.shape)],
            out_specs=pl.BlockSpec((tile, width), place),
            scratch_shapes=[pltpu.VMEM(wout.shape, BF16)],
        ),
        compiler_params=pltpu.CompilerParams(vmem_limit_bytes=VMEM_LIMIT),
        name="expert_rows",
    )(me, *acts, wout)


def norm_back(x, grad, gain):
    r = lax.rsqrt(jnp.mean(x * x, axis=-1, keepdims=True) + EPS)
    u = grad * gain
    inner = jnp.mean(u * x, axis=-1, keepdims=True)
    xr = x * r
    return r * u - (r * r * r) * x * inner, jnp.sum(grad * xr, axis=0, keepdims=True)


def pair_gates(slot_ref, logit_ref):
    logits = logit_ref[...]
    lane = iota(logits.shape, 1)
    hot0 = lane == slot_ref[:, 2:3].astype(jnp.int32)
    hot1 = lane == slot_ref[:, 3:4].astype(jnp.int32)
    c0 = jnp.sum(jnp.where(hot0, logits, 0.0), axis=1, keepdims=True)
    c1 = jnp.sum(jnp.where(hot1, logits, 0.0), axis=1, keepdims=True)
    top = jnp.maximum(c0, c1)
    e0, e1 = jnp.exp(c0 - top), jnp.exp(c1 - top)
    return e0 / (e0 + e1), e1 / (e0 + e1), hot0, hot1


def pair_hits(slot_ref, slots):
    spot = iota((slot_ref.shape[0], slots), 1)
    h0 = (spot == slot_ref[:, 0:1].astype(jnp.int32)).astype(BF16)
    h1 = (spot == slot_ref[:, 1:2].astype(jnp.int32)).astype(BF16)
    return h0, h1


def output_kernel(ret_ref, slot_ref, res_ref, logit_ref, out_ref):
    h0, h1 = pair_hits(slot_ref, ret_ref.shape[0])
    g0, g1, _, _ = pair_gates(slot_ref, logit_ref)
    ret = ret_ref[...]
    out_ref[...] = (res_ref[...] + (g0 * dot(h0, ret) + g1 * dot(h1, ret))).astype(BF16)


def output_rows(returned, slot_col, res, logits):
    ins = (returned, slot_col, res, logits)
    return call(
        output_kernel,
        sds(res.shape, BF16),
        grid=(1,),
        in_specs=[whole(x.shape) for x in ins],
        out_specs=whole(res.shape),
        flops=4 * returned.shape[0] * res.size,
        moved=6_000_000,
        name="output_rows",
    )(*ins)


def heads_back(prob_ref, q_ref, k_ref, v_ref, gatt_ref, g_scr, diag_ref):
    seq = q_ref.shape[0]
    half = seq // 2
    scale = HEAD_DIM ** (-0.5)
    lane = iota((half, LANES), 1)
    full_lane = iota((seq, LANES), 1)
    for pair in range(GROUP // LANES):
        cols = slice(pair * LANES, (pair + 1) * LANES)
        dk = [jnp.zeros((seq, LANES), F32)] * 2
        dv = [jnp.zeros((seq, LANES), F32)] * 2
        skew = [jnp.zeros((LANES, seq), F32)] * 2
        for rb in range(2):
            span = (rb + 1) * half
            qrows = slice(rb * half, (rb + 1) * half)
            qp = q_ref[qrows, cols]
            gp = gatt_ref[qrows, cols]
            kp = k_ref[:span, cols]
            vp = v_ref[:span, cols]
            dq = []
            for parity in range(2):
                mine = (lane // HEAD_DIM) == parity
                gm = jnp.where(mine, gp, jnp.zeros_like(gp))
                low_p = prob_ref[2 * pair + parity, qrows, :span]
                p = low_p.astype(F32)
                dp = dot_nt(gm, vp)
                d = jnp.sum(p * dp, axis=1, keepdims=True)
                ds = p * (dp - d)
                low = ds.astype(BF16)
                dq.append(dot(low, kp) * scale)
                add_k = dot_tn(low, qp) * scale
                add_v = dot_tn(low_p, gp)
                if span < seq:
                    zero = jnp.zeros((seq - span, LANES), F32)
                    add_k = jnp.concatenate([add_k, zero], axis=0)
                    add_v = jnp.concatenate([add_v, zero], axis=0)
                dk[parity] = dk[parity] + add_k
                dv[parity] = dv[parity] + add_v
                wide = low.astype(F32)
                if span < seq:
                    wide = jnp.concatenate([wide, jnp.zeros((half, seq - span), F32)], axis=1)
                for b in range(half // LANES):
                    shift = rb * half + b * LANES
                    rows = wide[b * LANES : (b + 1) * LANES, :]
                    if shift:
                        rows = jnp.concatenate([rows[:, shift:], rows[:, :shift]], axis=1)
                    skew[parity] = skew[parity] + rows
            g_scr[0, qrows, cols] = jnp.where(lane < HEAD_DIM, dq[0], dq[1]).astype(BF16)
        g_scr[1, :, cols] = jnp.where(full_lane < HEAD_DIM, dk[0], dk[1]).astype(BF16)
        g_scr[2, :, cols] = jnp.where(full_lane < HEAD_DIM, dv[0], dv[1]).astype(BF16)
        for parity in range(2):
            acc = skew[parity][0:8, :]
            for i in range(1, LANES // 8):
                acc = acc + pltpu.roll(skew[parity][i * 8 : (i + 1) * 8, :], seq - i * 8, 1)
            at = 8 * (2 * pair + parity)
            diag_ref[at : at + 8, :] = acc


class Parted:
    def __init__(self, size, rows, refs, scratch):
        self.size, self.rows, self.refs, self.scratch = size, rows, refs, scratch

    def put(self, core, value, lanes):
        if self.size != 8:
            self.refs[0][:, lanes] = value
            return
        for b in range(8):
            self.scratch[(b % 2) ^ core, b // 2, :, lanes] = value[b * self.rows : (b + 1) * self.rows, :]

    def done(self):
        if self.size == 8:
            self.refs[0][...] = self.scratch[0]
            self.refs[1][...] = self.scratch[1]


def parted_shapes(size, rows, width, wide):
    if size != 8:
        return [(width, wide)], []
    return [(4, rows, wide)] * 2, [pltpu.VMEM((2, 4, rows, wide), BF16)]


def weights_back(group_at, n1_ref, g_scr, w_refs, core, parted):
    acc = None
    for i, w_ref in enumerate(w_refs):
        g = g_scr[i]
        at = group_at + i * GROUP
        if not isinstance(at, int):
            at = pl.multiple_of(at, GROUP)
        parted.put(core, dot_tn(n1_ref[...], g).astype(BF16), pl.ds(at, GROUP))
        more = dot_nt(g, w_ref[...])
        acc = more if acc is None else acc + more
    return acc


def token_kernel(
    experts, size, own_rows, outs, parts_in, me_ref, slot_ref, res_ref, logit_ref, cot_ref, n2_ref, att_ref,
    proj_ref, small_ref, small_t_ref, prob_ref, q_ref, k_ref, v_ref, n1_ref, wq_ref, wk_ref, wv_ref, *refs,
):
    blocks, refs = refs[:parts_in], refs[parts_in:]
    gres_ref, gatt_ref, acc_ref, diag_ref = refs[:4]
    parts = refs[4 : 4 + outs]
    g_scr, gatt_scr, back_ref = refs[4 + outs : 7 + outs]
    parted = Parted(size, own_rows, parts, refs[7 + outs] if size == 8 else None)
    step = pl.program_id(0)
    seq, width = res_ref.shape
    core = me_ref[0] % 2
    groups = width // GROUP
    extra = (groups - 1) * 3 * GROUP

    @pl.when(step == 0)
    def _():
        at = 0
        for block in blocks:
            back_ref[:, at : at + block.shape[1]] = block[...]
            at += block.shape[1]
        h0, h1 = pair_hits(slot_ref, back_ref.shape[0])
        g0, g1, hot0, hot1 = pair_gates(slot_ref, logit_ref)
        back = back_ref[:, :width]
        sides = back_ref[:, width:]
        d0 = jnp.sum(dot(h0, sides), axis=1, keepdims=True)
        d1 = jnp.sum(dot(h1, sides), axis=1, keepdims=True)
        glog = jnp.where(hot0, d0 - g0 * (d0 + d1), 0.0) + jnp.where(hot1, d1 - g1 * (d0 + d1), 0.0)
        glog = glog.astype(BF16)
        x = res_ref[...]
        small = small_ref[...]
        router = jnp.where(iota((width, LANES), 1) < experts, small, jnp.zeros_like(small))
        grad = dot(h0 + h1, back) + dot_nt(glog, router)
        gx, ggain = norm_back(x, grad, small_t_ref[experts + 1 : experts + 2, :])
        gres = gx + cot_ref[...].astype(F32)
        gres_ref[...] = gres
        branch = gres.astype(BF16)
        gatt = dot_nt(branch, proj_ref[...]).astype(BF16)
        for g in range(groups):
            gatt_scr[g] = gatt[:, g * GROUP : (g + 1) * GROUP]
        gatt_ref[...] = gatt[:, (groups - 1) * GROUP :]
        parted.put(core, dot_tn(att_ref[...], branch).astype(BF16), slice(extra, extra + width))
        gain_rows = jnp.where(iota((LANES, width), 0) == experts + 1, ggain, 0.0)
        more = (dot_tn(n2_ref[...], glog) + gain_rows.T).astype(BF16)
        parted.put(core, more, slice(extra + width, extra + width + LANES))

    @pl.when(step > 0)
    def _():
        group = step - 1
        heads_back(prob_ref, q_ref, k_ref, v_ref, gatt_scr.at[group], g_scr, diag_ref)
        more = weights_back(group * 3 * GROUP, n1_ref, g_scr, (wq_ref, wk_ref, wv_ref), core, parted)

        @pl.when(step == 1)
        def _():
            acc_ref[...] = more

        @pl.when(step > 1)
        def _():
            acc_ref[...] += more

    @pl.when(step == pl.num_programs(0) - 1)
    def _():
        parted.done()


def token_side(
    experts, size, own_rows, me, back, slot_col, res, logits, cot, n2, att, proj, small, small_t,
    probs, q, k, v, n1, qkv,
):
    seq, width = res.shape
    groups = width // GROUP
    per_group = GROUP // HEAD_DIM
    wide = (groups - 1) * 3 * GROUP + width + LANES
    shapes, scratch = parted_shapes(size, own_rows, width, wide)

    def at(s):
        return jnp.maximum(s - 1, 0)

    col = pl.BlockSpec((seq, GROUP), lambda s: (0, at(s)))

    def wcol(i):
        return pl.BlockSpec((width, GROUP), lambda s: (0, i * groups + at(s)))

    first = (slot_col, res, logits, cot, n2, att, proj, small, small_t)
    return call(
        functools.partial(token_kernel, experts, size, own_rows, len(shapes), len(back)),
        [
            sds((seq, width), F32), sds((seq, GROUP), BF16), sds((seq, width), F32),
            sds(((groups - 1) * 8 * per_group, seq), F32),
        ]
        + [sds(x, BF16) for x in shapes],
        grid=(groups,),
        in_specs=[smem()] + [once(a.shape) for a in first]
        + [pl.BlockSpec((per_group, seq, seq), lambda s: (at(s), 0, 0)), col, col, col]
        + [once((seq, width)), wcol(0), wcol(1), wcol(2)]
        + [once(b.shape) for b in back],
        out_specs=[
            whole((seq, width)), whole((seq, GROUP)), whole((seq, width)),
            pl.BlockSpec((8 * per_group, seq), lambda s: (at(s), 0)),
        ]
        + [whole(x) for x in shapes],
        scratch_shapes=[
            pltpu.VMEM((3, seq, GROUP), BF16), pltpu.VMEM((groups, seq, GROUP), BF16),
            pltpu.VMEM((back[0].shape[0], width + LANES), BF16),
        ]
        + scratch,
        flops=3072 * seq * width + 12 * seq * width * width + 14 * seq * seq * width,
        moved=30_000_000,
        name="token_side",
    )(me, *first, probs, q, k, v, n1, qkv, qkv, qkv, *back)


def tail_kernel(
    experts, size, own_rows, outs, me_ref, prob_ref, q_ref, k_ref, v_ref, gatt_ref, n1_ref,
    wq_ref, wk_ref, wv_ref, acc_ref, diag_in, tokens_ref, gres_ref, small_t_ref, rev_ref, gtok_ref, *refs,
):
    parts = refs[:outs]
    g_scr, diag_scr = refs[outs : outs + 2]
    parted = Parted(size, own_rows, parts, refs[outs + 2] if size == 8 else None)
    seq, width = tokens_ref.shape
    core = me_ref[0] % 2
    heads_back(prob_ref, q_ref, k_ref, v_ref, gatt_ref, g_scr, diag_scr)
    acc = acc_ref[...] + weights_back(0, n1_ref, g_scr, (wq_ref, wk_ref, wv_ref), core, parted)
    x = tokens_ref[...].astype(F32)
    gx, ggain = norm_back(x, acc, small_t_ref[experts : experts + 1, :])
    gtok_ref[...] = (gx + gres_ref[...]).astype(BF16)
    gain_rows = jnp.where(iota((LANES, width), 0) == experts, ggain, 0.0)
    diag = jnp.concatenate([diag_in[...], diag_scr[...]], axis=0)
    count = diag.shape[0]
    place = lax.rem(iota((count, seq), 0), 8)
    total = jnp.where(place == 0, diag, 0.0)
    for r in range(1, 8):
        total = total + jnp.where(place == r, pltpu.roll(diag, seq - r, 1), 0.0)
    hot = (iota((LANES, seq), 0) - (experts + 2) == rev_ref[...]).astype(F32)
    per_row = lax.dot_general(
        total, hot, (((1,), (1,)), ((), ())), precision=lax.Precision.HIGHEST, preferred_element_type=F32
    )
    copies = (lax.rem(iota((width, count), 0), own_rows) == lax.div(iota((width, count), 1), 8)).astype(F32)
    spread = jnp.dot(copies, per_row, precision=lax.Precision.HIGHEST, preferred_element_type=F32)
    parted.put(core, (gain_rows.T + spread).astype(BF16), slice(3 * GROUP, 3 * GROUP + LANES))
    parted.done()


def tail(experts, size, own_rows, me, probs, q, k, v, gatt, n1, qkv, acc, diag, tokens, gres, small_t, rev_buckets):
    seq, width = n1.shape
    groups = width // GROUP
    group = groups - 1
    per_group = GROUP // HEAD_DIM
    col = pl.BlockSpec((seq, GROUP), lambda _: (0, group))
    shapes, scratch = parted_shapes(size, own_rows, width, 3 * GROUP + LANES)

    def wcol(i):
        return pl.BlockSpec((width, GROUP), lambda _: (0, i * groups + group))

    rest = (acc, diag, tokens, gres, small_t, rev_buckets[None, :])
    return call(
        functools.partial(tail_kernel, experts, size, own_rows, len(shapes)),
        [sds((seq, width), BF16)] + [sds(x, BF16) for x in shapes],
        grid=(1,),
        in_specs=[
            smem(), pl.BlockSpec((per_group, seq, seq), lambda _: (group, 0, 0)),
            col, col, col, whole((seq, GROUP)),
            whole((seq, width)),
            wcol(0), wcol(1), wcol(2),
        ]
        + [whole(x.shape) for x in rest],
        out_specs=[whole((seq, width))] + [whole(x) for x in shapes],
        scratch_shapes=[pltpu.VMEM((3, seq, GROUP), BF16), pltpu.VMEM((8 * per_group, seq), F32)] + scratch,
        flops=4 * seq * width * width + 7 * seq * seq * width,
        moved=10_000_000,
        name="tail",
    )(me, probs, q, k, v, gatt, n1, qkv, qkv, qkv, *rest)


def swap(value, mask, size):
    return lax.ppermute(value, "shard", [(i, i ^ mask) for i in range(size)])


def gather_blocks(value, size, beside):
    if size != 8:
        return [lax.all_gather(value, "shard", axis=0, tiled=True)], beside
    one, six, two, four = (swap(value, j, size) for j in (1, 6, 2, 4))
    one, six, two, four, *beside = lax.optimization_barrier((one, six, two, four, *beside))
    far = {0: value, 1: one, 6: six, 2: two, 4: four}
    near = {j ^ 1: swap(far[j], 1, size) for j in (6, 2, 4)}
    return [far[j] if j in far else near[j] for j in range(8)], beside


def tie(*values):
    return lax.optimization_barrier(values)


def across(value, mask, ranks):
    return lax.ppermute(value, "rep", [(i, i ^ mask) for i in range(ranks)])


def add(*values):
    total = values[0].astype(F32)
    for value in values[1:]:
        total = total + value.astype(F32)
    return total.astype(BF16)


def spread_kernel(terms, rank_ref, *refs):
    outs, total = refs[terms:-1], refs[-1]
    value = refs[0][...].astype(F32)
    for ref in refs[1:terms]:
        value = value + ref[...].astype(F32)
    wide = value.shape[1]
    total[:, :wide] = value
    if total.shape[1] > wide:
        total[:, wide:] = jnp.zeros((value.shape[0], total.shape[1] - wide), F32)
    part = outs[0].shape[1]
    for j, out in enumerate(outs):
        at = pl.multiple_of((rank_ref[0] ^ j) * part, LANES)
        out[...] = total[:, pl.ds(at, part)].astype(BF16)


def line_total(terms, rank, ranks):
    rows, wide = terms[0].shape
    part = -(-wide // (ranks * LANES)) * LANES
    parts = call(
        functools.partial(spread_kernel, len(terms)),
        [sds((rows, part), BF16)] * ranks,
        grid=(1,),
        in_specs=[smem()] + [whole((rows, wide))] * len(terms),
        out_specs=[whole((rows, part))] * ranks,
        scratch_shapes=[pltpu.VMEM((rows, part * ranks), F32)],
        name="spread",
    )(rank, *terms)
    own = add(parts[0], *[across(parts[j], j, ranks) for j in range(1, ranks)])
    return [own] + [across(own, j, ranks) for j in range(1, ranks)]


def finish_kernel(width, src_ref, *refs):
    in_ref, out_ref = refs[-2:]
    total = src_ref[0].astype(F32)
    part, block = in_ref.shape
    piece = out_ref.shape[0]
    in_ref[...] = total[:part, :]
    for j in range(width // block):
        out_ref[:, j * block : (j + 1) * block] = total[part + j * piece : part + (j + 1) * piece, :]


def finish(src, start, earlier, width, hidden, ranks):
    count, high, wide = src.shape
    block = wide // ranks
    part = width // ranks
    piece = block // ranks
    per_rank = hidden // ranks // block
    return call(
        functools.partial(finish_kernel, width),
        [sds((part, hidden), F32), sds((hidden // ranks, width), F32)],
        grid=(count, ranks),
        in_specs=[pl.BlockSpec((1, high, block), lambda c, r: (c, 0, r))]
        + [pl.BlockSpec(memory_space=pl.ANY)] * len(earlier),
        out_specs=[
            pl.BlockSpec((part, block), lambda c, r: (0, r * per_rank + start + c)),
            pl.BlockSpec((piece, width), lambda c, r: ((start + c) * ranks + r, 0)),
        ],
        input_output_aliases={1: 0, 2: 1} if earlier else {},
        name="finish",
    )(src, *earlier)


def pick_kernel(chip_ref, keep_ref, got_ref, six_ref, two_ref, four_ref, own_ref):
    chip = chip_ref[0]
    for ref, other in ((six_ref, 3), (two_ref, 1), (four_ref, 2), (own_ref, 0)):
        at = chip ^ other
        ref[...] = (keep_ref[at].astype(F32) + got_ref[at].astype(F32)).astype(BF16)


def core_sum(parts, me, size, *beside):
    if size != 8:
        return [parts[0]], beside
    keep, send = parts
    got, *beside = tie(swap(send, 1, size), *beside)
    block = keep.shape[1:]
    blocks = call(
        pick_kernel,
        [sds(block, BF16)] * 4,
        grid=(1,),
        in_specs=[smem(), whole(keep.shape), whole(keep.shape)],
        out_specs=[whole(block)] * 4,
        name="pick",
    )((me // 2).reshape(1), keep, got)
    return blocks, beside


def chips_sum(blocks, size):
    if size != 8:
        return [lax.psum_scatter(blocks[0], "shard", scatter_dimension=0, tiled=True)]
    return [blocks[3]] + [swap(block, j, size) for block, j in zip(blocks, (6, 2, 4))]


def layout_kernel(width, experts, ranks, rank_ref, *refs):
    a_parts, b_parts = refs[:ranks], refs[ranks : 2 * ranks]
    qkv_ref, proj_ref, router_ref, gain_a, gain_b, bias_ref, a, b = refs[2 * ranks :]
    for parts, total in ((a_parts, a), (b_parts, b)):
        part = parts[0].shape[1]
        for j, ref in enumerate(parts):
            at = pl.multiple_of((rank_ref[0] ^ j) * part, LANES)
            total[:, pl.ds(at, part)] = ref[...].astype(F32)
    groups = width // GROUP
    for g in range(groups):
        src, base = (a, g * 3 * GROUP) if g < groups - 1 else (b, 0)
        for i in range(3):
            qkv_ref[:, i * width + g * GROUP : i * width + (g + 1) * GROUP] = src[:, base + i * GROUP : base + (i + 1) * GROUP]
    extra = (groups - 1) * 3 * GROUP
    proj_ref[...] = a[:, extra : extra + width]
    small_a = a[:, extra + width : extra + width + LANES]
    small_b = b[:, 3 * GROUP : 3 * GROUP + LANES]
    rows = small_a.shape[0]
    pad = jnp.zeros((LANES - rows, LANES), F32)
    turned_a = jnp.concatenate([small_a, pad], axis=0).T
    turned_b = jnp.concatenate([small_b, pad], axis=0).T
    router_ref[...] = turned_a[:experts, :rows]
    gain_b[...] = turned_a[experts + 1, :rows]
    gain_a[...] = turned_b[experts, :rows]
    heads, buckets = bias_ref.shape
    bias_ref[...] = small_b[:heads, experts + 2 : experts + 2 + buckets]


def layout(rank, a, b, width, experts, bias_shape):
    rows = a[0].shape[0]
    ranks = len(a)
    ins = (*a, *b)
    shapes = [(rows, 3 * width), (rows, width), (experts, rows), (rows,), (rows,), bias_shape]
    return call(
        functools.partial(layout_kernel, width, experts, ranks),
        [sds(x, F32) for x in shapes],
        grid=(1,),
        in_specs=[smem()] + [whole(x.shape) for x in ins],
        out_specs=[whole(x) for x in shapes],
        scratch_shapes=[pltpu.VMEM((rows, ranks * a[0].shape[1]), F32), pltpu.VMEM((rows, ranks * b[0].shape[1]), F32)],
        name="layout",
    )(rank, *ins)


def body(
    tokens, cotangent, segments, buckets, routes, attn_gain, qkv_weight, proj_weight,
    rel_bias, moe_gain, router, expert_in, expert_out,
):
    seq, width = tokens.shape
    size = lax.axis_size("shard")
    ranks = lax.axis_size("rep")
    top = routes.shape[1]
    experts = expert_in.shape[0] * size
    hidden = expert_in.shape[2]
    capacity = 3 * seq * top // (2 * experts)
    slots = experts * capacity
    bucket_count = rel_bias.shape[0]
    me = lax.axis_index("shard").astype(jnp.int32)
    me_arr = me.reshape(1)
    own_rows = router.shape[0]

    packed = pack_weights(qkv_weight, proj_weight, router.T, attn_gain, moe_gain)
    rev_buckets = jnp.roll(buckets[::-1], 1)
    *tables, other = prep(routes.T, segments, rev_buckets, rel_bias, cotangent, experts, capacity)
    other = lax.all_to_all(
        other[:, 0, :].reshape(size, slots // size), "shard", split_axis=0, concat_axis=0, tiled=True
    )
    w_blocks, (table, slot_row, slot_col, cot_slots, other) = gather_blocks(packed, size, (*tables, other))
    other = other.reshape(8, slots // 8)
    (q, k, v, probs, att, res, n1, n2, logits, small_full, small_t, *sent) = front(
        me_arr, tokens, table, slot_row, w_blocks, experts, slots
    )
    me_late, logits = tie(me_arr, logits)
    qkv_full, proj_full = assemble(me_late, w_blocks, width)

    def exchange(value):
        wide = value.shape[1]
        moved = lax.all_to_all(
            value.reshape(size, slots // size, wide), "shard", split_axis=0, concat_axis=0, tiled=True
        )
        return moved.reshape(slots, wide)

    cot_rows = exchange(cot_slots)

    def exchange_blocks(blocks):
        if len(blocks) == 1:
            return [exchange(blocks[0])]
        return [blocks[0]] + [swap(block, j, size) for j, block in enumerate(blocks) if j]

    cot_rows, *sent = tie(cot_rows, *sent)
    rows = exchange_blocks(sent)
    win = expert_in[0]
    wout = expert_out[0]
    per_rank = hidden // ranks // 256

    def scatter(buf):
        count, high, wide = buf.shape[1:]
        moved = lax.psum_scatter(buf.reshape(ranks * count * high, wide), "rep", scatter_dimension=0, tiled=True)
        return moved.reshape(count, high, wide)

    qkv_full, proj_full, *rows = tie(qkv_full, proj_full, *rows)
    act0, gp0, d0, buf0, sg = expert_first(me_arr, rows, cot_rows, other, small_full, win, wout, ranks)
    part0 = scatter(buf0)
    act1, gp1, send_near, send_far = expert_rest(me_arr, rows, sg, win, wout, gp0, d0, ranks)
    near = exchange(send_near)
    buf1 = expert_weight_grads(rows, sg, act1, gp1, hidden, ranks)
    buf1, part0, near, act1, send_far = tie(buf1, part0, near, act1, send_far)
    part1 = scatter(buf1)
    far = exchange(send_far)
    result = expert_rows(me_arr, (act0, act1), wout, len(rows), ranks)
    near, far, result = tie(near, far, result)
    returned = exchange(result)
    gres, gatt, acc, diag, *parts_a = token_side(
        experts, size, own_rows, me_arr, [near, far], slot_col, res, logits, cotangent, n2, att, proj_full, small_full, small_t,
        probs, q, k, v, n1, qkv_full,
    )
    blocks_a, (returned,) = core_sum(parts_a, me, size, returned)
    gatt, *blocks_a = tie(gatt, *blocks_a)
    terms_a = chips_sum(blocks_a, size)
    grad_tokens, *parts_b = tail(
        experts, size, own_rows, me_arr, probs, q, k, v, gatt, n1, qkv_full, acc, diag, tokens, gres, small_t, rev_buckets
    )
    cut = len(parts_b)
    done = finish(part0, 0, (), width, hidden, ranks)
    one, two, *tied = tie(*done, *parts_b, *terms_a)
    done = (one, two)
    parts_b, terms_a = tied[:cut], tied[cut:]
    blocks_b, _ = core_sum(parts_b, me, size)
    rank_arr = lax.axis_index("rep").astype(jnp.int32).reshape(1)
    line_a = line_total(terms_a, rank_arr, ranks)
    terms_b = chips_sum(blocks_b, size)
    output = output_rows(returned, slot_col, res, logits)
    output, *terms_b = tie(output, *terms_b)
    line_b = line_total(terms_b, rank_arr, ranks)
    done = finish(part1, 1, done, width, hidden, ranks)
    line_a[0], *done = tie(line_a[0], *done)
    grad_qkv, grad_proj, grad_router, gain_a, gain_b, grad_bias = layout(
        rank_arr, line_a, line_b, width, experts, rel_bias.shape[::-1]
    )
    return (
        output,
        grad_tokens,
        grad_qkv,
        grad_proj,
        grad_router.T,
        gain_a,
        gain_b,
        grad_bias.T,
        done[0][None],
        done[1][None],
    )


def solution(mesh):
    both = P(("rep", "shard"), None)
    return jax.shard_map(
        body,
        mesh=mesh,
        in_specs=(
            both, both, P(("rep", "shard")), P(), both,
            P("shard"), P("shard", None), P("shard", None), P(), P("shard"), P("shard", None),
            P("shard", None, None), P("shard", None, None),
        ),
        out_specs=(
            both, both, P("shard", None), P("shard", None), P("shard", None), P("shard"), P("shard"), P(),
            P("shard", "rep", None), P("shard", "rep", None),
        ),
        check_vma=False,
    )
```
